32 devices in a mesh: dp: 8 (over y, x, core), blk: 4 (over z).
Axes of the slice: x: 2, y: 2, z: 4, core: 2. Of those that a mesh axis runs over, the one named last changes fastest.
Arguments:
- tokens: bfloat16 [8, 768, 768], P('dp', 'blk'), may hold values from -6 to 6
- lengths: int32 [8, 4], P('dp'), may hold values from 1 to 765, as said below
- distance_bucket: int32 [2049], replicated, may hold values from 0 to 512, as said below
- w_qkv: bfloat16 [768, 2304], P(('dp', 'blk')), may hold values from -0.21875 to 0.21875
- w_out: bfloat16 [768, 768], P(('dp', 'blk')), may hold values from -0.21875 to 0.21875
- w_fc1: bfloat16 [768, 3072], P(('dp', 'blk')), may hold values from -0.21875 to 0.21875
- w_fc2: bfloat16 [3072, 768], P(('dp', 'blk')), may hold values from -0.109375 to 0.109375
- gain_in: float32 [768], replicated, may hold values from 0.25 to 1.75
- gain_attn: float32 [768], replicated, may hold values from 0.25 to 1.75
- gain_ffn_in: float32 [768], replicated, may hold values from 0.25 to 1.75
- gain_hidden: float32 [3072], replicated, may hold values from 0.25 to 1.75
- head_scale: float32 [12], replicated, may hold values from 0.25 to 1.75
- bias_table: float32 [513, 12], replicated, may hold values from -5 to 5
- cotangent: bfloat16 [8, 768, 768], P('dp', 'blk'), may hold values from -6 to 6
Outputs:
- mixed: bfloat16 [8, 768, 768], P('dp', 'blk')
- grad_tokens: bfloat16 [8, 768, 768], P('dp', 'blk')
- grad_qkv: float32 [768, 2304], P(('dp', 'blk'))
- grad_out: float32 [768, 768], P(('dp', 'blk'))
- grad_fc1: float32 [768, 3072], P(('dp', 'blk'))
- grad_fc2: float32 [3072, 768], P(('dp', 'blk'))
- grad_gain_in: float32 [768], replicated
- grad_gain_attn: float32 [768], replicated
- grad_gain_ffn_in: float32 [768], replicated
- grad_gain_hidden: float32 [3072], replicated
- grad_head_scale: float32 [12], replicated
- grad_bias_table: float32 [513, 12], replicated
The draws below stay inside these ranges and needn't reach their ends.
Inputs may be any that keep to these rules, and one draw needn't show every extreme that they name: In every row the 4 lengths sum to 768; one document, at an index that varies, starts within the first 192 positions of the row and ends within the last 192. `distance_bucket`: entry 1024 + r is the bucket of the clipped relative distance r; it never falls as r rises and equals 256 at r = 0.
All inputs are finite; a program needn't handle non-finite values.
Results may differ from the reference program's by a relative error of at most 0.02.
Values may be sent and summed in bfloat16 or wider, within the bound.
No kernel may reach another device: no remote copies, remote signals or barrier semaphores. Data moves between devices by JAX's collectives and lax.ppermute only.
A program may use at most 320 MiB of HBM per device.

```python
import math
import jax
import jax.numpy as jnp
from jax import lax

D = 768
HEADS = 12
HEAD_DIM = 64
FF = 3072
ROW_DEV = 192
SEGS = 4
HALF = 256
MAXPOS = 1024
BUCKETS = 513
ROWS = 8
ROW_LEN = 768


def draw_lengths(key, part):
    key = jax.random.fold_in(key, 11)
    key_short, key_long, key_row = jax.random.split(key, 3)
    short = jax.random.randint(key_short, (ROWS, SEGS), 1, ROW_DEV // SEGS + 1)
    long_index = jax.random.randint(key_long, (ROWS, 1), 0, SEGS)
    slots = jnp.arange(SEGS)[None, :]
    is_long = slots == long_index
    unit_slot = slots == (long_index + 1) % SEGS
    short = jnp.where(unit_slot, 1, short)
    tight_row = jax.random.randint(key_row, (), 0, ROWS)
    short = jnp.where(jnp.arange(ROWS)[:, None] == tight_row, 1, short)
    rest = jnp.sum(jnp.where(is_long, 0, short), axis=1, keepdims=True)
    return jnp.where(is_long, ROW_LEN - rest, short).astype(jnp.int32)


def draw_distance_bucket(key, part):
    key = jax.random.fold_in(key, 23)
    key_up, key_down = jax.random.split(key)
    steps = jnp.arange(1, MAXPOS + 1)

    def one_side(side_key):
        rises = jax.random.randint(side_key, (MAXPOS,), 0, 2)
        rises = jnp.where(steps <= HALF // 2, 1, rises)
        offsets = jnp.minimum(jnp.cumsum(rises), HALF)
        return jnp.where(steps == MAXPOS, HALF, offsets).astype(jnp.int32)
    upper = HALF + one_side(key_up)
    lower = HALF - one_side(key_down)
    centre = jnp.full((1,), HALF, jnp.int32)
    return jnp.concatenate([lower[::-1], centre, upper]).astype(jnp.int32)


def block_scale(key, dims, cuts, least, top_value):
    level = 1.0
    for position, parts in cuts:
        heights = jax.random.uniform(jax.random.fold_in(jax.random.fold_in(key, 6), position), (parts,), jnp.float32, least / len(cuts), top_value / len(cuts))
        level = level * jnp.repeat(jnp.exp(heights), dims[position] // parts).reshape((-1,) + (1,) * (len(dims) - 1 - position))
    return level


def normal_values(stream_key, extent, scale, most, cuts=(), kind=jnp.bfloat16):
    drawn = scale * jax.random.normal(stream_key, extent, jnp.float32)
    if cuts:
        drawn = drawn * block_scale(stream_key, extent, cuts, -0.22, 0.18)
    return jnp.clip(drawn, -most, most).astype(kind)


def setup_inputs(seed: int = 0) -> dict:
    seeds = jax.random.split(jax.random.key(seed), 15)
    return {
        "tokens": normal_values(seeds[0], (ROWS, ROW_LEN, D), 1.0, 6.0, ((0, 8), (1, 4))),
        "lengths": draw_lengths(jax.random.fold_in(seeds[14], 71), 0),
        "distance_bucket": draw_distance_bucket(jax.random.fold_in(seeds[14], 71), 0),
        "w_qkv": normal_values(seeds[3], (D, 3 * D), D ** -0.5, 0.21875, ((0, 32),)),
        "w_out": normal_values(seeds[4], (D, D), D ** -0.5, 0.21875, ((0, 32),)),
        "w_fc1": normal_values(seeds[5], (D, FF), D ** -0.5, 0.21875, ((0, 32),)),
        "w_fc2": normal_values(seeds[6], (FF, D), FF ** -0.5, 0.109375, ((0, 32),)),
        "gain_in": jnp.clip(1.0 + 0.15 * jax.random.normal(seeds[7], (D,), jnp.float32), 0.25, 1.75),
        "gain_attn": jnp.clip(1.0 + 0.15 * jax.random.normal(seeds[8], (D,), jnp.float32), 0.25, 1.75),
        "gain_ffn_in": jnp.clip(1.0 + 0.15 * jax.random.normal(seeds[9], (D,), jnp.float32), 0.25, 1.75),
        "gain_hidden": jnp.clip(1.0 + 0.15 * jax.random.normal(seeds[10], (FF,), jnp.float32), 0.25, 1.75),
        "head_scale": jnp.clip(1.0 + 0.15 * jax.random.normal(seeds[11], (HEADS,), jnp.float32), 0.25, 1.75),
        "bias_table": normal_values(seeds[12], (BUCKETS, HEADS), 1.0, 5.0, (), jnp.float32),
        "cotangent": normal_values(seeds[13], (ROWS, ROW_LEN, D), 1.0, 6.0, ((0, 8), (1, 4))),
    }


epsilon = 1e-05
masked_score = -1e+30
query_scale = 0.125
highest = lax.Precision.HIGHEST

@jax.custom_vjp
def low(v):
    return lax.optimization_barrier(v.astype(jnp.bfloat16)).astype(jnp.float32)

@jax.custom_vjp
def low_back(v):
    return v

def low_keep(v):
    return (low(v), None)

def low_pass(kept, grad):
    return (grad,)

def back_keep(v):
    return (v, None)

def back_low(kept, grad):
    return (low(grad),)
low.defvjp(low_keep, low_pass)
low_back.defvjp(back_keep, back_low)

def round_both(value):
    return low(low_back(value))

def layer_norm(value, gain):
    center = value - lax.optimization_barrier(jnp.mean(value, axis=-1, keepdims=True))
    spread = lax.optimization_barrier(jnp.mean(center * center, axis=-1, keepdims=True))
    return center * lax.rsqrt(spread + epsilon) * gain

def matmul(left, right):
    return jnp.dot(left, right, precision=highest)

def row_forward(row_input, row_lengths, params):
    w_qkv, w_out, w_fc1, w_fc2, gain_in, gain_attn, gain_ffn_in, gain_hidden, head_scale, distance_bias = params
    normed_in = low(layer_norm(row_input, gain_in))
    projected = matmul(normed_in, w_qkv)
    queries = round_both(projected[:, :D] * query_scale).reshape(ROW_LEN, HEADS, HEAD_DIM)
    keys_all = round_both(projected[:, D:2 * D]).reshape(ROW_LEN, HEADS, HEAD_DIM)
    values_all = round_both(projected[:, 2 * D:]).reshape(ROW_LEN, HEADS, HEAD_DIM)
    positions = jnp.arange(ROW_LEN, dtype=jnp.int32)
    ends = jnp.cumsum(row_lengths).astype(jnp.int32)
    documents = lax.optimization_barrier(jnp.sum((positions[:, None] >= ends[None, :]).astype(jnp.int32), axis=1))
    block_rows = math.gcd(ROW_LEN, 512)
    count = ROW_LEN // block_rows

    def block_attend(pieces):
        query_block, query_pos, query_doc = pieces
        raw = low_back(jnp.einsum('qhd,khd->hqk', query_block, keys_all, precision=highest))
        offset = jnp.clip(positions[None, :] - query_pos[:, None], -MAXPOS, MAXPOS) + MAXPOS
        scores = raw + jnp.moveaxis(distance_bias[offset], -1, 0)
        same = query_doc[:, None] == documents[None, :]
        scores = jnp.where(same[None], scores, masked_score)
        probs = jax.nn.softmax(scores, axis=-1)
        return jnp.einsum('hqk,khd->qhd', low(probs), values_all, precision=highest)
    attention = lax.map(jax.checkpoint(block_attend), (queries.reshape(count, block_rows, HEADS, HEAD_DIM), positions.reshape(count, block_rows), documents.reshape(count, block_rows)))
    attention = attention.reshape(ROW_LEN, D)
    scale_cols = jnp.repeat(head_scale, HEAD_DIM)
    scaled = low(low_back(attention) * scale_cols)
    attn_out = low_back(matmul(scaled, w_out))
    middle = row_input + layer_norm(attn_out, gain_attn)
    normed_mid = low(layer_norm(middle, gain_ffn_in))
    hidden = low_back(matmul(normed_mid, w_fc1))
    activated = low(layer_norm(jax.nn.gelu(hidden, approximate=False), gain_hidden))
    return middle + matmul(activated, w_fc2)

def reference(tokens, lengths, distance_bucket, w_qkv, w_out, w_fc1, w_fc2, gain_in, gain_attn, gain_ffn_in, gain_hidden, head_scale, bias_table, cotangent):

    def forward(inputs, wq, wo, wa, wb, g_in, g_attn, g_ffn, g_hidden, scales, table):
        distance_bias = table[distance_bucket]
        params = (wq, wo, wa, wb, g_in, g_attn, g_ffn, g_hidden, scales, distance_bias)

        def one_row(pieces):
            return row_forward(pieces[0], pieces[1], params)
        return lax.map(jax.checkpoint(one_row), (inputs, lengths))
    start = (tokens.astype(jnp.float32), w_qkv.astype(jnp.float32), w_out.astype(jnp.float32), w_fc1.astype(jnp.float32), w_fc2.astype(jnp.float32), gain_in.astype(jnp.float32), gain_attn.astype(jnp.float32), gain_ffn_in.astype(jnp.float32), gain_hidden.astype(jnp.float32), head_scale.astype(jnp.float32), bias_table.astype(jnp.float32))
    output, pullback = jax.vjp(forward, *start)
    grads = pullback(cotangent.astype(jnp.float32))
    return (output.astype(jnp.bfloat16), grads[0].astype(jnp.bfloat16), grads[1], grads[2], grads[3], grads[4], grads[5], grads[6], grads[7], grads[8], grads[9], grads[10])
```

```python
import functools
import math

import jax
import jax.numpy as jnp
from jax import lax
from jax.experimental import pallas as pl
from jax.experimental.pallas import tpu as pltpu
from jax.sharding import PartitionSpec as P

epsilon = 1e-05
masked_score = -1e30
query_scale = 0.125
highest = lax.Precision.HIGHEST


def layer_norm(value, gain):
    center = value - jnp.mean(value, axis=-1, keepdims=True)
    spread = jnp.mean(center * center, axis=-1, keepdims=True)
    return center * lax.rsqrt(spread + epsilon) * gain


def hidden_norm(value, gain):
    return layer_norm(jax.nn.gelu(value, approximate=False), gain)


def column_product(left, right):
    return lax.dot_general(
        left, right, (((0,), (0,)), ((), ())), preferred_element_type=jnp.float32
    )


def times_transpose(left, matrix):
    return lax.dot_general(
        left, matrix, (((1,), (1,)), ((), ())), preferred_element_type=jnp.float32
    )


def toeplitz(diagonals, rows, cols):
    heads = diagonals.shape[0]
    padded = jnp.pad(diagonals, ((0, 0), (0, 1)))
    stride = rows + cols - 1
    tiled = jnp.tile(padded, (1, rows))[:, : rows * stride].reshape(heads, rows, stride)
    return tiled[:, :, rows - 1 : rows - 1 + cols]


def diagonal_sums(grid):
    heads, rows, cols = grid.shape
    flipped = grid[:, ::-1, :]
    padded = jnp.pad(flipped, ((0, 0), (0, 0), (0, rows)))
    skewed = padded.reshape(heads, -1)[:, : rows * (rows + cols - 1)].reshape(
        heads, rows, rows + cols - 1
    )
    return jnp.sum(skewed, axis=1)


def by_sequence(
    tokens,
    lengths,
    distance_bucket,
    w_qkv,
    w_out,
    w_fc1,
    w_fc2,
    gain_in,
    gain_attn,
    gain_ffn_in,
    gain_hidden,
    head_scale,
    bias_table,
    cotangent,
):
    rows_here = tokens.shape[1]
    width = tokens.shape[2]
    heads = head_scale.shape[0]
    head_size = width // heads
    reach = distance_bucket.shape[0] // 2
    bucket_count = bias_table.shape[0]
    row_len = rows_here * lax.axis_size("blk")
    key_block = math.gcd(row_len, 512)
    block_count = row_len // key_block
    query_anchor = lax.axis_index("blk") * rows_here
    positions = query_anchor + jnp.arange(rows_here, dtype=jnp.int32)
    ends = jnp.cumsum(lengths[0])
    bucket_ids = jnp.arange(bucket_count, dtype=jnp.int32)

    def document_of(where):
        return jnp.sum((where[:, None] >= ends[None, :]).astype(jnp.int32), axis=1)

    query_docs = document_of(positions)

    def bucket_index(query_start, rows, key_start, cols):
        steps = jnp.arange(rows + cols - 1, dtype=jnp.int32)
        relative = key_start - query_start - (rows - 1) + steps
        return jnp.take(distance_bucket, jnp.clip(relative, -reach, reach) + reach)

    def scores_for(query_heads, query_start, query_doc, key_heads, key_start, key_doc):
        rows = query_heads.shape[0]
        cols = key_heads.shape[0]
        raw = jnp.einsum("qhd,khd->hqk", query_heads, key_heads, preferred_element_type=jnp.float32)
        buckets = bucket_index(query_start, rows, key_start, cols)
        diagonals = jnp.take(bias_table, buckets, axis=0).T
        same = query_doc[:, None] == key_doc[None, :]
        full = raw + toeplitz(diagonals, rows, cols)
        return (jnp.where(same[None], full, masked_score), same, buckets)

    residual_in = tokens[0].astype(jnp.float32)
    wqkv_all, wout_all = (
        lax.all_gather(w_qkv, ("dp", "blk"), axis=0, tiled=True),
        lax.all_gather(w_out, ("dp", "blk"), axis=0, tiled=True),
    )
    normed_f, norm_in_back = jax.vjp(layer_norm, residual_in, gain_in)
    normed_in = normed_f.astype(jnp.bfloat16)
    projected = jnp.dot(normed_in, wqkv_all, preferred_element_type=jnp.float32)
    queries = (projected[:, :width] * query_scale).astype(jnp.bfloat16)
    keys_here = projected[:, width : 2 * width].astype(jnp.bfloat16)
    values_here = projected[:, 2 * width :].astype(jnp.bfloat16)
    query_heads = queries.reshape(rows_here, heads, head_size)
    best = jnp.full((heads, rows_here), masked_score, jnp.float32)
    key_piece = lax.all_gather(keys_here, "blk", axis=0, tiled=True)
    value_piece = lax.all_gather(values_here, "blk", axis=0, tiled=True)
    length = key_piece.shape[0]
    key_pos = jnp.arange(length, dtype=jnp.int32)
    scores, same, buckets = scores_for(
        query_heads,
        query_anchor,
        query_docs,
        key_piece.reshape(length, heads, head_size),
        jnp.int32(0),
        document_of(key_pos),
    )
    new_best = jnp.maximum(best, jnp.max(scores, axis=-1))
    weights = jnp.where(same[None], jnp.exp(scores - new_best[..., None]), 0.0)
    total = jnp.sum(weights, axis=-1)
    accum = jnp.einsum(
        "hqk,khd->hqd",
        weights.astype(jnp.bfloat16),
        value_piece.reshape(length, heads, head_size),
        preferred_element_type=jnp.float32,
    )
    best, total, accum = (new_best, total, accum)
    log_total = best + jnp.log(total)
    attention = jnp.transpose(accum / total[..., None], (1, 0, 2)).reshape(rows_here, width)
    scale_cols = jnp.repeat(head_scale, head_size)
    scaled = (attention * scale_cols).astype(jnp.bfloat16)
    attn_out = jnp.dot(scaled, wout_all, preferred_element_type=jnp.float32)
    normed_attn, norm_attn_back = jax.vjp(layer_norm, attn_out, gain_attn)
    middle = residual_in + normed_attn
    fc1_all, fc2_all = (
        lax.all_gather(w_fc1, ("dp", "blk"), axis=0, tiled=True),
        lax.all_gather(w_fc2, ("dp", "blk"), axis=0, tiled=True),
    )
    normed_mid_f, norm_mid_back = jax.vjp(layer_norm, middle, gain_ffn_in)
    normed_mid = normed_mid_f.astype(jnp.bfloat16)
    hidden = jnp.dot(normed_mid, fc1_all, preferred_element_type=jnp.float32)
    activated_f, hidden_back = jax.vjp(hidden_norm, hidden, gain_hidden)
    activated = activated_f.astype(jnp.bfloat16)
    mixed = (middle + jnp.dot(activated, fc2_all, preferred_element_type=jnp.float32)).astype(
        jnp.bfloat16
    )
    grad_in = cotangent[0]
    fc1_back, fc2_back = (
        lax.all_gather(w_fc1, ("dp", "blk"), axis=0, tiled=True),
        lax.all_gather(w_fc2, ("dp", "blk"), axis=0, tiled=True),
    )
    grad_fc2 = lax.psum_scatter(
        column_product(activated, grad_in), ("dp", "blk"), scatter_dimension=0, tiled=True
    )
    d_activated = times_transpose(grad_in, fc2_back)
    d_hidden_f, grad_gain_hidden = hidden_back(d_activated)
    d_hidden = d_hidden_f.astype(jnp.bfloat16)
    grad_fc1 = lax.psum_scatter(
        column_product(normed_mid, d_hidden), ("dp", "blk"), scatter_dimension=0, tiled=True
    )
    d_mid_part, grad_gain_ffn_in = norm_mid_back(times_transpose(d_hidden, fc1_back))
    d_middle = grad_in.astype(jnp.float32) + d_mid_part
    d_attn_f, grad_gain_attn = norm_attn_back(d_middle)
    d_attn_out = d_attn_f.astype(jnp.bfloat16)
    qkv_back, out_back = (
        lax.all_gather(w_qkv, ("dp", "blk"), axis=0, tiled=True),
        lax.all_gather(w_out, ("dp", "blk"), axis=0, tiled=True),
    )
    grad_out = lax.psum_scatter(
        column_product(scaled, d_attn_out), ("dp", "blk"), scatter_dimension=0, tiled=True
    )
    d_scaled = times_transpose(d_attn_out, out_back)
    grad_scale = jnp.sum((d_scaled * attention).reshape(rows_here, heads, head_size), axis=(0, 2))
    d_attention = (d_scaled * scale_cols).astype(jnp.bfloat16)
    grad_heads = d_attention.reshape(rows_here, heads, head_size)
    row_delta = jnp.sum(
        (d_attention.astype(jnp.float32) * attention).reshape(rows_here, heads, head_size), axis=2
    ).T
    keys_back, values_back = (
        lax.all_gather(keys_here, "blk", axis=0, tiled=True),
        lax.all_gather(values_here, "blk", axis=0, tiled=True),
    )

    def pair_grads(
        query_part,
        grad_part,
        total_part,
        delta_part,
        query_start,
        query_doc,
        key_part,
        value_part,
        key_start,
        key_doc,
    ):
        scores, same, buckets = scores_for(
            query_part, query_start, query_doc, key_part, key_start, key_doc
        )
        probs = jnp.where(same[None], jnp.exp(scores - total_part[..., None]), 0.0)
        d_probs = jnp.einsum(
            "qhd,khd->hqk", grad_part, value_part, preferred_element_type=jnp.float32
        )
        d_scores = probs * (d_probs - delta_part[..., None])
        return (probs.astype(jnp.bfloat16), d_scores, buckets)

    def bias_sum(d_scores, buckets):
        sums = diagonal_sums(d_scores)
        selector = (buckets[:, None] == bucket_ids[None, :]).astype(jnp.float32)
        return jnp.dot(sums, selector, precision=highest).T

    def key_slices(index):
        begin = index * key_block
        key_part = lax.dynamic_slice_in_dim(keys_back, begin, key_block, 0).reshape(
            key_block, heads, head_size
        )
        value_part = lax.dynamic_slice_in_dim(values_back, begin, key_block, 0).reshape(
            key_block, heads, head_size
        )
        return (key_part, value_part, begin)

    query_carry = (
        jnp.zeros((rows_here, heads, head_size), jnp.float32),
        jnp.zeros((bucket_count, heads), jnp.float32),
    )

    def key_step(carry, index):
        d_query, d_bias = carry
        key_part, value_part, begin = key_slices(index)
        key_doc = document_of(begin + jnp.arange(key_block, dtype=jnp.int32))
        probs_low, d_scores, buckets = pair_grads(
            query_heads,
            grad_heads,
            log_total,
            row_delta,
            query_anchor,
            query_docs,
            key_part,
            value_part,
            begin,
            key_doc,
        )
        scores_low = d_scores.astype(jnp.bfloat16)
        d_query = d_query + jnp.einsum(
            "hqk,khd->qhd", scores_low, key_part, preferred_element_type=jnp.float32
        )
        d_key = jnp.einsum(
            "hqk,qhd->khd", scores_low, query_heads, preferred_element_type=jnp.float32
        ).reshape(key_block, width)
        d_value = jnp.einsum(
            "hqk,qhd->khd", probs_low, grad_heads, preferred_element_type=jnp.float32
        ).reshape(key_block, width)
        return (
            (d_query, d_bias + bias_sum(d_scores, buckets)),
            jnp.concatenate([d_key, d_value], axis=1),
        )

    (d_query, d_bias), kv_terms = lax.scan(
        key_step, query_carry, jnp.arange(block_count, dtype=jnp.int32)
    )
    kv_grad = lax.psum_scatter(
        kv_terms.reshape(row_len, 2 * width).astype(jnp.bfloat16),
        "blk",
        scatter_dimension=0,
        tiled=True,
    )
    d_query_low = d_query.reshape(rows_here, width).astype(jnp.bfloat16)
    d_projected = jnp.concatenate(
        [d_query_low * jnp.asarray(query_scale, jnp.bfloat16), kv_grad], axis=1
    )
    grad_qkv = lax.psum_scatter(
        column_product(normed_in, d_projected), ("dp", "blk"), scatter_dimension=0, tiled=True
    )
    d_input_part, grad_gain_in = norm_in_back(times_transpose(d_projected, qkv_back))
    grad_tokens = (d_middle + d_input_part).astype(jnp.bfloat16)[None]
    small = lax.psum(
        (grad_gain_in, grad_gain_attn, grad_gain_ffn_in, grad_gain_hidden, grad_scale, d_bias),
        ("dp", "blk"),
    )
    return (
        mixed[None],
        grad_tokens,
        grad_qkv,
        grad_out,
        grad_fc1,
        grad_fc2,
        small[0],
        small[1],
        small[2],
        small[3],
        small[4],
        small[5],
    )


lanes = 128
core_bit, x_bit, y_bit = 1, 2, 4


def swap(value, bit):
    size = lax.axis_size("dp")
    return lax.ppermute(value, "dp", [(i, i ^ bit) for i in range(size)])


def turn(value, steps):
    size = lax.axis_size("blk")
    return lax.ppermute(value, "blk", [(i, (i + steps) % size) for i in range(size)])


def swap_line(value, bit):
    size = lax.axis_size("blk")
    return lax.ppermute(value, "blk", [(i, i ^ bit) for i in range(size)])


def pick(stack, index):
    return lax.dynamic_index_in_dim(stack, index, 0, keepdims=False)


def place(blocks):
    shape = blocks[0][1].shape
    out = jnp.zeros((len(blocks),) + shape, blocks[0][1].dtype)
    for index, block in blocks:
        out = lax.dynamic_update_index_in_dim(out, block, index, 0)
    return out


def gather_line(value):
    here, size = lax.axis_index("blk"), lax.axis_size("blk")
    blocks = [(here, value)]
    for steps in range(1, size):
        blocks.append((lax.rem(here - steps + size, size), turn(value, steps)))
    out = place(blocks)
    return out.reshape((size * value.shape[0],) + value.shape[1:])


def deal_line(stack):
    here, size = lax.axis_index("blk"), lax.axis_size("blk")
    got = [pick(stack, here)]
    for steps in range(1, size):
        got.append(turn(pick(stack, lax.rem(here + steps, size)), steps))
    return got


def gather_planes(line):
    me = lax.axis_index("dp")
    half = line.shape[0] // 2
    along_x, along_y = swap(line, x_bit), swap(line, y_bit)
    across = jnp.concatenate([swap(along_y[:half], x_bit), swap(along_x[half:], y_bit)], axis=0)
    blocks = []
    for bits, block in ((0, line), (x_bit, along_x), (y_bit, along_y), (x_bit | y_bit, across)):
        blocks.append((me ^ bits, block))
        blocks.append((me ^ bits ^ core_bit, swap(block, core_bit)))
    out = place(blocks)
    return out.reshape((-1,) + line.shape[1:])


def gather_weight(shard):
    return gather_planes(gather_line(shard))


def add_low(left, right):
    return (left.astype(jnp.float32) + right.astype(jnp.float32)).astype(jnp.bfloat16)


def scatter_planes(block_of):
    me = lax.axis_index("dp")

    def with_core(bits):
        other = swap(block_of(me ^ bits ^ core_bit), core_bit)
        return add_low(block_of(me ^ bits), other)

    across = with_core(x_bit | y_bit)
    half = across.shape[0] // 2
    from_x, from_y = swap(across[:half], x_bit), swap(across[half:], y_bit)
    to_x, to_y, own = with_core(x_bit), with_core(y_bit), with_core(0)
    to_y = jnp.concatenate([add_low(to_y[:half], from_x), to_y[half:]], axis=0)
    to_x = jnp.concatenate([to_x[:half], add_low(to_x[half:], from_y)], axis=0)
    got_x, got_y = swap(to_x, x_bit), swap(to_y, y_bit)
    total = own.astype(jnp.float32) + got_x.astype(jnp.float32) + got_y.astype(jnp.float32)
    return total.astype(jnp.bfloat16)


def sum_parts(parts):
    total = parts[0].astype(jnp.float32)
    for part in parts[1:]:
        total = total + part.astype(jnp.float32)
    return total


def scatter_weight(block_of):
    size = lax.axis_size("blk")
    line = scatter_planes(block_of)
    return sum_parts(deal_line(line.reshape((size, -1) + line.shape[1:])))


def sum_everywhere(value):
    for bit in (core_bit, x_bit, y_bit):
        value = value + swap(value, bit)
    bit = 1
    while bit < lax.axis_size("blk"):
        value = value + swap_line(value, bit)
        bit *= 2
    return value


def contract(left, right, left_axis, right_axis):
    return lax.dot_general(
        left, right, (((left_axis,), (right_axis,)), ((), ())), preferred_element_type=jnp.float32
    )


def attend_kernel(
    heads, head_size, qkv_ref, diagonal_ref, doc_col_ref, doc_row_ref, scale_ref, probs_ref, attention_ref, scaled_ref, bias
):
    length = qkv_ref.shape[0]
    blocks = length // lanes
    width = heads * head_size
    for head in range(heads):
        for step in range(2 * blocks - 1):
            window = diagonal_ref[head : head + 1, step * lanes : (step + 2) * lanes]
            window = jnp.broadcast_to(window, (lanes, 2 * lanes))
            window = pltpu.roll(window, 0, 1, stride=1, stride_axis=0)
            bias[:, step * lanes : (step + 1) * lanes] = window[:, lanes:]
        low = head * head_size
        keys = qkv_ref[:, width + low : width + low + head_size]
        values = qkv_ref[:, 2 * width + low : 2 * width + low + head_size]
        for block in range(blocks):
            rows = slice(block * lanes, (block + 1) * lanes)
            first = (blocks - 1 - block) * lanes
            scores = contract(qkv_ref[rows, low : low + head_size], keys, 1, 1)
            scores = scores + bias[:, first : first + length]
            same = doc_col_ref[rows, :] == doc_row_ref[...]
            scores = jnp.where(same, scores, masked_score)
            weights = jnp.exp(scores - jnp.max(scores, axis=1, keepdims=True))
            probs = weights * (1.0 / jnp.sum(weights, axis=1, keepdims=True))
            probs = probs.astype(jnp.bfloat16)
            probs_ref[head, rows, :] = probs
            attention_ref[rows, low : low + head_size] = contract(probs, values, 1, 0)
    scaled_ref[...] = (attention_ref[...] * scale_ref[...]).astype(jnp.bfloat16)


def attend(qkv, diagonals, doc_col, doc_row, scale_cols, heads, head_size):
    length, width = qkv.shape[0], heads * head_size
    return pl.pallas_call(
        functools.partial(attend_kernel, heads, head_size),
        out_shape=(
            jax.ShapeDtypeStruct((heads, length, length), jnp.bfloat16),
            jax.ShapeDtypeStruct((length, width), jnp.float32),
            jax.ShapeDtypeStruct((length, width), jnp.bfloat16),
        ),
        scratch_shapes=[pltpu.VMEM((lanes, 2 * length - lanes), jnp.float32)],
        compiler_params=pltpu.CompilerParams(vmem_limit_bytes=40 * 2**20),
        cost_estimate=pl.CostEstimate(
            flops=4 * heads * length * length * head_size,
            bytes_accessed=2 * heads * length * length,
            transcendentals=heads * length * length,
        ),
        name="attend",
    )(qkv, diagonals, doc_col, doc_row, scale_cols)


def attend_back_kernel(
    heads, head_size, qkv_ref, probs_ref, attention_ref, grad_ref, out_ref, diagonal_ref, delta_ref, sums
):
    length = qkv_ref.shape[0]
    blocks = length // lanes
    width = heads * head_size
    diagonal_ref[...] = jnp.zeros_like(diagonal_ref)
    for head in range(heads):
        sums[...] = jnp.zeros_like(sums)
        low = head * head_size
        keys = qkv_ref[:, width + low : width + low + head_size]
        values = qkv_ref[:, 2 * width + low : 2 * width + low + head_size]
        d_keys = jnp.zeros((head_size, length), jnp.float32)
        d_values = jnp.zeros((head_size, length), jnp.float32)
        for block in range(blocks):
            rows = slice(block * lanes, (block + 1) * lanes)
            first = (blocks - 1 - block) * lanes
            queries = qkv_ref[rows, low : low + head_size]
            grad = grad_ref[rows, low : low + head_size]
            probs = probs_ref[head, rows, :]
            part = grad.astype(jnp.float32) * attention_ref[rows, low : low + head_size]
            delta = jnp.sum(part, axis=1, keepdims=True)
            delta_ref[rows, head : head + 1] = delta
            d_scores = probs.astype(jnp.float32) * (contract(grad, values, 1, 1) - delta)
            sums[:, first : first + length] += d_scores
            d_scores = d_scores.astype(jnp.bfloat16)
            d_query = contract(d_scores, keys, 1, 0).astype(jnp.bfloat16)
            out_ref[rows, low : low + head_size] = d_query * jnp.asarray(query_scale, jnp.bfloat16)
            d_keys = d_keys + contract(queries, d_scores, 0, 0)
            d_values = d_values + contract(grad, probs, 0, 0)
        out_ref[:, width + low : width + low + head_size] = d_keys.T.astype(jnp.bfloat16)
        out_ref[:, 2 * width + low : 2 * width + low + head_size] = d_values.T.astype(jnp.bfloat16)
        row_ids = lax.broadcasted_iota(jnp.int32, (lanes, lanes), 0)
        col_ids = lax.broadcasted_iota(jnp.int32, (lanes, lanes), 1)
        reverse = (row_ids + col_ids == lanes - 1).astype(jnp.float32)
        flipped = jnp.dot(reverse, sums[...], precision=highest)
        for step in range(2 * blocks - 1):
            window = flipped[:, step * lanes : (step + 1) * lanes]
            window = jnp.concatenate([window, jnp.zeros_like(window)], axis=1)
            window = pltpu.roll(window, 1, 1, stride=1, stride_axis=0)
            diagonal_ref[head : head + 1, step * lanes : (step + 2) * lanes] += jnp.sum(
                window, axis=0, keepdims=True
            )


def attend_back(qkv, probs, attention, grad, heads, head_size):
    length, width = qkv.shape[0], heads * head_size
    return pl.pallas_call(
        functools.partial(attend_back_kernel, heads, head_size),
        out_shape=(
            jax.ShapeDtypeStruct((length, 3 * width), jnp.bfloat16),
            jax.ShapeDtypeStruct((heads, 2 * length), jnp.float32),
            jax.ShapeDtypeStruct((length, heads), jnp.float32),
        ),
        scratch_shapes=[pltpu.VMEM((lanes, 2 * length - lanes), jnp.float32)],
        compiler_params=pltpu.CompilerParams(vmem_limit_bytes=40 * 2**20),
        cost_estimate=pl.CostEstimate(
            flops=8 * heads * length * length * head_size,
            bytes_accessed=2 * heads * length * length,
            transcendentals=0,
        ),
        name="attend_back",
    )(qkv, probs, attention, grad)


def by_heads(
    tokens,
    lengths,
    distance_bucket,
    w_qkv,
    w_out,
    w_fc1,
    w_fc2,
    gain_in,
    gain_attn,
    gain_ffn_in,
    gain_hidden,
    head_scale,
    bias_table,
    cotangent,
):
    here, line_size = lax.axis_index("blk"), lax.axis_size("blk")
    rows_here, width = tokens.shape[1], tokens.shape[2]
    row_len = rows_here * line_size
    all_heads = head_scale.shape[0]
    head_size = width // all_heads
    heads = all_heads // line_size
    part = heads * head_size
    reach = distance_bucket.shape[0] // 2
    bucket_count = bias_table.shape[0]
    shard_rows = w_qkv.shape[0]

    row_tokens = gather_line(tokens[0])
    by_head = w_qkv.reshape(shard_rows, 3, line_size, part).transpose(2, 0, 1, 3)
    by_head = by_head.reshape(line_size, shard_rows, 3 * part)
    dealt = deal_line(by_head)
    qkv_line = place(
        [(lax.rem(here - steps + line_size, line_size), block) for steps, block in enumerate(dealt)]
    ).reshape(line_size * shard_rows, 3 * part)
    wqkv_part = gather_planes(qkv_line)
    wout_all = gather_weight(w_out)
    fc1_all = gather_weight(w_fc1)
    fc2_all = gather_weight(w_fc2)

    ends = jnp.cumsum(lengths[0])
    positions = jnp.arange(row_len, dtype=jnp.int32)
    documents = jnp.sum((positions[:, None] >= ends[None, :]).astype(jnp.int32), axis=1)
    relative = jnp.clip(jnp.arange(-row_len, row_len, dtype=jnp.int32), -reach, reach) + reach
    buckets = jnp.take(distance_bucket, relative)
    selector = (buckets[None, :] == jnp.arange(bucket_count, dtype=jnp.int32)[:, None]).astype(jnp.float32)
    head_table = lax.dynamic_slice_in_dim(bias_table.T, here * heads, heads, 0)
    diagonals = jnp.dot(head_table, selector, precision=highest)
    scale_cols = jnp.repeat(head_scale, head_size)
    head_cols = lax.dynamic_slice_in_dim(scale_cols, here * part, part, 0)[None, :]

    row_in = row_tokens.astype(jnp.float32)
    normed_row = layer_norm(row_in, gain_in).astype(jnp.bfloat16)
    projected = jnp.dot(normed_row, wqkv_part, preferred_element_type=jnp.float32)
    column_scale = jnp.where(jnp.arange(3 * part) < part, query_scale, 1.0)
    qkv = (projected * column_scale).astype(jnp.bfloat16)
    probs, attention, scaled_part = attend(
        qkv, diagonals, documents[:, None], documents[None, :], head_cols, heads, head_size
    )

    def arrival(stack):
        return jnp.concatenate(
            [pick(stack, lax.rem(here - steps + line_size, line_size)) for steps in range(line_size)], axis=0
        )

    scaled = jnp.concatenate(deal_line(scaled_part.reshape(line_size, rows_here, part)), axis=1)
    wout_here = arrival(wout_all.reshape(line_size, part, width))
    residual_in = tokens[0].astype(jnp.float32)
    attn_out = jnp.dot(scaled, wout_here, preferred_element_type=jnp.float32)
    normed_attn, norm_attn_back = jax.vjp(layer_norm, attn_out, gain_attn)
    middle = residual_in + normed_attn
    normed_mid_f, norm_mid_back = jax.vjp(layer_norm, middle, gain_ffn_in)
    normed_mid = normed_mid_f.astype(jnp.bfloat16)
    hidden = jnp.dot(normed_mid, fc1_all, preferred_element_type=jnp.float32)
    activated_f, hidden_back = jax.vjp(hidden_norm, hidden, gain_hidden)
    activated = activated_f.astype(jnp.bfloat16)
    mixed = (middle + jnp.dot(activated, fc2_all, preferred_element_type=jnp.float32)).astype(
        jnp.bfloat16
    )

    def blocks_of(grad):
        stack = grad.astype(jnp.bfloat16).reshape((lax.axis_size("dp"), -1) + grad.shape[1:])
        return lambda index: pick(stack, index)

    grad_in = cotangent[0]
    grad_fc2 = scatter_weight(blocks_of(column_product(activated, grad_in)))
    d_activated = times_transpose(grad_in, fc2_all)
    d_hidden_f, grad_gain_hidden = hidden_back(d_activated)
    d_hidden = d_hidden_f.astype(jnp.bfloat16)
    grad_fc1 = scatter_weight(blocks_of(column_product(normed_mid, d_hidden)))
    d_mid_part, grad_gain_ffn_in = norm_mid_back(times_transpose(d_hidden, fc1_all))
    d_middle = grad_in.astype(jnp.float32) + d_mid_part
    d_attn_f, grad_gain_attn = norm_attn_back(d_middle)
    d_attn_out = d_attn_f.astype(jnp.bfloat16)

    scale_here = arrival(scale_cols.reshape(line_size, part))
    d_scaled = times_transpose(d_attn_out, wout_here)
    d_attention = (d_scaled * scale_here).astype(jnp.bfloat16)
    pieces = [(here, d_attention[:, :part])]
    for steps in range(1, line_size):
        piece = d_attention[:, steps * part : (steps + 1) * part]
        pieces.append((lax.rem(here + steps, line_size), turn(piece, line_size - steps)))
    grad_row = place(pieces).reshape(row_len, part)

    out_grad = blocks_of(column_product(scaled, d_attn_out))
    per_part = lax.axis_size("dp") // line_size

    def out_block(index):
        owner = lax.div(index, per_part)
        steps = lax.rem(here - owner + line_size, line_size)
        return out_grad(steps * per_part + lax.rem(index, per_part))

    grad_out = scatter_weight(out_block)

    d_projected, diagonal_sums_here, deltas = attend_back(qkv, probs, attention, grad_row, heads, head_size)
    d_normed = times_transpose(d_projected, wqkv_part)
    d_normed_low = d_normed.astype(jnp.bfloat16).reshape(line_size, rows_here, width)
    d_normed_here = sum_parts(deal_line(d_normed_low))
    qkv_line_grad = scatter_planes(blocks_of(column_product(normed_row, d_projected)))
    qkv_dealt = deal_line(qkv_line_grad.reshape(line_size, shard_rows, 3 * part))
    grad_qkv = place(
        [
            (lax.rem(here - steps + line_size, line_size), block.astype(jnp.float32))
            for steps, block in enumerate(qkv_dealt)
        ]
    )
    grad_qkv = grad_qkv.reshape(line_size, shard_rows, 3, part).transpose(1, 2, 0, 3)
    grad_qkv = grad_qkv.reshape(shard_rows, 3 * width)

    _, gain_in_back = jax.vjp(lambda gain: layer_norm(row_in, gain), gain_in)
    (grad_gain_in,) = gain_in_back(d_normed)
    _, norm_in_back = jax.vjp(lambda value: layer_norm(value, gain_in), residual_in)
    (d_input_part,) = norm_in_back(d_normed_here)
    grad_tokens = (d_middle + d_input_part).astype(jnp.bfloat16)[None]

    d_table = lax.dot_general(
        diagonal_sums_here, selector, (((1,), (1,)), ((), ())), precision=highest
    )
    d_bias = lax.dynamic_update_slice_in_dim(
        jnp.zeros((all_heads, bucket_count), jnp.float32), d_table, here * heads, 0
    )
    scale_part = jnp.sum(deltas, axis=0)
    grad_scale = lax.dynamic_update_slice_in_dim(
        jnp.zeros((all_heads,), jnp.float32), scale_part, here * heads, 0
    )
    small = (grad_gain_in, grad_gain_attn, grad_gain_ffn_in, grad_gain_hidden, grad_scale, d_bias)
    sizes = [math.prod(value.shape) for value in small]
    flat = jnp.concatenate([value.reshape(-1) for value in small])
    flat = jnp.pad(flat, (0, -flat.shape[0] % 1024)).reshape(-1, lanes)
    flat = sum_everywhere(flat).reshape(-1)
    sums, begin = [], 0
    for value, size in zip(small, sizes):
        sums.append(flat[begin : begin + size].reshape(value.shape))
        begin += size
    return (
        mixed[None],
        grad_tokens,
        grad_qkv,
        grad_out,
        grad_fc1,
        grad_fc2,
        sums[0],
        sums[1],
        sums[2],
        sums[3],
        sums[4] / head_scale,
        sums[5].T,
    )


def on_device(dp_size, line_size, tokens, *rest):
    head_scale, row_len = rest[10], tokens.shape[1] * line_size
    whole_heads = head_scale.shape[0] % line_size == 0 and dp_size % line_size == 0
    if dp_size == 8 and line_size == 4 and whole_heads and row_len % lanes == 0:
        return by_heads(tokens, *rest)
    return by_sequence(tokens, *rest)


def solution(mesh):
    return jax.shard_map(
        functools.partial(on_device, mesh.shape["dp"], mesh.shape["blk"]),
        mesh=mesh,
        in_specs=(
            P("dp", "blk", None),
            P("dp", None),
            P(),
            P(("dp", "blk"), None),
            P(("dp", "blk"), None),
            P(("dp", "blk"), None),
            P(("dp", "blk"), None),
            P(),
            P(),
            P(),
            P(),
            P(),
            P(),
            P("dp", "blk", None),
        ),
        out_specs=(
            P("dp", "blk", None),
            P("dp", "blk", None),
            P(("dp", "blk"), None),
            P(("dp", "blk"), None),
            P(("dp", "blk"), None),
            P(("dp", "blk"), None),
            P(),
            P(),
            P(),
            P(),
            P(),
            P(),
        ),
        check_vma=False,
    )
```

```python
import functools
import math

import jax
import jax.numpy as jnp
from jax import lax
from jax.experimental import pallas as pl
from jax.experimental.pallas import tpu as pltpu
from jax.sharding import PartitionSpec as P

epsilon = 1e-05
masked_score = -1e30
query_scale = 0.125
highest = lax.Precision.HIGHEST


def layer_norm(value, gain):
    center = value - jnp.mean(value, axis=-1, keepdims=True)
    spread = jnp.mean(center * center, axis=-1, keepdims=True)
    return center * lax.rsqrt(spread + epsilon) * gain


def hidden_norm(value, gain):
    return layer_norm(jax.nn.gelu(value, approximate=False), gain)


def column_product(left, right):
    return lax.dot_general(
        left, right, (((0,), (0,)), ((), ())), preferred_element_type=jnp.float32
    )


def times_transpose(left, matrix):
    return lax.dot_general(
        left, matrix, (((1,), (1,)), ((), ())), preferred_element_type=jnp.float32
    )


def toeplitz(diagonals, rows, cols):
    heads = diagonals.shape[0]
    padded = jnp.pad(diagonals, ((0, 0), (0, 1)))
    stride = rows + cols - 1
    tiled = jnp.tile(padded, (1, rows))[:, : rows * stride].reshape(heads, rows, stride)
    return tiled[:, :, rows - 1 : rows - 1 + cols]


def diagonal_sums(grid):
    heads, rows, cols = grid.shape
    flipped = grid[:, ::-1, :]
    padded = jnp.pad(flipped, ((0, 0), (0, 0), (0, rows)))
    skewed = padded.reshape(heads, -1)[:, : rows * (rows + cols - 1)].reshape(
        heads, rows, rows + cols - 1
    )
    return jnp.sum(skewed, axis=1)


def by_sequence(
    tokens,
    lengths,
    distance_bucket,
    w_qkv,
    w_out,
    w_fc1,
    w_fc2,
    gain_in,
    gain_attn,
    gain_ffn_in,
    gain_hidden,
    head_scale,
    bias_table,
    cotangent,
):
    rows_here = tokens.shape[1]
    width = tokens.shape[2]
    heads = head_scale.shape[0]
    head_size = width // heads
    reach = distance_bucket.shape[0] // 2
    bucket_count = bias_table.shape[0]
    row_len = rows_here * lax.axis_size("blk")
    key_block = math.gcd(row_len, 512)
    block_count = row_len // key_block
    query_anchor = lax.axis_index("blk") * rows_here
    positions = query_anchor + jnp.arange(rows_here, dtype=jnp.int32)
    ends = jnp.cumsum(lengths[0])
    bucket_ids = jnp.arange(bucket_count, dtype=jnp.int32)

    def document_of(where):
        return jnp.sum((where[:, None] >= ends[None, :]).astype(jnp.int32), axis=1)

    query_docs = document_of(positions)

    def bucket_index(query_start, rows, key_start, cols):
        steps = jnp.arange(rows + cols - 1, dtype=jnp.int32)
        relative = key_start - query_start - (rows - 1) + steps
        return jnp.take(distance_bucket, jnp.clip(relative, -reach, reach) + reach)

    def scores_for(query_heads, query_start, query_doc, key_heads, key_start, key_doc):
        rows = query_heads.shape[0]
        cols = key_heads.shape[0]
        raw = jnp.einsum("qhd,khd->hqk", query_heads, key_heads, preferred_element_type=jnp.float32)
        buckets = bucket_index(query_start, rows, key_start, cols)
        diagonals = jnp.take(bias_table, buckets, axis=0).T
        same = query_doc[:, None] == key_doc[None, :]
        full = raw + toeplitz(diagonals, rows, cols)
        return (jnp.where(same[None], full, masked_score), same, buckets)

    residual_in = tokens[0].astype(jnp.float32)
    wqkv_all, wout_all = (
        lax.all_gather(w_qkv, ("dp", "blk"), axis=0, tiled=True),
        lax.all_gather(w_out, ("dp", "blk"), axis=0, tiled=True),
    )
    normed_f, norm_in_back = jax.vjp(layer_norm, residual_in, gain_in)
    normed_in = normed_f.astype(jnp.bfloat16)
    projected = jnp.dot(normed_in, wqkv_all, preferred_element_type=jnp.float32)
    queries = (projected[:, :width] * query_scale).astype(jnp.bfloat16)
    keys_here = projected[:, width : 2 * width].astype(jnp.bfloat16)
    values_here = projected[:, 2 * width :].astype(jnp.bfloat16)
    query_heads = queries.reshape(rows_here, heads, head_size)
    best = jnp.full((heads, rows_here), masked_score, jnp.float32)
    key_piece = lax.all_gather(keys_here, "blk", axis=0, tiled=True)
    value_piece = lax.all_gather(values_here, "blk", axis=0, tiled=True)
    length = key_piece.shape[0]
    key_pos = jnp.arange(length, dtype=jnp.int32)
    scores, same, buckets = scores_for(
        query_heads,
        query_anchor,
        query_docs,
        key_piece.reshape(length, heads, head_size),
        jnp.int32(0),
        document_of(key_pos),
    )
    new_best = jnp.maximum(best, jnp.max(scores, axis=-1))
    weights = jnp.where(same[None], jnp.exp(scores - new_best[..., None]), 0.0)
    total = jnp.sum(weights, axis=-1)
    accum = jnp.einsum(
        "hqk,khd->hqd",
        weights.astype(jnp.bfloat16),
        value_piece.reshape(length, heads, head_size),
        preferred_element_type=jnp.float32,
    )
    best, total, accum = (new_best, total, accum)
    log_total = best + jnp.log(total)
    attention = jnp.transpose(accum / total[..., None], (1, 0, 2)).reshape(rows_here, width)
    scale_cols = jnp.repeat(head_scale, head_size)
    scaled = (attention * scale_cols).astype(jnp.bfloat16)
    attn_out = jnp.dot(scaled, wout_all, preferred_element_type=jnp.float32)
    normed_attn, norm_attn_back = jax.vjp(layer_norm, attn_out, gain_attn)
    middle = residual_in + normed_attn
    fc1_all, fc2_all = (
        lax.all_gather(w_fc1, ("dp", "blk"), axis=0, tiled=True),
        lax.all_gather(w_fc2, ("dp", "blk"), axis=0, tiled=True),
    )
    normed_mid_f, norm_mid_back = jax.vjp(layer_norm, middle, gain_ffn_in)
    normed_mid = normed_mid_f.astype(jnp.bfloat16)
    hidden = jnp.dot(normed_mid, fc1_all, preferred_element_type=jnp.float32)
    activated_f, hidden_back = jax.vjp(hidden_norm, hidden, gain_hidden)
    activated = activated_f.astype(jnp.bfloat16)
    mixed = (middle + jnp.dot(activated, fc2_all, preferred_element_type=jnp.float32)).astype(
        jnp.bfloat16
    )
    grad_in = cotangent[0]
    fc1_back, fc2_back = (
        lax.all_gather(w_fc1, ("dp", "blk"), axis=0, tiled=True),
        lax.all_gather(w_fc2, ("dp", "blk"), axis=0, tiled=True),
    )
    grad_fc2 = lax.psum_scatter(
        column_product(activated, grad_in), ("dp", "blk"), scatter_dimension=0, tiled=True
    )
    d_activated = times_transpose(grad_in, fc2_back)
    d_hidden_f, grad_gain_hidden = hidden_back(d_activated)
    d_hidden = d_hidden_f.astype(jnp.bfloat16)
    grad_fc1 = lax.psum_scatter(
        column_product(normed_mid, d_hidden), ("dp", "blk"), scatter_dimension=0, tiled=True
    )
    d_mid_part, grad_gain_ffn_in = norm_mid_back(times_transpose(d_hidden, fc1_back))
    d_middle = grad_in.astype(jnp.float32) + d_mid_part
    d_attn_f, grad_gain_attn = norm_attn_back(d_middle)
    d_attn_out = d_attn_f.astype(jnp.bfloat16)
    qkv_back, out_back = (
        lax.all_gather(w_qkv, ("dp", "blk"), axis=0, tiled=True),
        lax.all_gather(w_out, ("dp", "blk"), axis=0, tiled=True),
    )
    grad_out = lax.psum_scatter(
        column_product(scaled, d_attn_out), ("dp", "blk"), scatter_dimension=0, tiled=True
    )
    d_scaled = times_transpose(d_attn_out, out_back)
    grad_scale = jnp.sum((d_scaled * attention).reshape(rows_here, heads, head_size), axis=(0, 2))
    d_attention = (d_scaled * scale_cols).astype(jnp.bfloat16)
    grad_heads = d_attention.reshape(rows_here, heads, head_size)
    row_delta = jnp.sum(
        (d_attention.astype(jnp.float32) * attention).reshape(rows_here, heads, head_size), axis=2
    ).T
    keys_back, values_back = (
        lax.all_gather(keys_here, "blk", axis=0, tiled=True),
        lax.all_gather(values_here, "blk", axis=0, tiled=True),
    )

    def pair_grads(
        query_part,
        grad_part,
        total_part,
        delta_part,
        query_start,
        query_doc,
        key_part,
        value_part,
        key_start,
        key_doc,
    ):
        scores, same, buckets = scores_for(
            query_part, query_start, query_doc, key_part, key_start, key_doc
        )
        probs = jnp.where(same[None], jnp.exp(scores - total_part[..., None]), 0.0)
        d_probs = jnp.einsum(
            "qhd,khd->hqk", grad_part, value_part, preferred_element_type=jnp.float32
        )
        d_scores = probs * (d_probs - delta_part[..., None])
        return (probs.astype(jnp.bfloat16), d_scores, buckets)

    def bias_sum(d_scores, buckets):
        sums = diagonal_sums(d_scores)
        selector = (buckets[:, None] == bucket_ids[None, :]).astype(jnp.float32)
        return jnp.dot(sums, selector, precision=highest).T

    def key_slices(index):
        begin = index * key_block
        key_part = lax.dynamic_slice_in_dim(keys_back, begin, key_block, 0).reshape(
            key_block, heads, head_size
        )
        value_part = lax.dynamic_slice_in_dim(values_back, begin, key_block, 0).reshape(
            key_block, heads, head_size
        )
        return (key_part, value_part, begin)

    query_carry = (
        jnp.zeros((rows_here, heads, head_size), jnp.float32),
        jnp.zeros((bucket_count, heads), jnp.float32),
    )

    def key_step(carry, index):
        d_query, d_bias = carry
        key_part, value_part, begin = key_slices(index)
        key_doc = document_of(begin + jnp.arange(key_block, dtype=jnp.int32))
        probs_low, d_scores, buckets = pair_grads(
            query_heads,
            grad_heads,
            log_total,
            row_delta,
            query_anchor,
            query_docs,
            key_part,
            value_part,
            begin,
            key_doc,
        )
        scores_low = d_scores.astype(jnp.bfloat16)
        d_query = d_query + jnp.einsum(
            "hqk,khd->qhd", scores_low, key_part, preferred_element_type=jnp.float32
        )
        d_key = jnp.einsum(
            "hqk,qhd->khd", scores_low, query_heads, preferred_element_type=jnp.float32
        ).reshape(key_block, width)
        d_value = jnp.einsum(
            "hqk,qhd->khd", probs_low, grad_heads, preferred_element_type=jnp.float32
        ).reshape(key_block, width)
        return (
            (d_query, d_bias + bias_sum(d_scores, buckets)),
            jnp.concatenate([d_key, d_value], axis=1),
        )

    (d_query, d_bias), kv_terms = lax.scan(
        key_step, query_carry, jnp.arange(block_count, dtype=jnp.int32)
    )
    kv_grad = lax.psum_scatter(
        kv_terms.reshape(row_len, 2 * width).astype(jnp.bfloat16),
        "blk",
        scatter_dimension=0,
        tiled=True,
    )
    d_query_low = d_query.reshape(rows_here, width).astype(jnp.bfloat16)
    d_projected = jnp.concatenate(
        [d_query_low * jnp.asarray(query_scale, jnp.bfloat16), kv_grad], axis=1
    )
    grad_qkv = lax.psum_scatter(
        column_product(normed_in, d_projected), ("dp", "blk"), scatter_dimension=0, tiled=True
    )
    d_input_part, grad_gain_in = norm_in_back(times_transpose(d_projected, qkv_back))
    grad_tokens = (d_middle + d_input_part).astype(jnp.bfloat16)[None]
    small = lax.psum(
        (grad_gain_in, grad_gain_attn, grad_gain_ffn_in, grad_gain_hidden, grad_scale, d_bias),
        ("dp", "blk"),
    )
    return (
        mixed[None],
        grad_tokens,
        grad_qkv,
        grad_out,
        grad_fc1,
        grad_fc2,
        small[0],
        small[1],
        small[2],
        small[3],
        small[4],
        small[5],
    )


lanes = 128
core_bit, x_bit, y_bit = 1, 2, 4


def swap(value, bit):
    size = lax.axis_size("dp")
    return lax.ppermute(value, "dp", [(i, i ^ bit) for i in range(size)])


def turn(value, steps):
    size = lax.axis_size("blk")
    return lax.ppermute(value, "blk", [(i, (i + steps) % size) for i in range(size)])


def swap_line(value, bit):
    size = lax.axis_size("blk")
    return lax.ppermute(value, "blk", [(i, i ^ bit) for i in range(size)])


def pick(stack, index):
    return lax.dynamic_index_in_dim(stack, index, 0, keepdims=False)


def place(blocks):
    shape = blocks[0][1].shape
    out = jnp.zeros((len(blocks),) + shape, blocks[0][1].dtype)
    for index, block in blocks:
        out = lax.dynamic_update_index_in_dim(out, block, index, 0)
    return out


def after(value, *others):
    return lax.optimization_barrier((value, *others))[0]


def all_after(values, *others):
    return list(lax.optimization_barrier((*values, *others))[: len(values)])


def turns(value):
    size = lax.axis_size("blk")
    return [value] + [turn(value, steps) for steps in range(1, size)]


def in_line(pieces):
    here, size = lax.axis_index("blk"), lax.axis_size("blk")
    ordered = [lax.select_n(lax.rem(here - owner + size, size), *pieces) for owner in range(size)]
    return jnp.concatenate(ordered, axis=0)


def deal_line(stack):
    here, size = lax.axis_index("blk"), lax.axis_size("blk")
    got = [pick(stack, here)]
    for steps in range(1, size):
        got.append(turn(pick(stack, lax.rem(here + steps, size)), steps))
    return got


def swap_cores(blocks):
    return [swap(block, core_bit) for block in blocks]


def in_planes(blocks, others, cut):
    me = lax.axis_index("dp")
    bits = (0, x_bit, y_bit, x_bit | y_bit)
    both = [(me ^ bit, block) for bit, block in zip(bits, blocks)]
    both += [(me ^ bit ^ core_bit, block) for bit, block in zip(bits, others)]
    outs = []
    for begin, end in cut:
        out = place([(index, block[:, begin:end]) for index, block in both])
        outs.append(out.reshape((-1, end - begin)))
    return outs


def beside(line):
    return [line, swap(line, x_bit), swap(line, y_bit)]


def across_plane(near):
    line, along_x, along_y = near
    half = line.shape[0] // 2
    across = [swap(along_y[:half], x_bit), swap(along_x[half:], y_bit)]
    return [line, along_x, along_y, jnp.concatenate(across, axis=0)]


def near_planes(line):
    return beside(line) + [swap(line, x_bit | y_bit)]


def add_low(left, right):
    return (left.astype(jnp.float32) + right.astype(jnp.float32)).astype(jnp.bfloat16)


def add_cores(block_of):
    me = lax.axis_index("dp")
    order = (x_bit | y_bit, x_bit, y_bit, 0)
    got = swap_cores([block_of(me ^ bits ^ core_bit) for bits in order])
    return [add_low(block_of(me ^ bits), term) for bits, term in zip(order, got)]


def add_across(across, to_x, to_y):
    half = across.shape[0] // 2
    from_x, from_y = swap(across[:half], x_bit), swap(across[half:], y_bit)
    to_y = jnp.concatenate([add_low(to_y[:half], from_x), to_y[half:]], axis=0)
    to_x = jnp.concatenate([to_x[:half], add_low(to_x[half:], from_y)], axis=0)
    return to_x, to_y


def add_planes(to_x, to_y, own):
    got_x, got_y = swap(to_x, x_bit), swap(to_y, y_bit)
    total = own.astype(jnp.float32) + got_x.astype(jnp.float32) + got_y.astype(jnp.float32)
    return total.astype(jnp.bfloat16)


def sum_parts(parts):
    total = parts[0].astype(jnp.float32)
    for part in parts[1:]:
        total = total + part.astype(jnp.float32)
    return total


def add_line(line):
    size = lax.axis_size("blk")
    return sum_parts(deal_line(line.reshape((size, -1) + line.shape[1:])))


def sum_everywhere(value):
    for bit in (core_bit, x_bit, y_bit):
        value = value + swap(value, bit)
    bit = 1
    while bit < lax.axis_size("blk"):
        value = value + swap_line(value, bit)
        bit *= 2
    return value


def contract(left, right, left_axis, right_axis):
    return lax.dot_general(
        left, right, (((left_axis,), (right_axis,)), ((), ())), preferred_element_type=jnp.float32
    )


def attend_kernel(
    heads, head_size, qkv_ref, diagonal_ref, doc_col_ref, doc_row_ref, scale_ref, probs_ref, attention_ref, scaled_ref, bias
):
    length = qkv_ref.shape[0]
    blocks = length // lanes
    width = heads * head_size
    for head in range(heads):
        for step in range(2 * blocks - 1):
            window = diagonal_ref[head : head + 1, step * lanes : (step + 2) * lanes]
            window = jnp.broadcast_to(window, (lanes, 2 * lanes))
            window = pltpu.roll(window, 0, 1, stride=1, stride_axis=0)
            bias[:, step * lanes : (step + 1) * lanes] = window[:, lanes:]
        low = head * head_size
        keys = qkv_ref[:, width + low : width + low + head_size]
        values = qkv_ref[:, 2 * width + low : 2 * width + low + head_size]
        for block in range(blocks):
            rows = slice(block * lanes, (block + 1) * lanes)
            first = (blocks - 1 - block) * lanes
            scores = contract(qkv_ref[rows, low : low + head_size], keys, 1, 1)
            scores = scores + bias[:, first : first + length]
            same = doc_col_ref[rows, :] == doc_row_ref[...]
            scores = jnp.where(same, scores, masked_score)
            weights = jnp.exp(scores - jnp.max(scores, axis=1, keepdims=True))
            probs = weights * (1.0 / jnp.sum(weights, axis=1, keepdims=True))
            probs = probs.astype(jnp.bfloat16)
            probs_ref[head, rows, :] = probs
            attention_ref[rows, low : low + head_size] = contract(probs, values, 1, 0)
    scaled_ref[...] = (attention_ref[...] * scale_ref[...]).astype(jnp.bfloat16)


def attend(qkv, diagonals, doc_col, doc_row, scale_cols, heads, head_size):
    length, width = qkv.shape[0], heads * head_size
    return pl.pallas_call(
        functools.partial(attend_kernel, heads, head_size),
        out_shape=(
            jax.ShapeDtypeStruct((heads, length, length), jnp.bfloat16),
            jax.ShapeDtypeStruct((length, width), jnp.float32),
            jax.ShapeDtypeStruct((length, width), jnp.bfloat16),
        ),
        scratch_shapes=[pltpu.VMEM((lanes, 2 * length - lanes), jnp.float32)],
        compiler_params=pltpu.CompilerParams(vmem_limit_bytes=40 * 2**20),
        cost_estimate=pl.CostEstimate(
            flops=4 * heads * length * length * head_size,
            bytes_accessed=2 * heads * length * length,
            transcendentals=heads * length * length,
        ),
        name="attend",
    )(qkv, diagonals, doc_col, doc_row, scale_cols)


def attend_back_kernel(
    heads, head_size, qkv_ref, probs_ref, attention_ref, grad_ref, out_ref, diagonal_ref, delta_ref, sums
):
    length = qkv_ref.shape[0]
    blocks = length // lanes
    width = heads * head_size
    diagonal_ref[...] = jnp.zeros_like(diagonal_ref)
    for head in range(heads):
        sums[...] = jnp.zeros_like(sums)
        low = head * head_size
        keys = qkv_ref[:, width + low : width + low + head_size]
        values = qkv_ref[:, 2 * width + low : 2 * width + low + head_size]
        d_keys = jnp.zeros((head_size, length), jnp.float32)
        d_values = jnp.zeros((head_size, length), jnp.float32)
        for block in range(blocks):
            rows = slice(block * lanes, (block + 1) * lanes)
            first = (blocks - 1 - block) * lanes
            queries = qkv_ref[rows, low : low + head_size]
            grad = grad_ref[rows, low : low + head_size]
            probs = probs_ref[head, rows, :]
            part = grad.astype(jnp.float32) * attention_ref[rows, low : low + head_size]
            delta = jnp.sum(part, axis=1, keepdims=True)
            delta_ref[rows, head : head + 1] = delta
            d_scores = probs.astype(jnp.float32) * (contract(grad, values, 1, 1) - delta)
            sums[:, first : first + length] += d_scores
            d_scores = d_scores.astype(jnp.bfloat16)
            d_query = contract(d_scores, keys, 1, 0).astype(jnp.bfloat16)
            out_ref[rows, low : low + head_size] = d_query * jnp.asarray(query_scale, jnp.bfloat16)
            d_keys = d_keys + contract(queries, d_scores, 0, 0)
            d_values = d_values + contract(grad, probs, 0, 0)
        out_ref[:, width + low : width + low + head_size] = d_keys.T.astype(jnp.bfloat16)
        out_ref[:, 2 * width + low : 2 * width + low + head_size] = d_values.T.astype(jnp.bfloat16)
        row_ids = lax.broadcasted_iota(jnp.int32, (lanes, lanes), 0)
        col_ids = lax.broadcasted_iota(jnp.int32, (lanes, lanes), 1)
        reverse = (row_ids + col_ids == lanes - 1).astype(jnp.float32)
        flipped = jnp.dot(reverse, sums[...], precision=highest)
        for step in range(2 * blocks - 1):
            window = flipped[:, step * lanes : (step + 1) * lanes]
            window = jnp.concatenate([window, jnp.zeros_like(window)], axis=1)
            window = pltpu.roll(window, 1, 1, stride=1, stride_axis=0)
            diagonal_ref[head : head + 1, step * lanes : (step + 2) * lanes] += jnp.sum(
                window, axis=0, keepdims=True
            )


def attend_back(qkv, probs, attention, grad, heads, head_size):
    length, width = qkv.shape[0], heads * head_size
    return pl.pallas_call(
        functools.partial(attend_back_kernel, heads, head_size),
        out_shape=(
            jax.ShapeDtypeStruct((length, 3 * width), jnp.bfloat16),
            jax.ShapeDtypeStruct((heads, 2 * length), jnp.float32),
            jax.ShapeDtypeStruct((length, heads), jnp.float32),
        ),
        scratch_shapes=[pltpu.VMEM((lanes, 2 * length - lanes), jnp.float32)],
        compiler_params=pltpu.CompilerParams(vmem_limit_bytes=40 * 2**20),
        cost_estimate=pl.CostEstimate(
            flops=8 * heads * length * length * head_size,
            bytes_accessed=2 * heads * length * length,
            transcendentals=0,
        ),
        name="attend_back",
    )(qkv, probs, attention, grad)


def by_heads(
    tokens,
    lengths,
    distance_bucket,
    w_qkv,
    w_out,
    w_fc1,
    w_fc2,
    gain_in,
    gain_attn,
    gain_ffn_in,
    gain_hidden,
    head_scale,
    bias_table,
    cotangent,
):
    here, line_size = lax.axis_index("blk"), lax.axis_size("blk")
    rows_here, width = tokens.shape[1], tokens.shape[2]
    row_len = rows_here * line_size
    all_heads = head_scale.shape[0]
    head_size = width // all_heads
    heads = all_heads // line_size
    part = heads * head_size
    reach = distance_bucket.shape[0] // 2
    bucket_count = bias_table.shape[0]
    shard_rows = w_qkv.shape[0]

    hidden_width = w_fc1.shape[1]
    summed = hidden_width + width
    by_head = w_qkv.reshape(shard_rows, 3, line_size, part).transpose(2, 0, 1, 3)
    by_head = by_head.reshape(line_size, shard_rows, 3 * part)
    shared = jnp.broadcast_to(
        jnp.concatenate([w_fc1, w_out], axis=1)[None], (line_size, shard_rows, summed)
    )
    first_pieces = deal_line(jnp.concatenate([shared, by_head], axis=2))
    first_line = in_line(first_pieces)
    row_tokens = lax.all_gather(after(tokens[0], *first_pieces[1:]), "blk", axis=0, tiled=True)
    second_pieces = turns(after(w_fc2, first_line))
    first_planes = across_plane(beside(first_line))
    first_others = swap_cores(first_planes)
    fc1_all, wout_all, wqkv_part = in_planes(
        first_planes, first_others, [(0, hidden_width), (hidden_width, summed), (summed, summed + 3 * part)]
    )
    second_near = beside(after(in_line(second_pieces), *first_planes))

    ends = jnp.cumsum(lengths[0])
    positions = jnp.arange(row_len, dtype=jnp.int32)
    documents = jnp.sum((positions[:, None] >= ends[None, :]).astype(jnp.int32), axis=1)
    if row_len <= reach:
        buckets = distance_bucket[reach - row_len : reach + row_len]
    else:
        buckets = jnp.pad(distance_bucket, row_len - reach, mode="edge")[: 2 * row_len]
    selector = (buckets[None, :] == jnp.arange(bucket_count, dtype=jnp.int32)[:, None]).astype(jnp.float32)
    head_table = lax.dynamic_slice_in_dim(bias_table.T, here * heads, heads, 0)
    diagonals = jnp.dot(head_table, selector, precision=highest)
    scale_cols = jnp.repeat(head_scale, head_size)
    head_cols = lax.dynamic_slice_in_dim(scale_cols, here * part, part, 0)[None, :]

    row_in = row_tokens.astype(jnp.float32)
    normed_row = layer_norm(row_in, gain_in).astype(jnp.bfloat16)
    projected = jnp.dot(normed_row, wqkv_part, preferred_element_type=jnp.float32)
    column_scale = jnp.where(jnp.arange(3 * part) < part, query_scale, 1.0)
    qkv = (projected * column_scale).astype(jnp.bfloat16)
    probs, attention, scaled_part = attend(
        qkv, diagonals, documents[:, None], documents[None, :], head_cols, heads, head_size
    )

    def arrival(stack):
        return jnp.concatenate(
            [pick(stack, lax.rem(here - steps + line_size, line_size)) for steps in range(line_size)], axis=0
        )

    dealt = deal_line(scaled_part.reshape(line_size, rows_here, part))
    scaled = jnp.concatenate(dealt, axis=1)
    wout_here = arrival(wout_all.reshape(line_size, part, width))
    residual_in = tokens[0].astype(jnp.float32)
    attn_out = jnp.dot(scaled, wout_here, preferred_element_type=jnp.float32)
    normed_attn, norm_attn_back = jax.vjp(layer_norm, attn_out, gain_attn)
    middle = residual_in + normed_attn
    normed_mid_f, norm_mid_back = jax.vjp(layer_norm, middle, gain_ffn_in)
    normed_mid = normed_mid_f.astype(jnp.bfloat16)
    hidden = jnp.dot(normed_mid, fc1_all, preferred_element_type=jnp.float32)
    second_planes = across_plane(all_after(second_near, *first_others))
    (fc2_all,) = in_planes(second_planes, swap_cores(second_planes), [(0, width)])
    activated_f, hidden_back = jax.vjp(hidden_norm, hidden, gain_hidden)
    activated = activated_f.astype(jnp.bfloat16)
    mixed = (middle + jnp.dot(activated, fc2_all, preferred_element_type=jnp.float32)).astype(
        jnp.bfloat16
    )

    def blocks_of(grad):
        stack = grad.astype(jnp.bfloat16).reshape((lax.axis_size("dp"), -1) + grad.shape[1:])
        return lambda index: pick(stack, index)

    grad_in = cotangent[0]
    second = add_cores(blocks_of(column_product(activated, grad_in)))
    d_activated = times_transpose(grad_in, fc2_all)
    d_hidden_f, grad_gain_hidden = hidden_back(d_activated)
    d_hidden = after(d_hidden_f.astype(jnp.bfloat16), *second)
    third = add_cores(blocks_of(column_product(normed_mid, d_hidden)))
    d_mid_part, grad_gain_ffn_in = norm_mid_back(times_transpose(d_hidden, fc1_all))
    d_middle = grad_in.astype(jnp.float32) + d_mid_part
    d_attn_f, grad_gain_attn = norm_attn_back(d_middle)
    d_attn_out = d_attn_f.astype(jnp.bfloat16)

    scale_here = arrival(scale_cols.reshape(line_size, part))
    d_scaled = times_transpose(d_attn_out, wout_here)
    second_x, second_y = add_across(*second[:3])
    d_attention = (d_scaled * scale_here).astype(jnp.bfloat16)
    pieces = [(here, d_attention[:, :part])]
    for steps in range(1, line_size):
        piece = d_attention[:, steps * part : (steps + 1) * part]
        pieces.append((lax.rem(here + steps, line_size), turn(piece, line_size - steps)))
    grad_row = place(pieces).reshape(row_len, part)

    out_grad = blocks_of(column_product(scaled, d_attn_out))
    per_part = lax.axis_size("dp") // line_size

    def out_block(index):
        owner = lax.div(index, per_part)
        steps = lax.rem(here - owner + line_size, line_size)
        return out_grad(steps * per_part + lax.rem(index, per_part))

    second_x, second_y = all_after([second_x, second_y], d_attention)
    second_line = add_planes(second_x, second_y, second[3])
    d_projected, diagonal_sums_here, deltas = attend_back(qkv, probs, attention, grad_row, heads, head_size)
    d_normed = times_transpose(d_projected, wqkv_part)
    d_normed_low = lax.psum_scatter(
        d_normed.astype(jnp.bfloat16), "blk", scatter_dimension=0, tiled=True
    )
    d_normed_here = d_normed_low.astype(jnp.float32)

    qkv_grad = blocks_of(column_product(normed_row, d_projected))

    def small_block(index):
        return jnp.concatenate([out_block(index), qkv_grad(index)], axis=1)

    fourth = add_cores(small_block)
    first = [jnp.concatenate(pair, axis=1) for pair in zip(third, fourth)]
    first[0] = after(first[0], second_line)
    first_x, first_y = add_across(*first[:3])
    grad_fc2 = add_line(after(second_line, d_projected))
    first_x, first_y = all_after([first_x, first_y], d_normed_low)
    first_line = add_planes(first_x, first_y, first[3])
    dealt = deal_line(first_line.reshape((line_size, shard_rows) + first_line.shape[1:]))
    first_grad = sum_parts([piece[:, :summed] for piece in dealt])
    grad_fc1, grad_out = first_grad[:, :hidden_width], first_grad[:, hidden_width:]
    grad_qkv = in_line([piece[:, summed:].astype(jnp.float32) for piece in dealt])
    grad_qkv = grad_qkv.reshape(line_size, shard_rows, 3, part).transpose(1, 2, 0, 3)
    grad_qkv = grad_qkv.reshape(shard_rows, 3 * width)

    _, gain_in_back = jax.vjp(lambda gain: layer_norm(row_in, gain), gain_in)
    (grad_gain_in,) = gain_in_back(d_normed)
    _, norm_in_back = jax.vjp(lambda value: layer_norm(value, gain_in), residual_in)
    (d_input_part,) = norm_in_back(d_normed_here)
    grad_tokens = (d_middle + d_input_part).astype(jnp.bfloat16)[None]

    d_table = lax.dot_general(
        diagonal_sums_here, selector, (((1,), (1,)), ((), ())), precision=highest
    )
    d_bias = lax.dynamic_update_slice_in_dim(
        jnp.zeros((all_heads, bucket_count), jnp.float32), d_table, here * heads, 0
    )
    scale_part = jnp.sum(deltas, axis=0)
    grad_scale = lax.dynamic_update_slice_in_dim(
        jnp.zeros((all_heads,), jnp.float32), scale_part, here * heads, 0
    )
    small = (grad_gain_in, grad_gain_attn, grad_gain_ffn_in, grad_gain_hidden, grad_scale, d_bias)
    sizes = [math.prod(value.shape) for value in small]
    flat = jnp.concatenate([value.reshape(-1) for value in small])
    flat = jnp.pad(flat, (0, -flat.shape[0] % 1024)).reshape(-1, lanes)
    flat = after(flat, grad_fc2, first_x, first_y)
    flat = sum_everywhere(flat).reshape(-1)
    sums, begin = [], 0
    for value, size in zip(small, sizes):
        sums.append(flat[begin : begin + size].reshape(value.shape))
        begin += size
    return (
        mixed[None],
        grad_tokens,
        grad_qkv,
        grad_out,
        grad_fc1,
        grad_fc2,
        sums[0],
        sums[1],
        sums[2],
        sums[3],
        sums[4] / head_scale,
        sums[5].T,
    )


def on_device(dp_size, line_size, tokens, *rest):
    head_scale, row_len = rest[10], tokens.shape[1] * line_size
    whole_heads = head_scale.shape[0] % line_size == 0 and dp_size % line_size == 0
    if dp_size == 8 and line_size == 4 and whole_heads and row_len % lanes == 0:
        return by_heads(tokens, *rest)
    return by_sequence(tokens, *rest)


def solution(mesh):
    return jax.shard_map(
        functools.partial(on_device, mesh.shape["dp"], mesh.shape["blk"]),
        mesh=mesh,
        in_specs=(
            P("dp", "blk", None),
            P("dp", None),
            P(),
            P(("dp", "blk"), None),
            P(("dp", "blk"), None),
            P(("dp", "blk"), None),
            P(("dp", "blk"), None),
            P(),
            P(),
            P(),
            P(),
            P(),
            P(),
            P("dp", "blk", None),
        ),
        out_specs=(
            P("dp", "blk", None),
            P("dp", "blk", None),
            P(("dp", "blk"), None),
            P(("dp", "blk"), None),
            P(("dp", "blk"), None),
            P(("dp", "blk"), None),
            P(),
            P(),
            P(),
            P(),
            P(),
            P(),
        ),
        check_vma=False,
    )
```

```python
import functools
import math

import jax
import jax.numpy as jnp
from jax import lax
from jax.experimental import pallas as pl
from jax.experimental.pallas import tpu as pltpu
from jax.sharding import PartitionSpec as P

epsilon = 1e-05
masked_score = -1e30
query_scale = 0.125
highest = lax.Precision.HIGHEST


def layer_norm(value, gain):
    center = value - jnp.mean(value, axis=-1, keepdims=True)
    spread = jnp.mean(center * center, axis=-1, keepdims=True)
    return center * lax.rsqrt(spread + epsilon) * gain


def hidden_norm(value, gain):
    return layer_norm(jax.nn.gelu(value, approximate=False), gain)


def column_product(left, right):
    return lax.dot_general(
        left, right, (((0,), (0,)), ((), ())), preferred_element_type=jnp.float32
    )


def times_transpose(left, matrix):
    return lax.dot_general(
        left, matrix, (((1,), (1,)), ((), ())), preferred_element_type=jnp.float32
    )


def toeplitz(diagonals, rows, cols):
    heads = diagonals.shape[0]
    padded = jnp.pad(diagonals, ((0, 0), (0, 1)))
    stride = rows + cols - 1
    tiled = jnp.tile(padded, (1, rows))[:, : rows * stride].reshape(heads, rows, stride)
    return tiled[:, :, rows - 1 : rows - 1 + cols]


def diagonal_sums(grid):
    heads, rows, cols = grid.shape
    flipped = grid[:, ::-1, :]
    padded = jnp.pad(flipped, ((0, 0), (0, 0), (0, rows)))
    skewed = padded.reshape(heads, -1)[:, : rows * (rows + cols - 1)].reshape(
        heads, rows, rows + cols - 1
    )
    return jnp.sum(skewed, axis=1)


def by_sequence(
    tokens,
    lengths,
    distance_bucket,
    w_qkv,
    w_out,
    w_fc1,
    w_fc2,
    gain_in,
    gain_attn,
    gain_ffn_in,
    gain_hidden,
    head_scale,
    bias_table,
    cotangent,
):
    rows_here = tokens.shape[1]
    width = tokens.shape[2]
    heads = head_scale.shape[0]
    head_size = width // heads
    reach = distance_bucket.shape[0] // 2
    bucket_count = bias_table.shape[0]
    row_len = rows_here * lax.axis_size("blk")
    key_block = math.gcd(row_len, 512)
    block_count = row_len // key_block
    query_anchor = lax.axis_index("blk") * rows_here
    positions = query_anchor + jnp.arange(rows_here, dtype=jnp.int32)
    ends = jnp.cumsum(lengths[0])
    bucket_ids = jnp.arange(bucket_count, dtype=jnp.int32)

    def document_of(where):
        return jnp.sum((where[:, None] >= ends[None, :]).astype(jnp.int32), axis=1)

    query_docs = document_of(positions)

    def bucket_index(query_start, rows, key_start, cols):
        steps = jnp.arange(rows + cols - 1, dtype=jnp.int32)
        relative = key_start - query_start - (rows - 1) + steps
        return jnp.take(distance_bucket, jnp.clip(relative, -reach, reach) + reach)

    def scores_for(query_heads, query_start, query_doc, key_heads, key_start, key_doc):
        rows = query_heads.shape[0]
        cols = key_heads.shape[0]
        raw = jnp.einsum("qhd,khd->hqk", query_heads, key_heads, preferred_element_type=jnp.float32)
        buckets = bucket_index(query_start, rows, key_start, cols)
        diagonals = jnp.take(bias_table, buckets, axis=0).T
        same = query_doc[:, None] == key_doc[None, :]
        full = raw + toeplitz(diagonals, rows, cols)
        return (jnp.where(same[None], full, masked_score), same, buckets)

    residual_in = tokens[0].astype(jnp.float32)
    wqkv_all, wout_all = (
        lax.all_gather(w_qkv, ("dp", "blk"), axis=0, tiled=True),
        lax.all_gather(w_out, ("dp", "blk"), axis=0, tiled=True),
    )
    normed_f, norm_in_back = jax.vjp(layer_norm, residual_in, gain_in)
    normed_in = normed_f.astype(jnp.bfloat16)
    projected = jnp.dot(normed_in, wqkv_all, preferred_element_type=jnp.float32)
    queries = (projected[:, :width] * query_scale).astype(jnp.bfloat16)
    keys_here = projected[:, width : 2 * width].astype(jnp.bfloat16)
    values_here = projected[:, 2 * width :].astype(jnp.bfloat16)
    query_heads = queries.reshape(rows_here, heads, head_size)
    best = jnp.full((heads, rows_here), masked_score, jnp.float32)
    key_piece = lax.all_gather(keys_here, "blk", axis=0, tiled=True)
    value_piece = lax.all_gather(values_here, "blk", axis=0, tiled=True)
    length = key_piece.shape[0]
    key_pos = jnp.arange(length, dtype=jnp.int32)
    scores, same, buckets = scores_for(
        query_heads,
        query_anchor,
        query_docs,
        key_piece.reshape(length, heads, head_size),
        jnp.int32(0),
        document_of(key_pos),
    )
    new_best = jnp.maximum(best, jnp.max(scores, axis=-1))
    weights = jnp.where(same[None], jnp.exp(scores - new_best[..., None]), 0.0)
    total = jnp.sum(weights, axis=-1)
    accum = jnp.einsum(
        "hqk,khd->hqd",
        weights.astype(jnp.bfloat16),
        value_piece.reshape(length, heads, head_size),
        preferred_element_type=jnp.float32,
    )
    best, total, accum = (new_best, total, accum)
    log_total = best + jnp.log(total)
    attention = jnp.transpose(accum / total[..., None], (1, 0, 2)).reshape(rows_here, width)
    scale_cols = jnp.repeat(head_scale, head_size)
    scaled = (attention * scale_cols).astype(jnp.bfloat16)
    attn_out = jnp.dot(scaled, wout_all, preferred_element_type=jnp.float32)
    normed_attn, norm_attn_back = jax.vjp(layer_norm, attn_out, gain_attn)
    middle = residual_in + normed_attn
    fc1_all, fc2_all = (
        lax.all_gather(w_fc1, ("dp", "blk"), axis=0, tiled=True),
        lax.all_gather(w_fc2, ("dp", "blk"), axis=0, tiled=True),
    )
    normed_mid_f, norm_mid_back = jax.vjp(layer_norm, middle, gain_ffn_in)
    normed_mid = normed_mid_f.astype(jnp.bfloat16)
    hidden = jnp.dot(normed_mid, fc1_all, preferred_element_type=jnp.float32)
    activated_f, hidden_back = jax.vjp(hidden_norm, hidden, gain_hidden)
    activated = activated_f.astype(jnp.bfloat16)
    mixed = (middle + jnp.dot(activated, fc2_all, preferred_element_type=jnp.float32)).astype(
        jnp.bfloat16
    )
    grad_in = cotangent[0]
    fc1_back, fc2_back = (
        lax.all_gather(w_fc1, ("dp", "blk"), axis=0, tiled=True),
        lax.all_gather(w_fc2, ("dp", "blk"), axis=0, tiled=True),
    )
    grad_fc2 = lax.psum_scatter(
        column_product(activated, grad_in), ("dp", "blk"), scatter_dimension=0, tiled=True
    )
    d_activated = times_transpose(grad_in, fc2_back)
    d_hidden_f, grad_gain_hidden = hidden_back(d_activated)
    d_hidden = d_hidden_f.astype(jnp.bfloat16)
    grad_fc1 = lax.psum_scatter(
        column_product(normed_mid, d_hidden), ("dp", "blk"), scatter_dimension=0, tiled=True
    )
    d_mid_part, grad_gain_ffn_in = norm_mid_back(times_transpose(d_hidden, fc1_back))
    d_middle = grad_in.astype(jnp.float32) + d_mid_part
    d_attn_f, grad_gain_attn = norm_attn_back(d_middle)
    d_attn_out = d_attn_f.astype(jnp.bfloat16)
    qkv_back, out_back = (
        lax.all_gather(w_qkv, ("dp", "blk"), axis=0, tiled=True),
        lax.all_gather(w_out, ("dp", "blk"), axis=0, tiled=True),
    )
    grad_out = lax.psum_scatter(
        column_product(scaled, d_attn_out), ("dp", "blk"), scatter_dimension=0, tiled=True
    )
    d_scaled = times_transpose(d_attn_out, out_back)
    grad_scale = jnp.sum((d_scaled * attention).reshape(rows_here, heads, head_size), axis=(0, 2))
    d_attention = (d_scaled * scale_cols).astype(jnp.bfloat16)
    grad_heads = d_attention.reshape(rows_here, heads, head_size)
    row_delta = jnp.sum(
        (d_attention.astype(jnp.float32) * attention).reshape(rows_here, heads, head_size), axis=2
    ).T
    keys_back, values_back = (
        lax.all_gather(keys_here, "blk", axis=0, tiled=True),
        lax.all_gather(values_here, "blk", axis=0, tiled=True),
    )

    def pair_grads(
        query_part,
        grad_part,
        total_part,
        delta_part,
        query_start,
        query_doc,
        key_part,
        value_part,
        key_start,
        key_doc,
    ):
        scores, same, buckets = scores_for(
            query_part, query_start, query_doc, key_part, key_start, key_doc
        )
        probs = jnp.where(same[None], jnp.exp(scores - total_part[..., None]), 0.0)
        d_probs = jnp.einsum(
            "qhd,khd->hqk", grad_part, value_part, preferred_element_type=jnp.float32
        )
        d_scores = probs * (d_probs - delta_part[..., None])
        return (probs.astype(jnp.bfloat16), d_scores, buckets)

    def bias_sum(d_scores, buckets):
        sums = diagonal_sums(d_scores)
        selector = (buckets[:, None] == bucket_ids[None, :]).astype(jnp.float32)
        return jnp.dot(sums, selector, precision=highest).T

    def key_slices(index):
        begin = index * key_block
        key_part = lax.dynamic_slice_in_dim(keys_back, begin, key_block, 0).reshape(
            key_block, heads, head_size
        )
        value_part = lax.dynamic_slice_in_dim(values_back, begin, key_block, 0).reshape(
            key_block, heads, head_size
        )
        return (key_part, value_part, begin)

    query_carry = (
        jnp.zeros((rows_here, heads, head_size), jnp.float32),
        jnp.zeros((bucket_count, heads), jnp.float32),
    )

    def key_step(carry, index):
        d_query, d_bias = carry
        key_part, value_part, begin = key_slices(index)
        key_doc = document_of(begin + jnp.arange(key_block, dtype=jnp.int32))
        probs_low, d_scores, buckets = pair_grads(
            query_heads,
            grad_heads,
            log_total,
            row_delta,
            query_anchor,
            query_docs,
            key_part,
            value_part,
            begin,
            key_doc,
        )
        scores_low = d_scores.astype(jnp.bfloat16)
        d_query = d_query + jnp.einsum(
            "hqk,khd->qhd", scores_low, key_part, preferred_element_type=jnp.float32
        )
        d_key = jnp.einsum(
            "hqk,qhd->khd", scores_low, query_heads, preferred_element_type=jnp.float32
        ).reshape(key_block, width)
        d_value = jnp.einsum(
            "hqk,qhd->khd", probs_low, grad_heads, preferred_element_type=jnp.float32
        ).reshape(key_block, width)
        return (
            (d_query, d_bias + bias_sum(d_scores, buckets)),
            jnp.concatenate([d_key, d_value], axis=1),
        )

    (d_query, d_bias), kv_terms = lax.scan(
        key_step, query_carry, jnp.arange(block_count, dtype=jnp.int32)
    )
    kv_grad = lax.psum_scatter(
        kv_terms.reshape(row_len, 2 * width).astype(jnp.bfloat16),
        "blk",
        scatter_dimension=0,
        tiled=True,
    )
    d_query_low = d_query.reshape(rows_here, width).astype(jnp.bfloat16)
    d_projected = jnp.concatenate(
        [d_query_low * jnp.asarray(query_scale, jnp.bfloat16), kv_grad], axis=1
    )
    grad_qkv = lax.psum_scatter(
        column_product(normed_in, d_projected), ("dp", "blk"), scatter_dimension=0, tiled=True
    )
    d_input_part, grad_gain_in = norm_in_back(times_transpose(d_projected, qkv_back))
    grad_tokens = (d_middle + d_input_part).astype(jnp.bfloat16)[None]
    small = lax.psum(
        (grad_gain_in, grad_gain_attn, grad_gain_ffn_in, grad_gain_hidden, grad_scale, d_bias),
        ("dp", "blk"),
    )
    return (
        mixed[None],
        grad_tokens,
        grad_qkv,
        grad_out,
        grad_fc1,
        grad_fc2,
        small[0],
        small[1],
        small[2],
        small[3],
        small[4],
        small[5],
    )


lanes = 128
core_bit, x_bit, y_bit = 1, 2, 4


def swap(value, bit):
    size = lax.axis_size("dp")
    return lax.ppermute(value, "dp", [(i, i ^ bit) for i in range(size)])


def turn(value, steps):
    size = lax.axis_size("blk")
    return lax.ppermute(value, "blk", [(i, (i + steps) % size) for i in range(size)])


def swap_line(value, bit):
    size = lax.axis_size("blk")
    return lax.ppermute(value, "blk", [(i, i ^ bit) for i in range(size)])


def pick(stack, index):
    return lax.dynamic_index_in_dim(stack, index, 0, keepdims=False)


def after(value, *others):
    return lax.optimization_barrier((value, *others))[0]


def all_after(values, *others):
    return list(lax.optimization_barrier((*values, *others))[: len(values)])


def turns(value):
    size = lax.axis_size("blk")
    return [value] + [turn(value, steps) for steps in range(1, size)]


def in_line(pieces):
    here, size = lax.axis_index("blk"), lax.axis_size("blk")
    ordered = [lax.select_n(lax.rem(here - owner + size, size), *pieces) for owner in range(size)]
    return jnp.concatenate(ordered, axis=0)


def deal_line(stack):
    here, size = lax.axis_index("blk"), lax.axis_size("blk")
    got = [pick(stack, here)]
    for steps in range(1, size):
        got.append(turn(pick(stack, lax.rem(here + steps, size)), steps))
    return got


def swap_cores(blocks):
    return [swap(block, core_bit) for block in blocks]


def beside(line):
    return [line, swap(line, x_bit), swap(line, y_bit)]


def across_halves(near):
    _, along_x, along_y = near
    half = along_x.shape[0] // 2
    return [swap(along_y[:half], x_bit), swap(along_x[half:], y_bit)]


def across_plane(near):
    return near + [jnp.concatenate(across_halves(near), axis=0)]


def add_low(left, right):
    return (left.astype(jnp.float32) + right.astype(jnp.float32)).astype(jnp.bfloat16)


def halves_across(across):
    half = across.shape[0] // 2
    return [swap(across[:half], x_bit), swap(across[half:], y_bit)]


def add_across(halves, to_x, to_y):
    from_x, from_y = halves
    half = from_x.shape[0]
    to_y = jnp.concatenate([add_low(to_y[:half], from_x), to_y[half:]], axis=0)
    to_x = jnp.concatenate([to_x[:half], add_low(to_x[half:], from_y)], axis=0)
    return to_x, to_y


def add_planes(to_x, to_y, own):
    got_x, got_y = swap(to_x, x_bit), swap(to_y, y_bit)
    total = own.astype(jnp.float32) + got_x.astype(jnp.float32) + got_y.astype(jnp.float32)
    return total.astype(jnp.bfloat16)


def sum_parts(parts):
    total = parts[0].astype(jnp.float32)
    for part in parts[1:]:
        total = total + part.astype(jnp.float32)
    return total


def add_line(line):
    size = lax.axis_size("blk")
    return sum_parts(deal_line(line.reshape((size, -1) + line.shape[1:])))


def contract(left, right, left_axis, right_axis):
    return lax.dot_general(
        left, right, (((left_axis,), (right_axis,)), ((), ())), preferred_element_type=jnp.float32
    )


tile_cols = 512
far_first = (x_bit | y_bit, x_bit, y_bit, 0)


def run_kernel(kernel, name, micros, place_here, operands, far, outputs, far_outputs, scratch=(), copies=1):
    near_spec, far_spec = pl.BlockSpec(memory_space=pltpu.VMEM), pl.BlockSpec(memory_space=pl.ANY)
    return pl.pallas_call(
        kernel,
        out_shape=[jax.ShapeDtypeStruct(shape, dtype) for shape, dtype in (*outputs, *far_outputs)],
        in_specs=[pl.BlockSpec(memory_space=pltpu.SMEM)] + [near_spec] * len(operands) + [far_spec] * len(far),
        out_specs=[near_spec] * len(outputs) + [far_spec] * len(far_outputs),
        scratch_shapes=[pltpu.VMEM(shape, dtype) for shape, dtype in scratch]
        + [pltpu.SemaphoreType.DMA((copies,))],
        compiler_params=pltpu.CompilerParams(vmem_limit_bytes=52 * 2**20),
        cost_estimate=pl.CostEstimate(
            flops=int(micros * 1.1e9), bytes_accessed=int(micros * 3.6e6), transcendentals=0
        ),
        name=name,
    )(place_here, *operands, *far)


class Copies:
    def __init__(self, semaphores):
        self.semaphores, self.used = semaphores, 0

    def start(self, source, target):
        copy = pltpu.make_async_copy(source, target, self.semaphores.at[self.used])
        self.used += 1
        copy.start()
        return copy


def wait_all(copies):
    for copy in copies:
        copy.wait()


def normalize(value):
    center = value - jnp.mean(value, axis=-1, keepdims=True)
    spread = jnp.mean(center * center, axis=-1, keepdims=True)
    scale = lax.rsqrt(spread + epsilon)
    return center * scale, scale


def normalize_back(normed, scale, grad, gain):
    inner = grad * gain
    middle = jnp.mean(inner, axis=-1, keepdims=True)
    along = jnp.mean(inner * normed, axis=-1, keepdims=True)
    return scale * (inner - middle - normed * along), jnp.sum(grad * normed, axis=0, keepdims=True)


def block_indices(place_ref):
    me = place_ref[0]
    return [me ^ bits ^ core_bit for bits in far_first], [me ^ bits for bits in far_first]


near_first = (0, x_bit, y_bit, x_bit | y_bit)


def fill_planes(copies, place_ref, blocks, cols, out_ref):
    bits = near_first + tuple(bit | core_bit for bit in near_first)
    started = []
    for bit, block in zip(bits, blocks):
        rows = block.shape[0]
        begin = pl.multiple_of((place_ref[0] ^ bit) * rows, rows)
        started.append(copies.start(block.at[:, cols], out_ref.at[pl.ds(begin, rows), :]))
    return started


def before(place_ref, steps, size):
    return lax.rem(place_ref[1] - steps + size, size)


def attend_kernel(
    heads, head_size, place_ref, gain_ref, diagonal_ref, doc_col_ref, doc_row_ref, scale_ref, tokens_ref, *refs
):
    parts, refs = refs[:8], refs[8:]
    w_ref, qkv_ref, normed_ref, attention_ref, scaled_ref, probs_out, bias, probs_ref, semaphores = refs
    copies = Copies(semaphores)
    last = parts[0].shape[1]
    arriving = fill_planes(copies, place_ref, parts, slice(last - w_ref.shape[1], last), w_ref)
    leaving = []
    length = tokens_ref.shape[0]
    blocks = length // lanes
    width = heads * head_size
    for block in range(blocks):
        rows = slice(block * lanes, (block + 1) * lanes)
        normed, _ = normalize(tokens_ref[rows, :].astype(jnp.float32))
        normed_ref[rows, :] = (normed * gain_ref[...]).astype(jnp.bfloat16)
    wait_all(arriving)
    projected = contract(normed_ref[...], w_ref[...], 1, 0)
    qkv_ref[:, :width] = (projected[:, :width] * query_scale).astype(jnp.bfloat16)
    qkv_ref[:, width:] = projected[:, width:].astype(jnp.bfloat16)
    for head in range(heads):
        for step in range(2 * blocks - 1):
            window = diagonal_ref[head : head + 1, step * lanes : (step + 2) * lanes]
            window = jnp.broadcast_to(window, (lanes, 2 * lanes))
            window = pltpu.roll(window, 0, 1, stride=1, stride_axis=0)
            bias[:, step * lanes : (step + 1) * lanes] = window[:, lanes:]
        low = head * head_size
        keys = qkv_ref[:, width + low : width + low + head_size]
        values = qkv_ref[:, 2 * width + low : 2 * width + low + head_size]
        all_scores = contract(qkv_ref[:, low : low + head_size], keys, 1, 1)
        for block in range(blocks):
            rows = slice(block * lanes, (block + 1) * lanes)
            first = (blocks - 1 - block) * lanes
            scores = all_scores[rows, :] + bias[:, first : first + length]
            same = doc_col_ref[rows, :] == doc_row_ref[...]
            scores = jnp.where(same, scores, masked_score)
            weights = jnp.exp(scores - jnp.max(scores, axis=1, keepdims=True))
            probs = weights * (1.0 / jnp.sum(weights, axis=1, keepdims=True))
            probs = probs.astype(jnp.bfloat16)
            probs_ref[head, rows, :] = probs
        leaving.append(copies.start(probs_ref.at[head], probs_out.at[head]))
        attention_ref[:, low : low + head_size] = contract(probs_ref[head], values, 1, 0)
    scaled_ref[...] = (attention_ref[...] * scale_ref[...]).astype(jnp.bfloat16)
    wait_all(leaving)


def forward_kernel(line, place_ref, *refs):
    pieces, refs = refs[:line], refs[line:]
    tokens_ref, gain_attn_ref, gain_mid_ref, gain_hidden_ref, cotangent_ref, *refs = refs
    blocks, refs = refs[:8], refs[8:]
    (attn_ref, middle_ref, normed_ref, mean_ref, scale_ref, activated_ref,
     hidden_out, below_out, across_out, send_out, keep_out,
     wout_ref, fc1_ref, hidden_ref, below_ref, grads_ref, semaphores) = refs
    copies = Copies(semaphores)
    part = pieces[0].shape[1]
    hidden_width, width = fc1_ref.shape[1], wout_ref.shape[1]
    wout_here = fill_planes(copies, place_ref, blocks, slice(hidden_width, hidden_width + width), wout_ref)
    fc1_here = fill_planes(copies, place_ref, blocks, slice(0, hidden_width), fc1_ref)
    leaving = []
    wait_all(wout_here)
    attn = jnp.zeros(attn_ref.shape, jnp.float32)
    for steps in range(line):
        rows = pl.ds(pl.multiple_of(before(place_ref, steps, line) * part, part), part)
        attn = attn + contract(pieces[steps][...], wout_ref[rows, :], 1, 0)
    attn_ref[...] = attn
    normed, _ = normalize(attn)
    middle = tokens_ref[...].astype(jnp.float32) + normed * gain_attn_ref[...]
    middle_ref[...] = middle
    normed, _ = normalize(middle)
    normed = (normed * gain_mid_ref[...]).astype(jnp.bfloat16)
    normed_ref[...] = normed
    tiles = [slice(begin, begin + tile_cols) for begin in range(0, hidden_width, tile_cols)]
    total = jnp.zeros(mean_ref.shape, jnp.float32)
    wait_all(fc1_here)
    for cols in tiles:
        hidden = contract(normed, fc1_ref[:, cols], 1, 0)
        below = 0.5 * (1.0 + lax.erf(hidden * (0.5**0.5)))
        hidden_ref[:, cols] = hidden
        below_ref[:, cols] = below
        leaving.append(copies.start(hidden_ref.at[:, cols], hidden_out.at[:, cols]))
        leaving.append(copies.start(below_ref.at[:, cols], below_out.at[:, cols]))
        total = total + jnp.sum(hidden * below, axis=1, keepdims=True)
    mean = total / hidden_width
    total = jnp.zeros(mean_ref.shape, jnp.float32)
    for cols in tiles:
        center = hidden_ref[:, cols] * below_ref[:, cols] - mean
        total = total + jnp.sum(center * center, axis=1, keepdims=True)
    scale = lax.rsqrt(total / hidden_width + epsilon)
    mean_ref[...] = mean
    scale_ref[...] = scale
    for cols in tiles:
        center = hidden_ref[:, cols] * below_ref[:, cols] - mean
        activated_ref[:, cols] = (center * scale * gain_hidden_ref[:, cols]).astype(jnp.bfloat16)
    size = grads_ref.shape[1]
    sent, kept = block_indices(place_ref)
    outs = [across_out] + [send_out.at[slot] for slot in range(3)] + [keep_out.at[slot] for slot in range(4)]
    for slot, (index, out) in enumerate(zip(sent + kept, outs)):
        cols = pl.ds(pl.multiple_of(index * size, lanes), size)
        grads_ref[slot] = contract(activated_ref[:, cols], cotangent_ref[...], 0, 0).astype(jnp.bfloat16)
        leaving.append(copies.start(grads_ref.at[slot], out))
    wait_all(leaving)


def backward_kernel(line, place_ref, *refs):
    pieces, refs = refs[:line], refs[line:]
    (cotangent_ref, attn_ref, middle_ref, normed_ref, mean_ref, scale_ref, gain_attn_ref, gain_mid_ref,
     gain_hidden_ref, head_scale_ref, *refs) = refs
    first_blocks, second_blocks, refs = refs[:8], refs[8:16], refs[16:]
    hidden_in, below_in, activated_in, *refs = refs
    mixed_ref, d_middle_ref, d_hidden_gain_ref, d_mid_gain_ref, d_attn_gain_ref, *refs = refs
    grads, refs = refs[:line], refs[line:]
    (send_out, keep_out, wout_ref, fc1_ref, fc2_ref, hidden_ref, below_ref, activated_ref, inner_ref, fc1_grad,
     out_grad, semaphores) = refs
    copies = Copies(semaphores)
    part = pieces[0].shape[1]
    hidden_width, width = fc1_ref.shape[1], wout_ref.shape[1]
    hidden_here = [copies.start(hidden_in, hidden_ref), copies.start(below_in, below_ref)]
    fc2_here = fill_planes(copies, place_ref, second_blocks, slice(0, width), fc2_ref)
    fc1_here = fill_planes(copies, place_ref, first_blocks, slice(0, hidden_width), fc1_ref)
    activated_here = copies.start(activated_in, activated_ref)
    wout_here = fill_planes(
        copies, place_ref, first_blocks, slice(hidden_width, hidden_width + width), wout_ref
    )
    grad_in = cotangent_ref[...]
    mean, scale = mean_ref[...], scale_ref[...]
    tiles = [slice(begin, begin + tile_cols) for begin in range(0, hidden_width, tile_cols)]
    wait_all(hidden_here + fc2_here)
    total = jnp.zeros(mean.shape, jnp.float32)
    along = jnp.zeros(mean.shape, jnp.float32)
    for cols in tiles:
        d_activated = contract(grad_in, fc2_ref[cols, :], 1, 1)
        normed = (hidden_ref[:, cols] * below_ref[:, cols] - mean) * scale
        d_hidden_gain_ref[:, cols] = jnp.sum(d_activated * normed, axis=0, keepdims=True)
        inner = d_activated * gain_hidden_ref[:, cols]
        inner_ref[:, cols] = inner
        total = total + jnp.sum(inner, axis=1, keepdims=True)
        along = along + jnp.sum(inner * normed, axis=1, keepdims=True)
    total, along = total / hidden_width, along / hidden_width
    d_normed = jnp.zeros(middle_ref.shape, jnp.float32)
    normed_mid = normed_ref[...].T
    wait_all(fc1_here)
    for cols in tiles:
        hidden, below = hidden_ref[:, cols], below_ref[:, cols]
        normed = (hidden * below - mean) * scale
        slope = below + hidden * jnp.exp(-0.5 * hidden * hidden) * (1.0 / math.sqrt(2.0 * math.pi))
        d_hidden = scale * (inner_ref[:, cols] - total - normed * along) * slope
        d_hidden = d_hidden.astype(jnp.bfloat16)
        fc1_grad[:, cols] = contract(normed_mid, d_hidden, 1, 0).astype(jnp.bfloat16)
        d_normed = d_normed + contract(d_hidden, fc1_ref[:, cols], 1, 1)
    size = send_out.shape[1]
    sent, kept = block_indices(place_ref)
    outs = [send_out.at[slot] for slot in range(4)] + [keep_out.at[slot] for slot in range(4)]
    places = [pl.ds(pl.multiple_of(index * size, size), size) for index in sent + kept]
    leaving = [
        copies.start(fc1_grad.at[rows, :], out.at[:, :hidden_width]) for rows, out in zip(places, outs)
    ]
    normed, scale = normalize(middle_ref[...])
    d_value, d_mid_gain_ref[...] = normalize_back(normed, scale, d_normed, gain_mid_ref[...])
    d_middle = grad_in.astype(jnp.float32) + d_value
    d_middle_ref[...] = d_middle
    normed, scale = normalize(attn_ref[...])
    d_value, d_attn_gain_ref[...] = normalize_back(normed, scale, d_middle, gain_attn_ref[...])
    d_attn = d_value.astype(jnp.bfloat16)
    wait_all(wout_here)
    for steps in range(line):
        owner = before(place_ref, steps, line)
        rows = pl.ds(pl.multiple_of(owner * part, part), part)
        d_scaled = contract(d_attn, wout_ref[rows, :], 1, 1)
        grads[steps][...] = (d_scaled * head_scale_ref[pl.ds(owner, 1), :]).astype(jnp.bfloat16)
        out_grad[rows, :] = contract(pieces[steps][...], d_attn, 0, 0).astype(jnp.bfloat16)
    leaving += [
        copies.start(out_grad.at[rows, :], out.at[:, hidden_width:]) for rows, out in zip(places, outs)
    ]
    activated_here.wait()
    mixed = middle_ref[...] + contract(activated_ref[...], fc2_ref[...], 1, 0)
    mixed_ref[...] = mixed.astype(jnp.bfloat16)
    wait_all(leaving)


def attend_back_kernel(heads, head_size, line, place_ref, *refs):
    pieces, refs = refs[:line], refs[line:]
    (qkv_ref, attention_ref, probs_in, normed_in, w_in,
     send_ref, keep_ref, diagonal_ref, delta_ref, gain_ref, d_normed_out,
     grad_ref, out_ref, w_grad, sums, probs_ref, normed_ref, w_ref, d_normed_ref, semaphores) = refs
    copies = Copies(semaphores)
    probs_here = [copies.start(probs_in.at[head], probs_ref.at[head]) for head in range(heads)]
    rest_here = [copies.start(w_in, w_ref), copies.start(normed_in, normed_ref)]
    length = qkv_ref.shape[0]
    blocks = length // lanes
    width = heads * head_size
    rows_here = pieces[0].shape[0]
    for steps in range(line):
        owner = lax.rem(place_ref[1] + steps, line)
        grad_ref[pl.ds(pl.multiple_of(owner * rows_here, rows_here), rows_here), :] = pieces[steps][...]
    diagonal_ref[...] = jnp.zeros_like(diagonal_ref)
    for head in range(heads):
        sums[...] = jnp.zeros_like(sums)
        probs_here[head].wait()
        low = head * head_size
        keys = qkv_ref[:, width + low : width + low + head_size]
        values = qkv_ref[:, 2 * width + low : 2 * width + low + head_size]
        d_keys = jnp.zeros((head_size, length), jnp.float32)
        d_values = jnp.zeros((head_size, length), jnp.float32)
        for block in range(blocks):
            rows = slice(block * lanes, (block + 1) * lanes)
            first = (blocks - 1 - block) * lanes
            queries = qkv_ref[rows, low : low + head_size]
            grad = grad_ref[rows, low : low + head_size]
            probs = probs_ref[head, rows, :]
            product = grad.astype(jnp.float32) * attention_ref[rows, low : low + head_size]
            delta = jnp.sum(product, axis=1, keepdims=True)
            delta_ref[rows, head : head + 1] = delta
            d_scores = probs.astype(jnp.float32) * (contract(grad, values, 1, 1) - delta)
            sums[:, first : first + length] += d_scores
            d_scores = d_scores.astype(jnp.bfloat16)
            d_query = contract(d_scores, keys, 1, 0).astype(jnp.bfloat16)
            out_ref[rows, low : low + head_size] = d_query * jnp.asarray(query_scale, jnp.bfloat16)
            d_keys = d_keys + contract(queries, d_scores, 0, 0)
            d_values = d_values + contract(grad, probs, 0, 0)
        out_ref[:, width + low : width + low + head_size] = d_keys.T.astype(jnp.bfloat16)
        out_ref[:, 2 * width + low : 2 * width + low + head_size] = d_values.T.astype(jnp.bfloat16)
        row_ids = lax.broadcasted_iota(jnp.int32, (lanes, lanes), 0)
        col_ids = lax.broadcasted_iota(jnp.int32, (lanes, lanes), 1)
        reverse = (row_ids + col_ids == lanes - 1).astype(jnp.float32)
        flipped = jnp.dot(reverse, sums[...], precision=highest)
        for step in range(2 * blocks - 1):
            window = flipped[:, step * lanes : (step + 1) * lanes]
            window = jnp.concatenate([window, jnp.zeros_like(window)], axis=1)
            window = pltpu.roll(window, 1, 1, stride=1, stride_axis=0)
            diagonal_ref[head : head + 1, step * lanes : (step + 2) * lanes] += jnp.sum(
                window, axis=0, keepdims=True
            )
    wait_all(rest_here)
    d_normed_ref[...] = contract(out_ref[...], w_ref[...], 1, 1).astype(jnp.bfloat16)
    leaving = copies.start(d_normed_ref, d_normed_out)
    for block in range(normed_ref.shape[1] // lanes):
        cols = slice(block * lanes, (block + 1) * lanes)
        grad = contract(normed_ref[:, cols], out_ref[...], 0, 0)
        gain_ref[cols, :] = jnp.sum(grad * w_ref[cols, :].astype(jnp.float32), axis=1, keepdims=True)
        w_grad[cols, :] = grad.astype(jnp.bfloat16)
    size = send_ref.shape[1]
    for indices, to_ref in zip(block_indices(place_ref), (send_ref, keep_ref)):
        for slot, index in enumerate(indices):
            to_ref[slot] = w_grad[pl.ds(pl.multiple_of(index * size, size), size), :]
    leaving.wait()


def by_heads(
    tokens,
    lengths,
    distance_bucket,
    w_qkv,
    w_out,
    w_fc1,
    w_fc2,
    gain_in,
    gain_attn,
    gain_ffn_in,
    gain_hidden,
    head_scale,
    bias_table,
    cotangent,
):
    here, line_size = lax.axis_index("blk"), lax.axis_size("blk")
    rows_here, width = tokens.shape[1], tokens.shape[2]
    row_len = rows_here * line_size
    all_heads = head_scale.shape[0]
    head_size = width // all_heads
    heads = all_heads // line_size
    part = heads * head_size
    reach = distance_bucket.shape[0] // 2
    bucket_count = bias_table.shape[0]
    shard_rows = w_qkv.shape[0]

    hidden_width = w_fc1.shape[1]
    summed = hidden_width + width
    by_head = w_qkv.reshape(shard_rows, 3, line_size, part).transpose(2, 0, 1, 3)
    by_head = by_head.reshape(line_size, shard_rows, 3 * part)
    shared = jnp.broadcast_to(
        jnp.concatenate([w_fc1, w_out], axis=1)[None], (line_size, shard_rows, summed)
    )
    first_pieces = deal_line(jnp.concatenate([shared, by_head], axis=2))
    first_line = in_line(first_pieces)
    row_tokens = lax.all_gather(after(tokens[0], first_line), "blk", axis=0, tiled=True)
    second_pieces = turns(after(w_fc2, first_line))
    first_planes = across_plane(all_after(beside(first_line), *second_pieces[1:]))
    first_others = swap_cores(first_planes[:3] + [after(first_planes[3], row_tokens)])
    second_near = beside(after(in_line(second_pieces), *first_planes))

    ends = jnp.cumsum(lengths[0])
    positions = jnp.arange(row_len, dtype=jnp.int32)
    documents = jnp.sum((positions[:, None] >= ends[None, :]).astype(jnp.int32), axis=1)
    if row_len <= reach:
        buckets = distance_bucket[reach - row_len : reach + row_len]
    else:
        buckets = jnp.pad(distance_bucket, row_len - reach, mode="edge")[: 2 * row_len]
    selector = (buckets[None, :] == jnp.arange(bucket_count, dtype=jnp.int32)[:, None]).astype(jnp.float32)
    head_table = lax.dynamic_slice_in_dim(bias_table.T, here * heads, heads, 0)
    diagonals = jnp.dot(head_table, selector, precision=highest)
    scale_cols = jnp.repeat(head_scale, head_size)
    head_cols = lax.dynamic_slice_in_dim(scale_cols, here * part, part, 0)[None, :]

    low, wide = jnp.bfloat16, jnp.float32
    planes = lax.axis_size("dp")
    place_here = jnp.stack([lax.axis_index("dp"), here]).astype(jnp.int32)
    wqkv_part, qkv, normed_row, attention, scaled_part, probs = run_kernel(
        functools.partial(attend_kernel, heads, head_size),
        "attend",
        13,
        place_here,
        (gain_in[None], diagonals, documents[:, None], documents[None, :], head_cols, row_tokens),
        (*first_planes, *first_others),
        [
            ((width, 3 * part), low),
            ((row_len, 3 * part), low),
            ((row_len, width), low),
            ((row_len, part), wide),
            ((row_len, part), low),
        ],
        [((heads, row_len, row_len), low)],
        [((lanes, 2 * row_len - lanes), wide), ((heads, row_len, row_len), low)],
        8 + heads,
    )

    dealt = deal_line(scaled_part.reshape(line_size, rows_here, part))
    second_halves = across_halves(all_after(second_near, scaled_part))
    dealt[0] = after(dealt[0], *second_halves)
    second_planes = second_near + [jnp.concatenate(second_halves, axis=0)]
    second_others = swap_cores(all_after(second_planes, *dealt[1:]))
    grad_in = cotangent[0]
    gains = (gain_attn[None], gain_ffn_in[None], gain_hidden[None])
    block_rows, hidden_rows = width // planes, hidden_width // planes
    *kept, activated, hidden, below, across_fc2, send_fc2, keep_fc2 = run_kernel(
        functools.partial(forward_kernel, line_size),
        "feed_forward",
        9,
        place_here,
        (*dealt, tokens[0], *gains, grad_in),
        (*first_planes, *first_others),
        [
            ((rows_here, width), wide),
            ((rows_here, width), wide),
            ((rows_here, width), low),
            ((rows_here, 1), wide),
            ((rows_here, 1), wide),
            ((rows_here, hidden_width), low),
        ],
        [
            ((rows_here, hidden_width), wide),
            ((rows_here, hidden_width), wide),
            ((hidden_rows, width), low),
            ((3, hidden_rows, width), low),
            ((4, hidden_rows, width), low),
        ],
        [
            ((width, width), low),
            ((width, hidden_width), low),
            ((rows_here, hidden_width), wide),
            ((rows_here, hidden_width), wide),
            ((8, hidden_rows, width), low),
        ],
        24 + 2 * (hidden_width // tile_cols),
    )
    across_fc2, send_fc2 = all_after([across_fc2, send_fc2], *second_others)
    second_across = add_low(keep_fc2[0], swap(across_fc2, core_bit))
    halves = halves_across(second_across)
    second_rest = add_low(keep_fc2[1:], swap(send_fc2, core_bit))
    (
        mixed,
        d_middle,
        grad_gain_hidden,
        grad_gain_ffn_in,
        grad_gain_attn,
        *grad_pieces,
        send_first,
        keep_first,
    ) = run_kernel(
        functools.partial(backward_kernel, line_size),
        "feed_forward_back",
        13,
        place_here,
        (
            *dealt,
            after(grad_in, second_across),
            *kept,
            *gains,
            scale_cols.reshape(line_size, part),
        ),
        (*first_planes, *first_others, *second_planes, *second_others, hidden, below, activated),
        [
            ((rows_here, width), low),
            ((rows_here, width), wide),
            ((1, hidden_width), wide),
            ((1, width), wide),
            ((1, width), wide),
            *[((rows_here, part), low)] * line_size,
        ],
        [((4, block_rows, summed), low), ((4, block_rows, summed), low)],
        [
            ((width, width), low),
            ((width, hidden_width), low),
            ((hidden_width, width), low),
            ((rows_here, hidden_width), wide),
            ((rows_here, hidden_width), wide),
            ((rows_here, hidden_width), low),
            ((rows_here, hidden_width), wide),
            ((width, hidden_width), low),
            ((width, width), low),
        ],
        3 + 24 + 16,
    )

    grad_pieces = all_after(grad_pieces, *halves)
    grad_pieces = grad_pieces[:1] + [
        turn(piece, line_size - steps) for steps, piece in enumerate(grad_pieces[1:], 1)
    ]
    got_first = swap(after(send_first, *halves), core_bit)
    first = add_low(keep_first, got_first)
    grad_pieces[0] = after(grad_pieces[0], got_first)
    second_x, second_y = add_across(halves, second_rest[0], second_rest[1])
    second_got = [swap(second_x, x_bit), swap(second_y, y_bit)]
    send_qkv, keep_qkv, diagonal_sums_here, deltas, gain_sums, d_normed = run_kernel(
        functools.partial(attend_back_kernel, heads, head_size, line_size),
        "attend_back",
        12,
        place_here,
        (*grad_pieces, qkv, attention),
        (probs, normed_row, wqkv_part),
        [
            ((4, block_rows, 3 * part), low),
            ((4, block_rows, 3 * part), low),
            ((heads, 2 * row_len), wide),
            ((row_len, heads), wide),
            ((width, 1), wide),
        ],
        [((row_len, width), low)],
        [
            ((row_len, part), low),
            ((row_len, 3 * part), low),
            ((width, 3 * part), low),
            ((lanes, 2 * row_len - lanes), wide),
            ((heads, row_len, row_len), low),
            ((row_len, width), low),
            ((width, 3 * part), low),
            ((row_len, width), low),
        ],
        heads + 3,
    )
    d_normed_low = lax.psum_scatter(d_normed, "blk", scatter_dimension=0, tiled=True)
    d_normed_here = d_normed_low.astype(jnp.float32)

    second_got = all_after(second_got, d_normed)
    second_line = sum_parts([second_rest[2], *second_got]).astype(low)
    grad_gain_in = gain_sums[:, 0] / gain_in
    d_table = lax.dot_general(
        diagonal_sums_here, selector, (((1,), (1,)), ((), ())), precision=highest
    )
    small = (gain_sums[:, 0], grad_gain_attn[0], grad_gain_ffn_in[0], grad_gain_hidden[0])
    own_small = (jnp.sum(deltas, axis=0), d_table)
    sizes = [math.prod(value.shape) for value in small]
    flat = jnp.concatenate([value.reshape(-1) for value in small + own_small])
    tail_cols, pack_cols = 3 * part, summed + 3 * part
    flat = jnp.pad(flat, (0, -flat.shape[0] % tail_cols)).reshape(-1, tail_cols)
    terms = flat.astype(low)
    got = swap(send_qkv, core_bit)
    halves = halves_across(after(first[0], second_line, got))
    first_x, first_y = add_across(halves, first[1], first[2])
    last = add_low(keep_qkv, got)
    terms = add_low(terms, swap(terms, core_bit))
    last_got = [
        swap(jnp.concatenate([last[slot], terms], axis=0), bits) for slot, bits in enumerate(far_first[:3])
    ]
    last_line = sum_parts([last[3]] + [piece[:block_rows] for piece in last_got]).astype(low)
    plane_sums = [piece[block_rows:].astype(wide) for piece in last_got]
    flat = (terms.astype(wide) + plane_sums[1]) + (plane_sums[2] + plane_sums[0])
    flat = flat.reshape(-1)
    flat = jnp.pad(flat, (0, -flat.shape[0] % (2 * pack_cols))).reshape(-1, pack_cols).astype(low)
    first_x, first_y = all_after([first_x, first_y], *last_got)
    first_got = [swap(first_x, x_bit), swap(first_y, y_bit)]
    first_line = sum_parts([first[3], *first_got]).astype(low)
    second_line = after(second_line, *last_got, *halves)
    second_dealt = deal_line(second_line.reshape((line_size, -1, width)))
    grad_fc2 = sum_parts(second_dealt)
    both_lines = after(jnp.concatenate([first_line, last_line], axis=1), d_normed_low, *second_dealt[1:])
    both_lines = both_lines.reshape(line_size, shard_rows, pack_cols)
    spread = jnp.broadcast_to(flat[None], (line_size,) + flat.shape)
    dealt_back = deal_line(jnp.concatenate([both_lines, spread], axis=1))
    flats = [piece[shard_rows:].astype(wide).reshape(-1) for piece in dealt_back]
    common = sum(sizes)
    totals = [flat[:common] for flat in flats]
    while len(totals) > 1:
        half = len(totals) // 2
        totals = [totals[step] + totals[step + half] for step in range(half)]
    owned = common + heads + heads * bucket_count
    by_owner = in_line([flat[None, common:owned] for flat in flats])
    grad_scale = by_owner[:, :heads].reshape(-1)
    d_bias = by_owner[:, heads:].reshape(all_heads, bucket_count)
    dealt_back = [piece[:shard_rows] for piece in dealt_back]
    grad_fc1 = sum_parts([piece[:, :hidden_width] for piece in dealt_back])
    grad_out = sum_parts([piece[:, hidden_width:summed] for piece in dealt_back])
    grad_qkv = in_line([piece[:, summed:].astype(jnp.float32) for piece in dealt_back])
    grad_qkv = grad_qkv.reshape(line_size, shard_rows, 3, part).transpose(1, 2, 0, 3)
    grad_qkv = grad_qkv.reshape(shard_rows, 3 * width)

    _, norm_in_back = jax.vjp(lambda value: layer_norm(value, gain_in), tokens[0].astype(jnp.float32))
    (d_input_part,) = norm_in_back(d_normed_here)
    grad_tokens = (d_middle + d_input_part).astype(jnp.bfloat16)[None]

    sums, begin = [], 0
    for size in sizes:
        sums.append(totals[0][begin : begin + size])
        begin += size
    return (
        mixed[None],
        grad_tokens,
        grad_qkv,
        grad_out,
        grad_fc1,
        grad_fc2,
        sums[0] / gain_in,
        sums[1],
        sums[2],
        sums[3],
        grad_scale / head_scale,
        d_bias.T,
    )


def on_device(dp_size, line_size, tokens, *rest):
    head_scale, row_len = rest[10], tokens.shape[1] * line_size
    whole_heads = head_scale.shape[0] % line_size == 0 and dp_size % line_size == 0
    if dp_size == 8 and line_size == 4 and whole_heads and row_len % lanes == 0:
        return by_heads(tokens, *rest)
    return by_sequence(tokens, *rest)


def solution(mesh):
    return jax.shard_map(
        functools.partial(on_device, mesh.shape["dp"], mesh.shape["blk"]),
        mesh=mesh,
        in_specs=(
            P("dp", "blk", None),
            P("dp", None),
            P(),
            P(("dp", "blk"), None),
            P(("dp", "blk"), None),
            P(("dp", "blk"), None),
            P(("dp", "blk"), None),
            P(),
            P(),
            P(),
            P(),
            P(),
            P(),
            P("dp", "blk", None),
        ),
        out_specs=(
            P("dp", "blk", None),
            P("dp", "blk", None),
            P(("dp", "blk"), None),
            P(("dp", "blk"), None),
            P(("dp", "blk"), None),
            P(("dp", "blk"), None),
            P(),
            P(),
            P(),
            P(),
            P(),
            P(),
        ),
        check_vma=False,
    )
```

```python
import functools
import math

import jax
import jax.numpy as jnp
from jax import lax
from jax.experimental import pallas as pl
from jax.experimental.pallas import tpu as pltpu
from jax.sharding import PartitionSpec as P

epsilon = 1e-05
masked_score = -1e30
query_scale = 0.125
highest = lax.Precision.HIGHEST


def layer_norm(value, gain):
    center = value - jnp.mean(value, axis=-1, keepdims=True)
    spread = jnp.mean(center * center, axis=-1, keepdims=True)
    return center * lax.rsqrt(spread + epsilon) * gain


def hidden_norm(value, gain):
    return layer_norm(jax.nn.gelu(value, approximate=False), gain)


def column_product(left, right):
    return lax.dot_general(
        left, right, (((0,), (0,)), ((), ())), preferred_element_type=jnp.float32
    )


def times_transpose(left, matrix):
    return lax.dot_general(
        left, matrix, (((1,), (1,)), ((), ())), preferred_element_type=jnp.float32
    )


def toeplitz(diagonals, rows, cols):
    heads = diagonals.shape[0]
    padded = jnp.pad(diagonals, ((0, 0), (0, 1)))
    stride = rows + cols - 1
    tiled = jnp.tile(padded, (1, rows))[:, : rows * stride].reshape(heads, rows, stride)
    return tiled[:, :, rows - 1 : rows - 1 + cols]


def diagonal_sums(grid):
    heads, rows, cols = grid.shape
    flipped = grid[:, ::-1, :]
    padded = jnp.pad(flipped, ((0, 0), (0, 0), (0, rows)))
    skewed = padded.reshape(heads, -1)[:, : rows * (rows + cols - 1)].reshape(
        heads, rows, rows + cols - 1
    )
    return jnp.sum(skewed, axis=1)


def by_sequence(
    tokens,
    lengths,
    distance_bucket,
    w_qkv,
    w_out,
    w_fc1,
    w_fc2,
    gain_in,
    gain_attn,
    gain_ffn_in,
    gain_hidden,
    head_scale,
    bias_table,
    cotangent,
):
    rows_here = tokens.shape[1]
    width = tokens.shape[2]
    heads = head_scale.shape[0]
    head_size = width // heads
    reach = distance_bucket.shape[0] // 2
    bucket_count = bias_table.shape[0]
    row_len = rows_here * lax.axis_size("blk")
    key_block = math.gcd(row_len, 512)
    block_count = row_len // key_block
    query_anchor = lax.axis_index("blk") * rows_here
    positions = query_anchor + jnp.arange(rows_here, dtype=jnp.int32)
    ends = jnp.cumsum(lengths[0])
    bucket_ids = jnp.arange(bucket_count, dtype=jnp.int32)

    def document_of(where):
        return jnp.sum((where[:, None] >= ends[None, :]).astype(jnp.int32), axis=1)

    query_docs = document_of(positions)

    def bucket_index(query_start, rows, key_start, cols):
        steps = jnp.arange(rows + cols - 1, dtype=jnp.int32)
        relative = key_start - query_start - (rows - 1) + steps
        return jnp.take(distance_bucket, jnp.clip(relative, -reach, reach) + reach)

    def scores_for(query_heads, query_start, query_doc, key_heads, key_start, key_doc):
        rows = query_heads.shape[0]
        cols = key_heads.shape[0]
        raw = jnp.einsum("qhd,khd->hqk", query_heads, key_heads, preferred_element_type=jnp.float32)
        buckets = bucket_index(query_start, rows, key_start, cols)
        diagonals = jnp.take(bias_table, buckets, axis=0).T
        same = query_doc[:, None] == key_doc[None, :]
        full = raw + toeplitz(diagonals, rows, cols)
        return (jnp.where(same[None], full, masked_score), same, buckets)

    residual_in = tokens[0].astype(jnp.float32)
    wqkv_all, wout_all = (
        lax.all_gather(w_qkv, ("dp", "blk"), axis=0, tiled=True),
        lax.all_gather(w_out, ("dp", "blk"), axis=0, tiled=True),
    )
    normed_f, norm_in_back = jax.vjp(layer_norm, residual_in, gain_in)
    normed_in = normed_f.astype(jnp.bfloat16)
    projected = jnp.dot(normed_in, wqkv_all, preferred_element_type=jnp.float32)
    queries = (projected[:, :width] * query_scale).astype(jnp.bfloat16)
    keys_here = projected[:, width : 2 * width].astype(jnp.bfloat16)
    values_here = projected[:, 2 * width :].astype(jnp.bfloat16)
    query_heads = queries.reshape(rows_here, heads, head_size)
    best = jnp.full((heads, rows_here), masked_score, jnp.float32)
    key_piece = lax.all_gather(keys_here, "blk", axis=0, tiled=True)
    value_piece = lax.all_gather(values_here, "blk", axis=0, tiled=True)
    length = key_piece.shape[0]
    key_pos = jnp.arange(length, dtype=jnp.int32)
    scores, same, buckets = scores_for(
        query_heads,
        query_anchor,
        query_docs,
        key_piece.reshape(length, heads, head_size),
        jnp.int32(0),
        document_of(key_pos),
    )
    new_best = jnp.maximum(best, jnp.max(scores, axis=-1))
    weights = jnp.where(same[None], jnp.exp(scores - new_best[..., None]), 0.0)
    total = jnp.sum(weights, axis=-1)
    accum = jnp.einsum(
        "hqk,khd->hqd",
        weights.astype(jnp.bfloat16),
        value_piece.reshape(length, heads, head_size),
        preferred_element_type=jnp.float32,
    )
    best, total, accum = (new_best, total, accum)
    log_total = best + jnp.log(total)
    attention = jnp.transpose(accum / total[..., None], (1, 0, 2)).reshape(rows_here, width)
    scale_cols = jnp.repeat(head_scale, head_size)
    scaled = (attention * scale_cols).astype(jnp.bfloat16)
    attn_out = jnp.dot(scaled, wout_all, preferred_element_type=jnp.float32)
    normed_attn, norm_attn_back = jax.vjp(layer_norm, attn_out, gain_attn)
    middle = residual_in + normed_attn
    fc1_all, fc2_all = (
        lax.all_gather(w_fc1, ("dp", "blk"), axis=0, tiled=True),
        lax.all_gather(w_fc2, ("dp", "blk"), axis=0, tiled=True),
    )
    normed_mid_f, norm_mid_back = jax.vjp(layer_norm, middle, gain_ffn_in)
    normed_mid = normed_mid_f.astype(jnp.bfloat16)
    hidden = jnp.dot(normed_mid, fc1_all, preferred_element_type=jnp.float32)
    activated_f, hidden_back = jax.vjp(hidden_norm, hidden, gain_hidden)
    activated = activated_f.astype(jnp.bfloat16)
    mixed = (middle + jnp.dot(activated, fc2_all, preferred_element_type=jnp.float32)).astype(
        jnp.bfloat16
    )
    grad_in = cotangent[0]
    fc1_back, fc2_back = (
        lax.all_gather(w_fc1, ("dp", "blk"), axis=0, tiled=True),
        lax.all_gather(w_fc2, ("dp", "blk"), axis=0, tiled=True),
    )
    grad_fc2 = lax.psum_scatter(
        column_product(activated, grad_in), ("dp", "blk"), scatter_dimension=0, tiled=True
    )
    d_activated = times_transpose(grad_in, fc2_back)
    d_hidden_f, grad_gain_hidden = hidden_back(d_activated)
    d_hidden = d_hidden_f.astype(jnp.bfloat16)
    grad_fc1 = lax.psum_scatter(
        column_product(normed_mid, d_hidden), ("dp", "blk"), scatter_dimension=0, tiled=True
    )
    d_mid_part, grad_gain_ffn_in = norm_mid_back(times_transpose(d_hidden, fc1_back))
    d_middle = grad_in.astype(jnp.float32) + d_mid_part
    d_attn_f, grad_gain_attn = norm_attn_back(d_middle)
    d_attn_out = d_attn_f.astype(jnp.bfloat16)
    qkv_back, out_back = (
        lax.all_gather(w_qkv, ("dp", "blk"), axis=0, tiled=True),
        lax.all_gather(w_out, ("dp", "blk"), axis=0, tiled=True),
    )
    grad_out = lax.psum_scatter(
        column_product(scaled, d_attn_out), ("dp", "blk"), scatter_dimension=0, tiled=True
    )
    d_scaled = times_transpose(d_attn_out, out_back)
    grad_scale = jnp.sum((d_scaled * attention).reshape(rows_here, heads, head_size), axis=(0, 2))
    d_attention = (d_scaled * scale_cols).astype(jnp.bfloat16)
    grad_heads = d_attention.reshape(rows_here, heads, head_size)
    row_delta = jnp.sum(
        (d_attention.astype(jnp.float32) * attention).reshape(rows_here, heads, head_size), axis=2
    ).T
    keys_back, values_back = (
        lax.all_gather(keys_here, "blk", axis=0, tiled=True),
        lax.all_gather(values_here, "blk", axis=0, tiled=True),
    )

    def pair_grads(
        query_part,
        grad_part,
        total_part,
        delta_part,
        query_start,
        query_doc,
        key_part,
        value_part,
        key_start,
        key_doc,
    ):
        scores, same, buckets = scores_for(
            query_part, query_start, query_doc, key_part, key_start, key_doc
        )
        probs = jnp.where(same[None], jnp.exp(scores - total_part[..., None]), 0.0)
        d_probs = jnp.einsum(
            "qhd,khd->hqk", grad_part, value_part, preferred_element_type=jnp.float32
        )
        d_scores = probs * (d_probs - delta_part[..., None])
        return (probs.astype(jnp.bfloat16), d_scores, buckets)

    def bias_sum(d_scores, buckets):
        sums = diagonal_sums(d_scores)
        selector = (buckets[:, None] == bucket_ids[None, :]).astype(jnp.float32)
        return jnp.dot(sums, selector, precision=highest).T

    def key_slices(index):
        begin = index * key_block
        key_part = lax.dynamic_slice_in_dim(keys_back, begin, key_block, 0).reshape(
            key_block, heads, head_size
        )
        value_part = lax.dynamic_slice_in_dim(values_back, begin, key_block, 0).reshape(
            key_block, heads, head_size
        )
        return (key_part, value_part, begin)

    query_carry = (
        jnp.zeros((rows_here, heads, head_size), jnp.float32),
        jnp.zeros((bucket_count, heads), jnp.float32),
    )

    def key_step(carry, index):
        d_query, d_bias = carry
        key_part, value_part, begin = key_slices(index)
        key_doc = document_of(begin + jnp.arange(key_block, dtype=jnp.int32))
        probs_low, d_scores, buckets = pair_grads(
            query_heads,
            grad_heads,
            log_total,
            row_delta,
            query_anchor,
            query_docs,
            key_part,
            value_part,
            begin,
            key_doc,
        )
        scores_low = d_scores.astype(jnp.bfloat16)
        d_query = d_query + jnp.einsum(
            "hqk,khd->qhd", scores_low, key_part, preferred_element_type=jnp.float32
        )
        d_key = jnp.einsum(
            "hqk,qhd->khd", scores_low, query_heads, preferred_element_type=jnp.float32
        ).reshape(key_block, width)
        d_value = jnp.einsum(
            "hqk,qhd->khd", probs_low, grad_heads, preferred_element_type=jnp.float32
        ).reshape(key_block, width)
        return (
            (d_query, d_bias + bias_sum(d_scores, buckets)),
            jnp.concatenate([d_key, d_value], axis=1),
        )

    (d_query, d_bias), kv_terms = lax.scan(
        key_step, query_carry, jnp.arange(block_count, dtype=jnp.int32)
    )
    kv_grad = lax.psum_scatter(
        kv_terms.reshape(row_len, 2 * width).astype(jnp.bfloat16),
        "blk",
        scatter_dimension=0,
        tiled=True,
    )
    d_query_low = d_query.reshape(rows_here, width).astype(jnp.bfloat16)
    d_projected = jnp.concatenate(
        [d_query_low * jnp.asarray(query_scale, jnp.bfloat16), kv_grad], axis=1
    )
    grad_qkv = lax.psum_scatter(
        column_product(normed_in, d_projected), ("dp", "blk"), scatter_dimension=0, tiled=True
    )
    d_input_part, grad_gain_in = norm_in_back(times_transpose(d_projected, qkv_back))
    grad_tokens = (d_middle + d_input_part).astype(jnp.bfloat16)[None]
    small = lax.psum(
        (grad_gain_in, grad_gain_attn, grad_gain_ffn_in, grad_gain_hidden, grad_scale, d_bias),
        ("dp", "blk"),
    )
    return (
        mixed[None],
        grad_tokens,
        grad_qkv,
        grad_out,
        grad_fc1,
        grad_fc2,
        small[0],
        small[1],
        small[2],
        small[3],
        small[4],
        small[5],
    )


lanes = 128
core_bit, x_bit, y_bit = 1, 2, 4


def swap(value, bit):
    size = lax.axis_size("dp")
    return lax.ppermute(value, "dp", [(i, i ^ bit) for i in range(size)])


def turn(value, steps):
    size = lax.axis_size("blk")
    return lax.ppermute(value, "blk", [(i, (i + steps) % size) for i in range(size)])


def swap_line(value, bit):
    size = lax.axis_size("blk")
    return lax.ppermute(value, "blk", [(i, i ^ bit) for i in range(size)])


def pick(stack, index):
    return lax.dynamic_index_in_dim(stack, index, 0, keepdims=False)


def after(value, *others):
    return lax.optimization_barrier((value, *others))[0]


def all_after(values, *others):
    return list(lax.optimization_barrier((*values, *others))[: len(values)])


def turns(value):
    size = lax.axis_size("blk")
    return [value] + [turn(value, steps) for steps in range(1, size)]


def in_line(pieces):
    here, size = lax.axis_index("blk"), lax.axis_size("blk")
    ordered = [lax.select_n(lax.rem(here - owner + size, size), *pieces) for owner in range(size)]
    return jnp.concatenate(ordered, axis=0)


def deal_line(stack):
    here, size = lax.axis_index("blk"), lax.axis_size("blk")
    got = [pick(stack, here)]
    for steps in range(1, size):
        got.append(turn(pick(stack, lax.rem(here + steps, size)), steps))
    return got


def swap_cores(blocks):
    return [swap(block, core_bit) for block in blocks]


def beside(line):
    return [line, swap(line, x_bit), swap(line, y_bit)]


def across_halves(near):
    _, along_x, along_y = near
    half = along_x.shape[0] // 2
    return [swap(along_y[:half], x_bit), swap(along_x[half:], y_bit)]


def across_plane(near):
    return near + [jnp.concatenate(across_halves(near), axis=0)]


def add_low(left, right):
    return (left.astype(jnp.float32) + right.astype(jnp.float32)).astype(jnp.bfloat16)


def halves_across(across):
    half = across.shape[0] // 2
    return [swap(across[:half], x_bit), swap(across[half:], y_bit)]


def add_across(halves, to_x, to_y):
    from_x, from_y = halves
    half = from_x.shape[0]
    to_y = jnp.concatenate([add_low(to_y[:half], from_x), to_y[half:]], axis=0)
    to_x = jnp.concatenate([to_x[:half], add_low(to_x[half:], from_y)], axis=0)
    return to_x, to_y


def add_planes(to_x, to_y, own):
    got_x, got_y = swap(to_x, x_bit), swap(to_y, y_bit)
    total = own.astype(jnp.float32) + got_x.astype(jnp.float32) + got_y.astype(jnp.float32)
    return total.astype(jnp.bfloat16)


def sum_parts(parts):
    total = parts[0].astype(jnp.float32)
    for part in parts[1:]:
        total = total + part.astype(jnp.float32)
    return total


def add_line(line):
    size = lax.axis_size("blk")
    return sum_parts(deal_line(line.reshape((size, -1) + line.shape[1:])))


def contract(left, right, left_axis, right_axis):
    return lax.dot_general(
        left, right, (((left_axis,), (right_axis,)), ((), ())), preferred_element_type=jnp.float32
    )


tile_cols = 512
far_first = (x_bit | y_bit, x_bit, y_bit, 0)


def run_kernel(kernel, name, micros, place_here, operands, far, outputs, far_outputs, scratch=(), copies=1):
    near_spec, far_spec = pl.BlockSpec(memory_space=pltpu.VMEM), pl.BlockSpec(memory_space=pl.ANY)
    return pl.pallas_call(
        kernel,
        out_shape=[jax.ShapeDtypeStruct(shape, dtype) for shape, dtype in (*outputs, *far_outputs)],
        in_specs=[pl.BlockSpec(memory_space=pltpu.SMEM)] + [near_spec] * len(operands) + [far_spec] * len(far),
        out_specs=[near_spec] * len(outputs) + [far_spec] * len(far_outputs),
        scratch_shapes=[pltpu.VMEM(shape, dtype) for shape, dtype in scratch]
        + [pltpu.SemaphoreType.DMA((copies,))],
        compiler_params=pltpu.CompilerParams(vmem_limit_bytes=52 * 2**20),
        cost_estimate=pl.CostEstimate(
            flops=int(micros * 1.1e9), bytes_accessed=int(micros * 3.6e6), transcendentals=0
        ),
        name=name,
    )(place_here, *operands, *far)


class Copies:
    def __init__(self, semaphores):
        self.semaphores, self.used = semaphores, 0

    def start(self, source, target):
        copy = pltpu.make_async_copy(source, target, self.semaphores.at[self.used])
        self.used += 1
        copy.start()
        return copy


def wait_all(copies):
    for copy in copies:
        copy.wait()


def normalize(value):
    center = value - jnp.mean(value, axis=-1, keepdims=True)
    spread = jnp.mean(center * center, axis=-1, keepdims=True)
    scale = lax.rsqrt(spread + epsilon)
    return center * scale, scale


def normalize_back(normed, scale, grad, gain):
    inner = grad * gain
    middle = jnp.mean(inner, axis=-1, keepdims=True)
    along = jnp.mean(inner * normed, axis=-1, keepdims=True)
    return scale * (inner - middle - normed * along), jnp.sum(grad * normed, axis=0, keepdims=True)


def block_indices(place_ref):
    me = place_ref[0]
    return [me ^ bits ^ core_bit for bits in far_first], [me ^ bits for bits in far_first]


near_first = (0, x_bit, y_bit, x_bit | y_bit)


def fill_planes(copies, place_ref, blocks, cols, out_ref):
    bits = near_first + tuple(bit | core_bit for bit in near_first)
    started = []
    for bit, block in zip(bits, blocks):
        rows = block.shape[0]
        begin = pl.multiple_of((place_ref[0] ^ bit) * rows, rows)
        started.append(copies.start(block.at[:, cols], out_ref.at[pl.ds(begin, rows), :]))
    return started


def before(place_ref, steps, size):
    return lax.rem(place_ref[1] - steps + size, size)


def bias_kernel(heads, place_ref, diagonal_ref, bias_ref, semaphores):
    for head in range(heads):
        for step in range(diagonal_ref.shape[1] // lanes - 1):
            window = diagonal_ref[head : head + 1, step * lanes : (step + 2) * lanes]
            window = jnp.broadcast_to(window, (lanes, 2 * lanes))
            window = pltpu.roll(window, 0, 1, stride=1, stride_axis=0)
            bias_ref[head, :, step * lanes : (step + 1) * lanes] = window[:, lanes:]


def attend_kernel(
    heads, head_size, place_ref, gain_ref, doc_col_ref, doc_row_ref, scale_ref, tokens_ref, *refs
):
    parts, refs = refs[:8], refs[8:]
    bias_in, w_ref, qkv_ref, normed_ref, attention_ref, scaled_ref, probs_out, bias, probs_ref, semaphores = refs
    copies = Copies(semaphores)
    last = parts[0].shape[1]
    arriving = fill_planes(copies, place_ref, parts, slice(last - w_ref.shape[1], last), w_ref)
    bias_here = copies.start(bias_in, bias)
    leaving = []
    length = tokens_ref.shape[0]
    blocks = length // lanes
    width = heads * head_size
    for block in range(blocks):
        rows = slice(block * lanes, (block + 1) * lanes)
        normed, _ = normalize(tokens_ref[rows, :].astype(jnp.float32))
        normed_ref[rows, :] = (normed * gain_ref[...]).astype(jnp.bfloat16)
    wait_all(arriving)
    bias_here.wait()
    projected = contract(normed_ref[...], w_ref[...], 1, 0)
    qkv_ref[:, :width] = (projected[:, :width] * query_scale).astype(jnp.bfloat16)
    qkv_ref[:, width:] = projected[:, width:].astype(jnp.bfloat16)
    for head in range(heads):
        low = head * head_size
        keys = qkv_ref[:, width + low : width + low + head_size]
        values = qkv_ref[:, 2 * width + low : 2 * width + low + head_size]
        all_scores = contract(qkv_ref[:, low : low + head_size], keys, 1, 1)
        for block in range(blocks):
            rows = slice(block * lanes, (block + 1) * lanes)
            first = (blocks - 1 - block) * lanes
            scores = all_scores[rows, :] + bias[head, :, first : first + length]
            same = doc_col_ref[rows, :] == doc_row_ref[...]
            scores = jnp.where(same, scores, masked_score)
            weights = jnp.exp(scores - jnp.max(scores, axis=1, keepdims=True))
            probs = weights * (1.0 / jnp.sum(weights, axis=1, keepdims=True))
            probs = probs.astype(jnp.bfloat16)
            probs_ref[head, rows, :] = probs
        leaving.append(copies.start(probs_ref.at[head], probs_out.at[head]))
        attention_ref[:, low : low + head_size] = contract(probs_ref[head], values, 1, 0)
    scaled_ref[...] = (attention_ref[...] * scale_ref[...]).astype(jnp.bfloat16)
    wait_all(leaving)


def forward_kernel(line, place_ref, *refs):
    pieces, refs = refs[:line], refs[line:]
    tokens_ref, gain_attn_ref, gain_mid_ref, gain_hidden_ref, cotangent_ref, *refs = refs
    blocks, refs = refs[:8], refs[8:]
    (attn_ref, middle_ref, normed_ref, mean_ref, scale_ref, activated_ref,
     hidden_out, below_out, across_out, send_out, keep_out,
     wout_ref, fc1_ref, hidden_ref, below_ref, grads_ref, semaphores) = refs
    copies = Copies(semaphores)
    part = pieces[0].shape[1]
    hidden_width, width = fc1_ref.shape[1], wout_ref.shape[1]
    wout_here = fill_planes(copies, place_ref, blocks, slice(hidden_width, hidden_width + width), wout_ref)
    fc1_here = fill_planes(copies, place_ref, blocks, slice(0, hidden_width), fc1_ref)
    leaving = []
    wait_all(wout_here)
    attn = jnp.zeros(attn_ref.shape, jnp.float32)
    for steps in range(line):
        rows = pl.ds(pl.multiple_of(before(place_ref, steps, line) * part, part), part)
        attn = attn + contract(pieces[steps][...], wout_ref[rows, :], 1, 0)
    attn_ref[...] = attn
    normed, _ = normalize(attn)
    middle = tokens_ref[...].astype(jnp.float32) + normed * gain_attn_ref[...]
    middle_ref[...] = middle
    normed, _ = normalize(middle)
    normed = (normed * gain_mid_ref[...]).astype(jnp.bfloat16)
    normed_ref[...] = normed
    tiles = [slice(begin, begin + tile_cols) for begin in range(0, hidden_width, tile_cols)]
    total = jnp.zeros(mean_ref.shape, jnp.float32)
    wait_all(fc1_here)
    for cols in tiles:
        hidden = contract(normed, fc1_ref[:, cols], 1, 0)
        below = 0.5 * (1.0 + lax.erf(hidden * (0.5**0.5)))
        hidden_ref[:, cols] = hidden
        below_ref[:, cols] = below
        leaving.append(copies.start(hidden_ref.at[:, cols], hidden_out.at[:, cols]))
        leaving.append(copies.start(below_ref.at[:, cols], below_out.at[:, cols]))
        total = total + jnp.sum(hidden * below, axis=1, keepdims=True)
    mean = total / hidden_width
    total = jnp.zeros(mean_ref.shape, jnp.float32)
    for cols in tiles:
        center = hidden_ref[:, cols] * below_ref[:, cols] - mean
        total = total + jnp.sum(center * center, axis=1, keepdims=True)
    scale = lax.rsqrt(total / hidden_width + epsilon)
    mean_ref[...] = mean
    scale_ref[...] = scale
    for cols in tiles:
        center = hidden_ref[:, cols] * below_ref[:, cols] - mean
        activated_ref[:, cols] = (center * scale * gain_hidden_ref[:, cols]).astype(jnp.bfloat16)
    size = grads_ref.shape[1]
    sent, kept = block_indices(place_ref)
    outs = [across_out] + [send_out.at[slot] for slot in range(3)] + [keep_out.at[slot] for slot in range(4)]
    for slot, (index, out) in enumerate(zip(sent + kept, outs)):
        cols = pl.ds(pl.multiple_of(index * size, lanes), size)
        grads_ref[slot] = contract(activated_ref[:, cols], cotangent_ref[...], 0, 0).astype(jnp.bfloat16)
        leaving.append(copies.start(grads_ref.at[slot], out))
    wait_all(leaving)


def backward_kernel(line, place_ref, *refs):
    pieces, refs = refs[:line], refs[line:]
    (cotangent_ref, attn_ref, middle_ref, normed_ref, mean_ref, scale_ref, gain_attn_ref, gain_mid_ref,
     gain_hidden_ref, head_scale_ref, *refs) = refs
    first_blocks, second_blocks, refs = refs[:8], refs[8:16], refs[16:]
    hidden_in, below_in, activated_in, *refs = refs
    mixed_ref, d_middle_ref, d_hidden_gain_ref, d_mid_gain_ref, d_attn_gain_ref, *refs = refs
    grads, refs = refs[:line], refs[line:]
    (send_out, keep_out, wout_ref, fc1_ref, fc2_ref, hidden_ref, below_ref, activated_ref, inner_ref, fc1_grad,
     out_grad, semaphores) = refs
    copies = Copies(semaphores)
    part = pieces[0].shape[1]
    hidden_width, width = fc1_ref.shape[1], wout_ref.shape[1]
    hidden_here = [copies.start(hidden_in, hidden_ref), copies.start(below_in, below_ref)]
    fc2_here = fill_planes(copies, place_ref, second_blocks, slice(0, width), fc2_ref)
    fc1_here = fill_planes(copies, place_ref, first_blocks, slice(0, hidden_width), fc1_ref)
    activated_here = copies.start(activated_in, activated_ref)
    wout_here = fill_planes(
        copies, place_ref, first_blocks, slice(hidden_width, hidden_width + width), wout_ref
    )
    grad_in = cotangent_ref[...]
    mean, scale = mean_ref[...], scale_ref[...]
    tiles = [slice(begin, begin + tile_cols) for begin in range(0, hidden_width, tile_cols)]
    wait_all(hidden_here + fc2_here)
    total = jnp.zeros(mean.shape, jnp.float32)
    along = jnp.zeros(mean.shape, jnp.float32)
    for cols in tiles:
        d_activated = contract(grad_in, fc2_ref[cols, :], 1, 1)
        normed = (hidden_ref[:, cols] * below_ref[:, cols] - mean) * scale
        d_hidden_gain_ref[:, cols] = jnp.sum(d_activated * normed, axis=0, keepdims=True)
        inner = d_activated * gain_hidden_ref[:, cols]
        inner_ref[:, cols] = inner
        total = total + jnp.sum(inner, axis=1, keepdims=True)
        along = along + jnp.sum(inner * normed, axis=1, keepdims=True)
    total, along = total / hidden_width, along / hidden_width
    d_normed = jnp.zeros(middle_ref.shape, jnp.float32)
    normed_mid = normed_ref[...].T
    wait_all(fc1_here)
    for cols in tiles:
        hidden, below = hidden_ref[:, cols], below_ref[:, cols]
        normed = (hidden * below - mean) * scale
        slope = below + hidden * jnp.exp(-0.5 * hidden * hidden) * (1.0 / math.sqrt(2.0 * math.pi))
        d_hidden = scale * (inner_ref[:, cols] - total - normed * along) * slope
        d_hidden = d_hidden.astype(jnp.bfloat16)
        fc1_grad[:, cols] = contract(normed_mid, d_hidden, 1, 0).astype(jnp.bfloat16)
        d_normed = d_normed + contract(d_hidden, fc1_ref[:, cols], 1, 1)
    size = send_out.shape[1]
    sent, kept = block_indices(place_ref)
    outs = [send_out.at[slot] for slot in range(4)] + [keep_out.at[slot] for slot in range(4)]
    places = [pl.ds(pl.multiple_of(index * size, size), size) for index in sent + kept]
    leaving = [
        copies.start(fc1_grad.at[rows, :], out.at[:, :hidden_width]) for rows, out in zip(places, outs)
    ]
    normed, scale = normalize(middle_ref[...])
    d_value, d_mid_gain_ref[...] = normalize_back(normed, scale, d_normed, gain_mid_ref[...])
    d_middle = grad_in.astype(jnp.float32) + d_value
    d_middle_ref[...] = d_middle
    normed, scale = normalize(attn_ref[...])
    d_value, d_attn_gain_ref[...] = normalize_back(normed, scale, d_middle, gain_attn_ref[...])
    d_attn = d_value.astype(jnp.bfloat16)
    wait_all(wout_here)
    for steps in range(line):
        owner = before(place_ref, steps, line)
        rows = pl.ds(pl.multiple_of(owner * part, part), part)
        d_scaled = contract(d_attn, wout_ref[rows, :], 1, 1)
        grads[steps][...] = (d_scaled * head_scale_ref[pl.ds(owner, 1), :]).astype(jnp.bfloat16)
        out_grad[rows, :] = contract(pieces[steps][...], d_attn, 0, 0).astype(jnp.bfloat16)
    leaving += [
        copies.start(out_grad.at[rows, :], out.at[:, hidden_width:]) for rows, out in zip(places, outs)
    ]
    activated_here.wait()
    mixed = middle_ref[...] + contract(activated_ref[...], fc2_ref[...], 1, 0)
    mixed_ref[...] = mixed.astype(jnp.bfloat16)
    wait_all(leaving)


def attend_back_kernel(heads, head_size, line, place_ref, *refs):
    pieces, refs = refs[:line], refs[line:]
    (qkv_ref, attention_ref, probs_in, normed_in, w_in,
     send_ref, keep_ref, diagonal_ref, delta_ref, gain_ref, d_normed_out,
     grad_ref, out_ref, w_grad, sums, probs_ref, normed_ref, w_ref, d_normed_ref, semaphores) = refs
    copies = Copies(semaphores)
    probs_here = [copies.start(probs_in.at[head], probs_ref.at[head]) for head in range(heads)]
    rest_here = [copies.start(w_in, w_ref), copies.start(normed_in, normed_ref)]
    length = qkv_ref.shape[0]
    blocks = length // lanes
    width = heads * head_size
    rows_here = pieces[0].shape[0]
    for steps in range(line):
        owner = lax.rem(place_ref[1] + steps, line)
        grad_ref[pl.ds(pl.multiple_of(owner * rows_here, rows_here), rows_here), :] = pieces[steps][...]
    diagonal_ref[...] = jnp.zeros_like(diagonal_ref)
    for head in range(heads):
        sums[...] = jnp.zeros_like(sums)
        probs_here[head].wait()
        low = head * head_size
        keys = qkv_ref[:, width + low : width + low + head_size]
        values = qkv_ref[:, 2 * width + low : 2 * width + low + head_size]
        d_keys = jnp.zeros((head_size, length), jnp.float32)
        d_values = jnp.zeros((head_size, length), jnp.float32)
        for block in range(blocks):
            rows = slice(block * lanes, (block + 1) * lanes)
            first = (blocks - 1 - block) * lanes
            queries = qkv_ref[rows, low : low + head_size]
            grad = grad_ref[rows, low : low + head_size]
            probs = probs_ref[head, rows, :]
            product = grad.astype(jnp.float32) * attention_ref[rows, low : low + head_size]
            delta = jnp.sum(product, axis=1, keepdims=True)
            delta_ref[rows, head : head + 1] = delta
            d_scores = probs.astype(jnp.float32) * (contract(grad, values, 1, 1) - delta)
            sums[:, first : first + length] += d_scores
            d_scores = d_scores.astype(jnp.bfloat16)
            d_query = contract(d_scores, keys, 1, 0).astype(jnp.bfloat16)
            out_ref[rows, low : low + head_size] = d_query * jnp.asarray(query_scale, jnp.bfloat16)
            d_keys = d_keys + contract(queries, d_scores, 0, 0)
            d_values = d_values + contract(grad, probs, 0, 0)
        out_ref[:, width + low : width + low + head_size] = d_keys.T.astype(jnp.bfloat16)
        out_ref[:, 2 * width + low : 2 * width + low + head_size] = d_values.T.astype(jnp.bfloat16)
        row_ids = lax.broadcasted_iota(jnp.int32, (lanes, lanes), 0)
        col_ids = lax.broadcasted_iota(jnp.int32, (lanes, lanes), 1)
        reverse = (row_ids + col_ids == lanes - 1).astype(jnp.bfloat16)
        high = sums[...].astype(jnp.bfloat16)
        rest = (sums[...] - high.astype(jnp.float32)).astype(jnp.bfloat16)
        flipped = contract(reverse, high, 1, 0) + contract(reverse, rest, 1, 0)
        for step in range(2 * blocks - 1):
            window = flipped[:, step * lanes : (step + 1) * lanes]
            window = jnp.concatenate([window, jnp.zeros_like(window)], axis=1)
            window = pltpu.roll(window, 1, 1, stride=1, stride_axis=0)
            diagonal_ref[head : head + 1, step * lanes : (step + 2) * lanes] += jnp.sum(
                window, axis=0, keepdims=True
            )
    wait_all(rest_here)
    d_normed_ref[...] = contract(out_ref[...], w_ref[...], 1, 1).astype(jnp.bfloat16)
    leaving = copies.start(d_normed_ref, d_normed_out)
    for block in range(normed_ref.shape[1] // lanes):
        cols = slice(block * lanes, (block + 1) * lanes)
        grad = contract(normed_ref[:, cols], out_ref[...], 0, 0)
        gain_ref[cols, :] = jnp.sum(grad * w_ref[cols, :].astype(jnp.float32), axis=1, keepdims=True)
        w_grad[cols, :] = grad.astype(jnp.bfloat16)
    size = send_ref.shape[1]
    for indices, to_ref in zip(block_indices(place_ref), (send_ref, keep_ref)):
        for slot, index in enumerate(indices):
            to_ref[slot] = w_grad[pl.ds(pl.multiple_of(index * size, size), size), :]
    leaving.wait()


def by_heads(
    tokens,
    lengths,
    distance_bucket,
    w_qkv,
    w_out,
    w_fc1,
    w_fc2,
    gain_in,
    gain_attn,
    gain_ffn_in,
    gain_hidden,
    head_scale,
    bias_table,
    cotangent,
):
    here, line_size = lax.axis_index("blk"), lax.axis_size("blk")
    rows_here, width = tokens.shape[1], tokens.shape[2]
    row_len = rows_here * line_size
    all_heads = head_scale.shape[0]
    head_size = width // all_heads
    heads = all_heads // line_size
    part = heads * head_size
    reach = distance_bucket.shape[0] // 2
    bucket_count = bias_table.shape[0]
    shard_rows = w_qkv.shape[0]

    low, wide = jnp.bfloat16, jnp.float32
    planes = lax.axis_size("dp")
    place_here = jnp.stack([lax.axis_index("dp"), here]).astype(jnp.int32)
    ends = jnp.cumsum(lengths[0])
    positions = jnp.arange(row_len, dtype=jnp.int32)
    documents = jnp.sum((positions[:, None] >= ends[None, :]).astype(jnp.int32), axis=1)
    if row_len <= reach:
        buckets = distance_bucket[reach - row_len : reach + row_len]
    else:
        buckets = jnp.pad(distance_bucket, row_len - reach, mode="edge")[: 2 * row_len]
    selector = (buckets[None, :] == jnp.arange(bucket_count, dtype=jnp.int32)[:, None]).astype(jnp.float32)
    head_table = lax.dynamic_slice_in_dim(bias_table.T, here * heads, heads, 0)
    diagonals = jnp.dot(head_table, selector, precision=highest)
    scale_cols = jnp.repeat(head_scale, head_size)
    head_cols = lax.dynamic_slice_in_dim(scale_cols, here * part, part, 0)[None, :]

    (bias,) = run_kernel(
        functools.partial(bias_kernel, heads),
        "relative_bias",
        2,
        place_here,
        (diagonals,),
        (),
        [((heads, lanes, 2 * row_len - lanes), wide)],
        (),
    )

    hidden_width = w_fc1.shape[1]
    summed = hidden_width + width
    by_head = w_qkv.reshape(shard_rows, 3, line_size, part).transpose(2, 0, 1, 3)
    by_head = by_head.reshape(line_size, shard_rows, 3 * part)
    shared = jnp.broadcast_to(
        jnp.concatenate([w_fc1, w_out], axis=1)[None], (line_size, shard_rows, summed)
    )
    first_pieces = deal_line(jnp.concatenate([shared, by_head], axis=2))
    first_line = after(in_line(first_pieces), bias)
    row_tokens = lax.all_gather(after(tokens[0], first_line), "blk", axis=0, tiled=True)
    second_pieces = turns(after(w_fc2, first_line))
    first_planes = across_plane(all_after(beside(first_line), *second_pieces[1:]))
    first_others = swap_cores(first_planes[:3] + [after(first_planes[3], row_tokens)])
    second_near = beside(after(in_line(second_pieces), *first_planes))

    wqkv_part, qkv, normed_row, attention, scaled_part, probs = run_kernel(
        functools.partial(attend_kernel, heads, head_size),
        "attend",
        13,
        place_here,
        (gain_in[None], documents[:, None], documents[None, :], head_cols, row_tokens),
        (*first_planes, *first_others, bias),
        [
            ((width, 3 * part), low),
            ((row_len, 3 * part), low),
            ((row_len, width), low),
            ((row_len, part), wide),
            ((row_len, part), low),
        ],
        [((heads, row_len, row_len), low)],
        [((heads, lanes, 2 * row_len - lanes), wide), ((heads, row_len, row_len), low)],
        9 + heads,
    )

    dealt = deal_line(scaled_part.reshape(line_size, rows_here, part))
    second_halves = across_halves(all_after(second_near, scaled_part))
    dealt[0] = after(dealt[0], *second_halves)
    second_planes = second_near + [jnp.concatenate(second_halves, axis=0)]
    second_others = swap_cores(all_after(second_planes, *dealt[1:]))
    grad_in = cotangent[0]
    gains = (gain_attn[None], gain_ffn_in[None], gain_hidden[None])
    block_rows, hidden_rows = width // planes, hidden_width // planes
    *kept, activated, hidden, below, across_fc2, send_fc2, keep_fc2 = run_kernel(
        functools.partial(forward_kernel, line_size),
        "feed_forward",
        9,
        place_here,
        (*dealt, tokens[0], *gains, grad_in),
        (*first_planes, *first_others),
        [
            ((rows_here, width), wide),
            ((rows_here, width), wide),
            ((rows_here, width), low),
            ((rows_here, 1), wide),
            ((rows_here, 1), wide),
            ((rows_here, hidden_width), low),
        ],
        [
            ((rows_here, hidden_width), wide),
            ((rows_here, hidden_width), wide),
            ((hidden_rows, width), low),
            ((3, hidden_rows, width), low),
            ((4, hidden_rows, width), low),
        ],
        [
            ((width, width), low),
            ((width, hidden_width), low),
            ((rows_here, hidden_width), wide),
            ((rows_here, hidden_width), wide),
            ((8, hidden_rows, width), low),
        ],
        24 + 2 * (hidden_width // tile_cols),
    )
    across_fc2, send_fc2 = all_after([across_fc2, send_fc2], *second_others)
    second_across = add_low(keep_fc2[0], swap(across_fc2, core_bit))
    halves = halves_across(second_across)
    second_rest = add_low(keep_fc2[1:], swap(send_fc2, core_bit))
    (
        mixed,
        d_middle,
        grad_gain_hidden,
        grad_gain_ffn_in,
        grad_gain_attn,
        *grad_pieces,
        send_first,
        keep_first,
    ) = run_kernel(
        functools.partial(backward_kernel, line_size),
        "feed_forward_back",
        13,
        place_here,
        (
            *dealt,
            after(grad_in, second_across),
            *kept,
            *gains,
            scale_cols.reshape(line_size, part),
        ),
        (*first_planes, *first_others, *second_planes, *second_others, hidden, below, activated),
        [
            ((rows_here, width), low),
            ((rows_here, width), wide),
            ((1, hidden_width), wide),
            ((1, width), wide),
            ((1, width), wide),
            *[((rows_here, part), low)] * line_size,
        ],
        [((4, block_rows, summed), low), ((4, block_rows, summed), low)],
        [
            ((width, width), low),
            ((width, hidden_width), low),
            ((hidden_width, width), low),
            ((rows_here, hidden_width), wide),
            ((rows_here, hidden_width), wide),
            ((rows_here, hidden_width), low),
            ((rows_here, hidden_width), wide),
            ((width, hidden_width), low),
            ((width, width), low),
        ],
        3 + 24 + 16,
    )

    grad_pieces = all_after(grad_pieces, *halves)
    grad_pieces = grad_pieces[:1] + [
        turn(piece, line_size - steps) for steps, piece in enumerate(grad_pieces[1:], 1)
    ]
    got_first = swap(after(send_first, *halves), core_bit)
    first = add_low(keep_first, got_first)
    grad_pieces[0] = after(grad_pieces[0], first)
    second_x, second_y = add_across(halves, second_rest[0], second_rest[1])
    second_got = [swap(second_x, x_bit), swap(second_y, y_bit)]
    send_qkv, keep_qkv, diagonal_sums_here, deltas, gain_sums, d_normed = run_kernel(
        functools.partial(attend_back_kernel, heads, head_size, line_size),
        "attend_back",
        12,
        place_here,
        (*grad_pieces, qkv, attention),
        (probs, normed_row, wqkv_part),
        [
            ((4, block_rows, 3 * part), low),
            ((4, block_rows, 3 * part), low),
            ((heads, 2 * row_len), wide),
            ((row_len, heads), wide),
            ((width, 1), wide),
        ],
        [((row_len, width), low)],
        [
            ((row_len, part), low),
            ((row_len, 3 * part), low),
            ((width, 3 * part), low),
            ((lanes, 2 * row_len - lanes), wide),
            ((heads, row_len, row_len), low),
            ((row_len, width), low),
            ((width, 3 * part), low),
            ((row_len, width), low),
        ],
        heads + 3,
    )
    d_normed_low = lax.psum_scatter(d_normed, "blk", scatter_dimension=0, tiled=True)
    d_normed_here = d_normed_low.astype(jnp.float32)

    second_got = all_after(second_got, d_normed)
    second_line = sum_parts([second_rest[2], *second_got]).astype(low)
    grad_gain_in = gain_sums[:, 0] / gain_in
    d_table = lax.dot_general(
        diagonal_sums_here, selector, (((1,), (1,)), ((), ())), precision=highest
    )
    small = (gain_sums[:, 0], grad_gain_attn[0], grad_gain_ffn_in[0], grad_gain_hidden[0])
    own_small = (jnp.sum(deltas, axis=0), d_table)
    sizes = [math.prod(value.shape) for value in small]
    flat = jnp.concatenate([value.reshape(-1) for value in small + own_small])
    tail_cols, pack_cols = 3 * part, summed + 3 * part
    flat = jnp.pad(flat, (0, -flat.shape[0] % tail_cols)).reshape(-1, tail_cols)
    terms = flat.astype(low)
    got = swap(send_qkv, core_bit)
    halves = halves_across(after(first[0], second_line, got))
    last = add_low(keep_qkv, got)
    terms = add_low(terms, swap(terms, core_bit))
    last_got = [
        swap(jnp.concatenate([last[slot], terms], axis=0), bits) for slot, bits in enumerate(far_first[:3])
    ]
    arrived = all_after([*halves, *last_got])
    halves, last_got = arrived[:2], arrived[2:]
    first_x, first_y = add_across(halves, first[1], first[2])
    first_got = [swap(first_x, x_bit), swap(first_y, y_bit)]
    last_line = sum_parts([last[3]] + [piece[:block_rows] for piece in last_got]).astype(low)
    plane_sums = [piece[block_rows:].astype(wide) for piece in last_got]
    flat = (terms.astype(wide) + plane_sums[1]) + (plane_sums[2] + plane_sums[0])
    flat = flat.reshape(-1)
    flat = jnp.pad(flat, (0, -flat.shape[0] % (2 * width))).reshape(-1, width).astype(low)

    second_rows = hidden_rows // line_size
    spread = jnp.broadcast_to(flat[None], (line_size,) + flat.shape)
    second_stack = jnp.concatenate([second_line.reshape(line_size, second_rows, width), spread], axis=1)
    second_dealt = deal_line(after(second_stack, d_normed_low, *last_got))
    first_line = sum_parts([first[3], *all_after(first_got, *second_dealt[1:])]).astype(low)
    both_lines = after(jnp.concatenate([first_line, last_line], axis=1), *second_dealt[1:])
    dealt_back = deal_line(both_lines.reshape(line_size, shard_rows, pack_cols))
    grad_fc2 = sum_parts([piece[:second_rows] for piece in second_dealt])
    flats = [
        piece[second_rows:].astype(wide).reshape(-1) for piece in all_after(second_dealt, dealt_back[1])
    ]
    common = sum(sizes)
    totals = [flat[:common] for flat in flats]
    while len(totals) > 1:
        half = len(totals) // 2
        totals = [totals[step] + totals[step + half] for step in range(half)]
    owned = common + heads + heads * bucket_count
    by_owner = in_line([flat[None, common:owned] for flat in flats])
    grad_scale = by_owner[:, :heads].reshape(-1)
    d_bias = by_owner[:, heads:].reshape(all_heads, bucket_count)

    grad_fc1 = sum_parts([piece[:, :hidden_width] for piece in dealt_back])
    grad_out = sum_parts([piece[:, hidden_width:summed] for piece in dealt_back])
    grad_qkv = in_line([piece[:, summed:].astype(jnp.float32) for piece in dealt_back])
    grad_qkv = grad_qkv.reshape(line_size, shard_rows, 3, part).transpose(1, 2, 0, 3)
    grad_qkv = grad_qkv.reshape(shard_rows, 3 * width)

    _, norm_in_back = jax.vjp(lambda value: layer_norm(value, gain_in), tokens[0].astype(jnp.float32))
    (d_input_part,) = norm_in_back(d_normed_here)
    grad_tokens = (d_middle + d_input_part).astype(jnp.bfloat16)[None]

    sums, begin = [], 0
    for size in sizes:
        sums.append(totals[0][begin : begin + size])
        begin += size
    return (
        mixed[None],
        grad_tokens,
        grad_qkv,
        grad_out,
        grad_fc1,
        grad_fc2,
        sums[0] / gain_in,
        sums[1],
        sums[2],
        sums[3],
        grad_scale / head_scale,
        d_bias.T,
    )


def on_device(dp_size, line_size, tokens, *rest):
    head_scale, row_len = rest[10], tokens.shape[1] * line_size
    whole_heads = head_scale.shape[0] % line_size == 0 and dp_size % line_size == 0
    if dp_size == 8 and line_size == 4 and whole_heads and row_len % lanes == 0:
        return by_heads(tokens, *rest)
    return by_sequence(tokens, *rest)


def solution(mesh):
    return jax.shard_map(
        functools.partial(on_device, mesh.shape["dp"], mesh.shape["blk"]),
        mesh=mesh,
        in_specs=(
            P("dp", "blk", None),
            P("dp", None),
            P(),
            P(("dp", "blk"), None),
            P(("dp", "blk"), None),
            P(("dp", "blk"), None),
            P(("dp", "blk"), None),
            P(),
            P(),
            P(),
            P(),
            P(),
            P(),
            P("dp", "blk", None),
        ),
        out_specs=(
            P("dp", "blk", None),
            P("dp", "blk", None),
            P(("dp", "blk"), None),
            P(("dp", "blk"), None),
            P(("dp", "blk"), None),
            P(("dp", "blk"), None),
            P(),
            P(),
            P(),
            P(),
            P(),
            P(),
        ),
        check_vma=False,
    )
```

```python
import functools
import math

import jax
import jax.numpy as jnp
from jax import lax
from jax.experimental import pallas as pl
from jax.experimental.pallas import tpu as pltpu
from jax.sharding import PartitionSpec as P

epsilon = 1e-05
masked_score = -1e30
query_scale = 0.125
highest = lax.Precision.HIGHEST


def layer_norm(value, gain):
    center = value - jnp.mean(value, axis=-1, keepdims=True)
    spread = jnp.mean(center * center, axis=-1, keepdims=True)
    return center * lax.rsqrt(spread + epsilon) * gain


def hidden_norm(value, gain):
    return layer_norm(jax.nn.gelu(value, approximate=False), gain)


def column_product(left, right):
    return lax.dot_general(
        left, right, (((0,), (0,)), ((), ())), preferred_element_type=jnp.float32
    )


def times_transpose(left, matrix):
    return lax.dot_general(
        left, matrix, (((1,), (1,)), ((), ())), preferred_element_type=jnp.float32
    )


def toeplitz(diagonals, rows, cols):
    heads = diagonals.shape[0]
    padded = jnp.pad(diagonals, ((0, 0), (0, 1)))
    stride = rows + cols - 1
    tiled = jnp.tile(padded, (1, rows))[:, : rows * stride].reshape(heads, rows, stride)
    return tiled[:, :, rows - 1 : rows - 1 + cols]


def diagonal_sums(grid):
    heads, rows, cols = grid.shape
    flipped = grid[:, ::-1, :]
    padded = jnp.pad(flipped, ((0, 0), (0, 0), (0, rows)))
    skewed = padded.reshape(heads, -1)[:, : rows * (rows + cols - 1)].reshape(
        heads, rows, rows + cols - 1
    )
    return jnp.sum(skewed, axis=1)


def by_sequence(
    tokens,
    lengths,
    distance_bucket,
    w_qkv,
    w_out,
    w_fc1,
    w_fc2,
    gain_in,
    gain_attn,
    gain_ffn_in,
    gain_hidden,
    head_scale,
    bias_table,
    cotangent,
):
    rows_here = tokens.shape[1]
    width = tokens.shape[2]
    heads = head_scale.shape[0]
    head_size = width // heads
    reach = distance_bucket.shape[0] // 2
    bucket_count = bias_table.shape[0]
    row_len = rows_here * lax.axis_size("blk")
    key_block = math.gcd(row_len, 512)
    block_count = row_len // key_block
    query_anchor = lax.axis_index("blk") * rows_here
    positions = query_anchor + jnp.arange(rows_here, dtype=jnp.int32)
    ends = jnp.cumsum(lengths[0])
    bucket_ids = jnp.arange(bucket_count, dtype=jnp.int32)

    def document_of(where):
        return jnp.sum((where[:, None] >= ends[None, :]).astype(jnp.int32), axis=1)

    query_docs = document_of(positions)

    def bucket_index(query_start, rows, key_start, cols):
        steps = jnp.arange(rows + cols - 1, dtype=jnp.int32)
        relative = key_start - query_start - (rows - 1) + steps
        return jnp.take(distance_bucket, jnp.clip(relative, -reach, reach) + reach)

    def scores_for(query_heads, query_start, query_doc, key_heads, key_start, key_doc):
        rows = query_heads.shape[0]
        cols = key_heads.shape[0]
        raw = jnp.einsum("qhd,khd->hqk", query_heads, key_heads, preferred_element_type=jnp.float32)
        buckets = bucket_index(query_start, rows, key_start, cols)
        diagonals = jnp.take(bias_table, buckets, axis=0).T
        same = query_doc[:, None] == key_doc[None, :]
        full = raw + toeplitz(diagonals, rows, cols)
        return (jnp.where(same[None], full, masked_score), same, buckets)

    residual_in = tokens[0].astype(jnp.float32)
    wqkv_all, wout_all = (
        lax.all_gather(w_qkv, ("dp", "blk"), axis=0, tiled=True),
        lax.all_gather(w_out, ("dp", "blk"), axis=0, tiled=True),
    )
    normed_f, norm_in_back = jax.vjp(layer_norm, residual_in, gain_in)
    normed_in = normed_f.astype(jnp.bfloat16)
    projected = jnp.dot(normed_in, wqkv_all, preferred_element_type=jnp.float32)
    queries = (projected[:, :width] * query_scale).astype(jnp.bfloat16)
    keys_here = projected[:, width : 2 * width].astype(jnp.bfloat16)
    values_here = projected[:, 2 * width :].astype(jnp.bfloat16)
    query_heads = queries.reshape(rows_here, heads, head_size)
    best = jnp.full((heads, rows_here), masked_score, jnp.float32)
    key_piece = lax.all_gather(keys_here, "blk", axis=0, tiled=True)
    value_piece = lax.all_gather(values_here, "blk", axis=0, tiled=True)
    length = key_piece.shape[0]
    key_pos = jnp.arange(length, dtype=jnp.int32)
    scores, same, buckets = scores_for(
        query_heads,
        query_anchor,
        query_docs,
        key_piece.reshape(length, heads, head_size),
        jnp.int32(0),
        document_of(key_pos),
    )
    new_best = jnp.maximum(best, jnp.max(scores, axis=-1))
    weights = jnp.where(same[None], jnp.exp(scores - new_best[..., None]), 0.0)
    total = jnp.sum(weights, axis=-1)
    accum = jnp.einsum(
        "hqk,khd->hqd",
        weights.astype(jnp.bfloat16),
        value_piece.reshape(length, heads, head_size),
        preferred_element_type=jnp.float32,
    )
    best, total, accum = (new_best, total, accum)
    log_total = best + jnp.log(total)
    attention = jnp.transpose(accum / total[..., None], (1, 0, 2)).reshape(rows_here, width)
    scale_cols = jnp.repeat(head_scale, head_size)
    scaled = (attention * scale_cols).astype(jnp.bfloat16)
    attn_out = jnp.dot(scaled, wout_all, preferred_element_type=jnp.float32)
    normed_attn, norm_attn_back = jax.vjp(layer_norm, attn_out, gain_attn)
    middle = residual_in + normed_attn
    fc1_all, fc2_all = (
        lax.all_gather(w_fc1, ("dp", "blk"), axis=0, tiled=True),
        lax.all_gather(w_fc2, ("dp", "blk"), axis=0, tiled=True),
    )
    normed_mid_f, norm_mid_back = jax.vjp(layer_norm, middle, gain_ffn_in)
    normed_mid = normed_mid_f.astype(jnp.bfloat16)
    hidden = jnp.dot(normed_mid, fc1_all, preferred_element_type=jnp.float32)
    activated_f, hidden_back = jax.vjp(hidden_norm, hidden, gain_hidden)
    activated = activated_f.astype(jnp.bfloat16)
    mixed = (middle + jnp.dot(activated, fc2_all, preferred_element_type=jnp.float32)).astype(
        jnp.bfloat16
    )
    grad_in = cotangent[0]
    fc1_back, fc2_back = (
        lax.all_gather(w_fc1, ("dp", "blk"), axis=0, tiled=True),
        lax.all_gather(w_fc2, ("dp", "blk"), axis=0, tiled=True),
    )
    grad_fc2 = lax.psum_scatter(
        column_product(activated, grad_in), ("dp", "blk"), scatter_dimension=0, tiled=True
    )
    d_activated = times_transpose(grad_in, fc2_back)
    d_hidden_f, grad_gain_hidden = hidden_back(d_activated)
    d_hidden = d_hidden_f.astype(jnp.bfloat16)
    grad_fc1 = lax.psum_scatter(
        column_product(normed_mid, d_hidden), ("dp", "blk"), scatter_dimension=0, tiled=True
    )
    d_mid_part, grad_gain_ffn_in = norm_mid_back(times_transpose(d_hidden, fc1_back))
    d_middle = grad_in.astype(jnp.float32) + d_mid_part
    d_attn_f, grad_gain_attn = norm_attn_back(d_middle)
    d_attn_out = d_attn_f.astype(jnp.bfloat16)
    qkv_back, out_back = (
        lax.all_gather(w_qkv, ("dp", "blk"), axis=0, tiled=True),
        lax.all_gather(w_out, ("dp", "blk"), axis=0, tiled=True),
    )
    grad_out = lax.psum_scatter(
        column_product(scaled, d_attn_out), ("dp", "blk"), scatter_dimension=0, tiled=True
    )
    d_scaled = times_transpose(d_attn_out, out_back)
    grad_scale = jnp.sum((d_scaled * attention).reshape(rows_here, heads, head_size), axis=(0, 2))
    d_attention = (d_scaled * scale_cols).astype(jnp.bfloat16)
    grad_heads = d_attention.reshape(rows_here, heads, head_size)
    row_delta = jnp.sum(
        (d_attention.astype(jnp.float32) * attention).reshape(rows_here, heads, head_size), axis=2
    ).T
    keys_back, values_back = (
        lax.all_gather(keys_here, "blk", axis=0, tiled=True),
        lax.all_gather(values_here, "blk", axis=0, tiled=True),
    )

    def pair_grads(
        query_part,
        grad_part,
        total_part,
        delta_part,
        query_start,
        query_doc,
        key_part,
        value_part,
        key_start,
        key_doc,
    ):
        scores, same, buckets = scores_for(
            query_part, query_start, query_doc, key_part, key_start, key_doc
        )
        probs = jnp.where(same[None], jnp.exp(scores - total_part[..., None]), 0.0)
        d_probs = jnp.einsum(
            "qhd,khd->hqk", grad_part, value_part, preferred_element_type=jnp.float32
        )
        d_scores = probs * (d_probs - delta_part[..., None])
        return (probs.astype(jnp.bfloat16), d_scores, buckets)

    def bias_sum(d_scores, buckets):
        sums = diagonal_sums(d_scores)
        selector = (buckets[:, None] == bucket_ids[None, :]).astype(jnp.float32)
        return jnp.dot(sums, selector, precision=highest).T

    def key_slices(index):
        begin = index * key_block
        key_part = lax.dynamic_slice_in_dim(keys_back, begin, key_block, 0).reshape(
            key_block, heads, head_size
        )
        value_part = lax.dynamic_slice_in_dim(values_back, begin, key_block, 0).reshape(
            key_block, heads, head_size
        )
        return (key_part, value_part, begin)

    query_carry = (
        jnp.zeros((rows_here, heads, head_size), jnp.float32),
        jnp.zeros((bucket_count, heads), jnp.float32),
    )

    def key_step(carry, index):
        d_query, d_bias = carry
        key_part, value_part, begin = key_slices(index)
        key_doc = document_of(begin + jnp.arange(key_block, dtype=jnp.int32))
        probs_low, d_scores, buckets = pair_grads(
            query_heads,
            grad_heads,
            log_total,
            row_delta,
            query_anchor,
            query_docs,
            key_part,
            value_part,
            begin,
            key_doc,
        )
        scores_low = d_scores.astype(jnp.bfloat16)
        d_query = d_query + jnp.einsum(
            "hqk,khd->qhd", scores_low, key_part, preferred_element_type=jnp.float32
        )
        d_key = jnp.einsum(
            "hqk,qhd->khd", scores_low, query_heads, preferred_element_type=jnp.float32
        ).reshape(key_block, width)
        d_value = jnp.einsum(
            "hqk,qhd->khd", probs_low, grad_heads, preferred_element_type=jnp.float32
        ).reshape(key_block, width)
        return (
            (d_query, d_bias + bias_sum(d_scores, buckets)),
            jnp.concatenate([d_key, d_value], axis=1),
        )

    (d_query, d_bias), kv_terms = lax.scan(
        key_step, query_carry, jnp.arange(block_count, dtype=jnp.int32)
    )
    kv_grad = lax.psum_scatter(
        kv_terms.reshape(row_len, 2 * width).astype(jnp.bfloat16),
        "blk",
        scatter_dimension=0,
        tiled=True,
    )
    d_query_low = d_query.reshape(rows_here, width).astype(jnp.bfloat16)
    d_projected = jnp.concatenate(
        [d_query_low * jnp.asarray(query_scale, jnp.bfloat16), kv_grad], axis=1
    )
    grad_qkv = lax.psum_scatter(
        column_product(normed_in, d_projected), ("dp", "blk"), scatter_dimension=0, tiled=True
    )
    d_input_part, grad_gain_in = norm_in_back(times_transpose(d_projected, qkv_back))
    grad_tokens = (d_middle + d_input_part).astype(jnp.bfloat16)[None]
    small = lax.psum(
        (grad_gain_in, grad_gain_attn, grad_gain_ffn_in, grad_gain_hidden, grad_scale, d_bias),
        ("dp", "blk"),
    )
    return (
        mixed[None],
        grad_tokens,
        grad_qkv,
        grad_out,
        grad_fc1,
        grad_fc2,
        small[0],
        small[1],
        small[2],
        small[3],
        small[4],
        small[5],
    )


lanes = 128
core_bit, x_bit, y_bit = 1, 2, 4


def swap(value, bit):
    size = lax.axis_size("dp")
    return lax.ppermute(value, "dp", [(i, i ^ bit) for i in range(size)])


def turn(value, steps):
    size = lax.axis_size("blk")
    return lax.ppermute(value, "blk", [(i, (i + steps) % size) for i in range(size)])


def swap_line(value, bit):
    size = lax.axis_size("blk")
    return lax.ppermute(value, "blk", [(i, i ^ bit) for i in range(size)])


def pick(stack, index):
    return lax.dynamic_index_in_dim(stack, index, 0, keepdims=False)


def after(value, *others):
    return lax.optimization_barrier((value, *others))[0]


def all_after(values, *others):
    return list(lax.optimization_barrier((*values, *others))[: len(values)])


def turns(value):
    size = lax.axis_size("blk")
    return [value] + [turn(value, steps) for steps in range(1, size)]


def in_line(pieces):
    here, size = lax.axis_index("blk"), lax.axis_size("blk")
    ordered = [lax.select_n(lax.rem(here - owner + size, size), *pieces) for owner in range(size)]
    return jnp.concatenate(ordered, axis=0)


def deal_line(stack):
    here, size = lax.axis_index("blk"), lax.axis_size("blk")
    got = [pick(stack, here)]
    for steps in range(1, size):
        got.append(turn(pick(stack, lax.rem(here + steps, size)), steps))
    return got


def swap_cores(blocks):
    return [swap(block, core_bit) for block in blocks]


def beside(line):
    return [line, swap(line, x_bit), swap(line, y_bit)]


def across_halves(near):
    _, along_x, along_y = near
    half = along_x.shape[0] // 2
    return [swap(along_y[:half], x_bit), swap(along_x[half:], y_bit)]


def across_plane(near):
    return near + [jnp.concatenate(across_halves(near), axis=0)]


def add_low(left, right):
    return (left.astype(jnp.float32) + right.astype(jnp.float32)).astype(jnp.bfloat16)


def halves_across(across):
    half = across.shape[0] // 2
    return [swap(across[:half], x_bit), swap(across[half:], y_bit)]


def add_across(halves, to_x, to_y):
    from_x, from_y = halves
    half = from_x.shape[0]
    to_y = jnp.concatenate([add_low(to_y[:half], from_x), to_y[half:]], axis=0)
    to_x = jnp.concatenate([to_x[:half], add_low(to_x[half:], from_y)], axis=0)
    return to_x, to_y


def add_planes(to_x, to_y, own):
    got_x, got_y = swap(to_x, x_bit), swap(to_y, y_bit)
    total = own.astype(jnp.float32) + got_x.astype(jnp.float32) + got_y.astype(jnp.float32)
    return total.astype(jnp.bfloat16)


def sum_parts(parts):
    total = parts[0].astype(jnp.float32)
    for part in parts[1:]:
        total = total + part.astype(jnp.float32)
    return total


def add_line(line):
    size = lax.axis_size("blk")
    return sum_parts(deal_line(line.reshape((size, -1) + line.shape[1:])))


def contract(left, right, left_axis, right_axis):
    return lax.dot_general(
        left, right, (((left_axis,), (right_axis,)), ((), ())), preferred_element_type=jnp.float32
    )


tile_cols = 256
far_first = (x_bit | y_bit, x_bit, y_bit, 0)


def run_kernel(kernel, name, micros, place_here, operands, far, outputs, far_outputs, scratch=(), copies=1):
    near_spec, far_spec = pl.BlockSpec(memory_space=pltpu.VMEM), pl.BlockSpec(memory_space=pl.ANY)
    return pl.pallas_call(
        kernel,
        out_shape=[jax.ShapeDtypeStruct(shape, dtype) for shape, dtype in (*outputs, *far_outputs)],
        in_specs=[pl.BlockSpec(memory_space=pltpu.SMEM)] + [near_spec] * len(operands) + [far_spec] * len(far),
        out_specs=[near_spec] * len(outputs) + [far_spec] * len(far_outputs),
        scratch_shapes=[pltpu.VMEM(shape, dtype) for shape, dtype in scratch]
        + [pltpu.SemaphoreType.DMA((copies,))],
        compiler_params=pltpu.CompilerParams(vmem_limit_bytes=52 * 2**20),
        cost_estimate=pl.CostEstimate(
            flops=int(micros * 1.1e9), bytes_accessed=int(micros * 3.6e6), transcendentals=0
        ),
        name=name,
    )(place_here, *operands, *far)


class Copies:
    def __init__(self, semaphores):
        self.semaphores, self.used = semaphores, 0

    def start(self, source, target):
        copy = pltpu.make_async_copy(source, target, self.semaphores.at[self.used])
        self.used += 1
        copy.start()
        return copy


def wait_all(copies):
    for copy in copies:
        copy.wait()


def normalize(value):
    center = value - jnp.mean(value, axis=-1, keepdims=True)
    spread = jnp.mean(center * center, axis=-1, keepdims=True)
    scale = lax.rsqrt(spread + epsilon)
    return center * scale, scale


def normalize_back(normed, scale, grad, gain):
    inner = grad * gain
    middle = jnp.mean(inner, axis=-1, keepdims=True)
    along = jnp.mean(inner * normed, axis=-1, keepdims=True)
    return scale * (inner - middle - normed * along), jnp.sum(grad * normed, axis=0, keepdims=True)


def block_indices(place_ref):
    me = place_ref[0]
    return [me ^ bits ^ core_bit for bits in far_first], [me ^ bits for bits in far_first]


near_first = (0, x_bit, y_bit, x_bit | y_bit)


def fill_planes(copies, place_ref, blocks, cols, out_ref):
    bits = near_first + tuple(bit | core_bit for bit in near_first)
    started = []
    for bit, block in zip(bits, blocks):
        rows = block.shape[0]
        begin = pl.multiple_of((place_ref[0] ^ bit) * rows, rows)
        started.append(copies.start(block.at[:, cols], out_ref.at[pl.ds(begin, rows), :]))
    return started


def before(place_ref, steps, size):
    return lax.rem(place_ref[1] - steps + size, size)


def bias_kernel(heads, place_ref, diagonal_ref, bias_ref, semaphores):
    for head in range(heads):
        for step in range(diagonal_ref.shape[1] // lanes - 1):
            window = diagonal_ref[head : head + 1, step * lanes : (step + 2) * lanes]
            window = jnp.broadcast_to(window, (lanes, 2 * lanes))
            window = pltpu.roll(window, 0, 1, stride=1, stride_axis=0)
            bias_ref[head, :, step * lanes : (step + 1) * lanes] = window[:, lanes:]


def attend_kernel(
    heads, head_size, place_ref, gain_ref, doc_col_ref, doc_row_ref, scale_ref, tokens_ref, *refs
):
    parts, refs = refs[:8], refs[8:]
    bias_in, w_ref, qkv_ref, normed_ref, attention_ref, scaled_ref, probs_out, bias, probs_ref, semaphores = refs
    copies = Copies(semaphores)
    last = parts[0].shape[1]
    arriving = fill_planes(copies, place_ref, parts, slice(last - w_ref.shape[1], last), w_ref)
    bias_here = copies.start(bias_in, bias)
    leaving = []
    length = tokens_ref.shape[0]
    blocks = length // lanes
    width = heads * head_size
    for block in range(blocks):
        rows = slice(block * lanes, (block + 1) * lanes)
        normed, _ = normalize(tokens_ref[rows, :].astype(jnp.float32))
        normed_ref[rows, :] = (normed * gain_ref[...]).astype(jnp.bfloat16)
    wait_all(arriving)
    bias_here.wait()
    projected = contract(normed_ref[...], w_ref[...], 1, 0)
    qkv_ref[:, :width] = (projected[:, :width] * query_scale).astype(jnp.bfloat16)
    qkv_ref[:, width:] = projected[:, width:].astype(jnp.bfloat16)
    for head in range(heads):
        low = head * head_size
        keys = qkv_ref[:, width + low : width + low + head_size]
        values = qkv_ref[:, 2 * width + low : 2 * width + low + head_size]
        all_scores = contract(qkv_ref[:, low : low + head_size], keys, 1, 1)
        for block in range(blocks):
            rows = slice(block * lanes, (block + 1) * lanes)
            first = (blocks - 1 - block) * lanes
            scores = all_scores[rows, :] + bias[head, :, first : first + length]
            same = doc_col_ref[rows, :] == doc_row_ref[...]
            scores = jnp.where(same, scores, masked_score)
            weights = jnp.exp(scores - jnp.max(scores, axis=1, keepdims=True))
            probs = weights * (1.0 / jnp.sum(weights, axis=1, keepdims=True))
            probs = probs.astype(jnp.bfloat16)
            probs_ref[head, rows, :] = probs
        leaving.append(copies.start(probs_ref.at[head], probs_out.at[head]))
        attention_ref[:, low : low + head_size] = contract(probs_ref[head], values, 1, 0)
    scaled_ref[...] = (attention_ref[...] * scale_ref[...]).astype(jnp.bfloat16)
    wait_all(leaving)


def forward_kernel(line, place_ref, *refs):
    pieces, refs = refs[:line], refs[line:]
    tokens_ref, gain_attn_ref, gain_mid_ref, gain_hidden_ref, cotangent_ref, *refs = refs
    blocks, refs = refs[:8], refs[8:]
    (attn_ref, middle_ref, normed_ref, mean_ref, scale_ref, activated_ref,
     hidden_out, across_out, send_out, keep_out,
     wout_ref, fc1_ref, hidden_ref, below_ref, grads_ref, semaphores) = refs
    copies = Copies(semaphores)
    part = pieces[0].shape[1]
    hidden_width, width = fc1_ref.shape[1], wout_ref.shape[1]
    wout_here = fill_planes(copies, place_ref, blocks, slice(hidden_width, hidden_width + width), wout_ref)
    fc1_here = fill_planes(copies, place_ref, blocks, slice(0, hidden_width), fc1_ref)
    leaving = []
    wait_all(wout_here)
    attn = jnp.zeros(attn_ref.shape, jnp.float32)
    for steps in range(line):
        rows = pl.ds(pl.multiple_of(before(place_ref, steps, line) * part, part), part)
        attn = attn + contract(pieces[steps][...], wout_ref[rows, :], 1, 0)
    attn_ref[...] = attn
    normed, _ = normalize(attn)
    middle = tokens_ref[...].astype(jnp.float32) + normed * gain_attn_ref[...]
    middle_ref[...] = middle
    normed, _ = normalize(middle)
    normed = (normed * gain_mid_ref[...]).astype(jnp.bfloat16)
    normed_ref[...] = normed
    tiles = [slice(begin, begin + tile_cols) for begin in range(0, hidden_width, tile_cols)]
    total = jnp.zeros(mean_ref.shape, jnp.float32)
    wait_all(fc1_here)
    for cols in tiles:
        hidden = contract(normed, fc1_ref[:, cols], 1, 0)
        below = 0.5 * (1.0 + lax.erf(hidden * (0.5**0.5)))
        hidden_ref[:, cols] = hidden
        below_ref[:, cols] = below
        leaving.append(copies.start(hidden_ref.at[:, cols], hidden_out.at[:, cols]))
        total = total + jnp.sum(hidden * below, axis=1, keepdims=True)
    mean = total / hidden_width
    total = jnp.zeros(mean_ref.shape, jnp.float32)
    for cols in tiles:
        center = hidden_ref[:, cols] * below_ref[:, cols] - mean
        total = total + jnp.sum(center * center, axis=1, keepdims=True)
    scale = lax.rsqrt(total / hidden_width + epsilon)
    mean_ref[...] = mean
    scale_ref[...] = scale
    for cols in tiles:
        center = hidden_ref[:, cols] * below_ref[:, cols] - mean
        activated_ref[:, cols] = (center * scale * gain_hidden_ref[:, cols]).astype(jnp.bfloat16)
    size = grads_ref.shape[1]
    sent, kept = block_indices(place_ref)
    outs = [across_out] + [send_out.at[slot] for slot in range(3)] + [keep_out.at[slot] for slot in range(4)]
    for slot, (index, out) in enumerate(zip(sent + kept, outs)):
        cols = pl.ds(pl.multiple_of(index * size, lanes), size)
        grads_ref[slot] = contract(activated_ref[:, cols], cotangent_ref[...], 0, 0).astype(jnp.bfloat16)
        leaving.append(copies.start(grads_ref.at[slot], out))
    wait_all(leaving)


def backward_kernel(line, place_ref, *refs):
    pieces, refs = refs[:line], refs[line:]
    (cotangent_ref, attn_ref, middle_ref, normed_ref, mean_ref, scale_ref, gain_attn_ref, gain_mid_ref,
     gain_hidden_ref, head_scale_ref, *refs) = refs
    first_blocks, second_blocks, refs = refs[:8], refs[8:16], refs[16:]
    hidden_in, activated_in, *refs = refs
    mixed_ref, d_middle_ref, d_hidden_gain_ref, d_mid_gain_ref, d_attn_gain_ref, *refs = refs
    grads, refs = refs[:line], refs[line:]
    (send_out, keep_out, wout_ref, fc1_ref, fc2_ref, hidden_ref, below_ref, activated_ref, inner_ref, fc1_grad,
     out_grad, semaphores) = refs
    copies = Copies(semaphores)
    part = pieces[0].shape[1]
    hidden_width, width = fc1_ref.shape[1], wout_ref.shape[1]
    fc2_here, hidden_here = [], []
    for bit, block in zip(near_first + tuple(bit | core_bit for bit in near_first), second_blocks):
        size = block.shape[0]
        part_here = pl.ds(pl.multiple_of((place_ref[0] ^ bit) * size, lanes), size)
        fc2_here.append(copies.start(block, fc2_ref.at[part_here, :]))
        hidden_here.append(copies.start(hidden_in.at[:, part_here], hidden_ref.at[:, part_here]))
    fc1_here = fill_planes(copies, place_ref, first_blocks, slice(0, hidden_width), fc1_ref)
    activated_here = copies.start(activated_in, activated_ref)
    wout_here = fill_planes(
        copies, place_ref, first_blocks, slice(hidden_width, hidden_width + width), wout_ref
    )
    grad_in = cotangent_ref[...]
    mean, scale = mean_ref[...], scale_ref[...]
    tiles = [slice(begin, begin + tile_cols) for begin in range(0, hidden_width, tile_cols)]
    size = hidden_width // len(fc2_here)
    bits = near_first + tuple(bit | core_bit for bit in near_first)
    total = jnp.zeros(mean.shape, jnp.float32)
    along = jnp.zeros(mean.shape, jnp.float32)
    for bit, arriving in zip(bits, zip(fc2_here, hidden_here)):
        wait_all(arriving)
        cols = pl.ds(pl.multiple_of((place_ref[0] ^ bit) * size, lanes), size)
        d_activated = contract(grad_in, fc2_ref[cols, :], 1, 1)
        hidden = hidden_ref[:, cols]
        below = 0.5 * (1.0 + lax.erf(hidden * (0.5**0.5)))
        below_ref[:, cols] = below
        normed = (hidden * below - mean) * scale
        d_hidden_gain_ref[:, cols] = jnp.sum(d_activated * normed, axis=0, keepdims=True)
        inner = d_activated * gain_hidden_ref[:, cols]
        inner_ref[:, cols] = inner
        total = total + jnp.sum(inner, axis=1, keepdims=True)
        along = along + jnp.sum(inner * normed, axis=1, keepdims=True)
    total, along = total / hidden_width, along / hidden_width
    d_normed = jnp.zeros(middle_ref.shape, jnp.float32)
    normed_mid = normed_ref[...].T
    wait_all(fc1_here)
    for cols in tiles:
        hidden, below = hidden_ref[:, cols], below_ref[:, cols]
        normed = (hidden * below - mean) * scale
        slope = below + hidden * jnp.exp(-0.5 * hidden * hidden) * (1.0 / math.sqrt(2.0 * math.pi))
        d_hidden = scale * (inner_ref[:, cols] - total - normed * along) * slope
        d_hidden = d_hidden.astype(jnp.bfloat16)
        fc1_grad[:, cols] = contract(normed_mid, d_hidden, 1, 0).astype(jnp.bfloat16)
        d_normed = d_normed + contract(d_hidden, fc1_ref[:, cols], 1, 1)
    size = send_out.shape[1]
    sent, kept = block_indices(place_ref)
    outs = [send_out.at[slot] for slot in range(4)] + [keep_out.at[slot] for slot in range(4)]
    places = [pl.ds(pl.multiple_of(index * size, size), size) for index in sent + kept]
    leaving = [
        copies.start(fc1_grad.at[rows, :], out.at[:, :hidden_width]) for rows, out in zip(places, outs)
    ]
    normed, scale = normalize(middle_ref[...])
    d_value, d_mid_gain_ref[...] = normalize_back(normed, scale, d_normed, gain_mid_ref[...])
    d_middle = grad_in.astype(jnp.float32) + d_value
    d_middle_ref[...] = d_middle
    normed, scale = normalize(attn_ref[...])
    d_value, d_attn_gain_ref[...] = normalize_back(normed, scale, d_middle, gain_attn_ref[...])
    d_attn = d_value.astype(jnp.bfloat16)
    wait_all(wout_here)
    for steps in range(line):
        owner = before(place_ref, steps, line)
        rows = pl.ds(pl.multiple_of(owner * part, part), part)
        d_scaled = contract(d_attn, wout_ref[rows, :], 1, 1)
        grads[steps][...] = (d_scaled * head_scale_ref[pl.ds(owner, 1), :]).astype(jnp.bfloat16)
        out_grad[rows, :] = contract(pieces[steps][...], d_attn, 0, 0).astype(jnp.bfloat16)
    leaving += [
        copies.start(out_grad.at[rows, :], out.at[:, hidden_width:]) for rows, out in zip(places, outs)
    ]
    activated_here.wait()
    mixed = middle_ref[...] + contract(activated_ref[...], fc2_ref[...], 1, 0)
    mixed_ref[...] = mixed.astype(jnp.bfloat16)
    wait_all(leaving)


def attend_back_kernel(heads, head_size, line, place_ref, *refs):
    pieces, refs = refs[:line], refs[line:]
    (qkv_ref, attention_ref, probs_in, normed_in, w_in,
     send_ref, keep_ref, diagonal_ref, delta_ref, gain_ref, d_normed_out,
     grad_ref, out_ref, w_grad, sums, probs_ref, normed_ref, w_ref, d_normed_ref, scores_ref, semaphores) = refs
    copies = Copies(semaphores)
    probs_here = [copies.start(probs_in.at[head], probs_ref.at[head]) for head in range(heads)]
    rest_here = [copies.start(w_in, w_ref), copies.start(normed_in, normed_ref)]
    length = qkv_ref.shape[0]
    blocks = length // lanes
    width = heads * head_size
    rows_here = pieces[0].shape[0]
    for steps in range(line):
        owner = lax.rem(place_ref[1] + steps, line)
        grad_ref[pl.ds(pl.multiple_of(owner * rows_here, rows_here), rows_here), :] = pieces[steps][...]
    diagonal_ref[...] = jnp.zeros_like(diagonal_ref)
    for head in range(heads):
        sums[...] = jnp.zeros_like(sums)
        probs_here[head].wait()
        low = head * head_size
        keys = qkv_ref[:, width + low : width + low + head_size]
        values = qkv_ref[:, 2 * width + low : 2 * width + low + head_size]
        queries = qkv_ref[:, low : low + head_size]
        grad = grad_ref[:, low : low + head_size]
        product = grad.astype(jnp.float32) * attention_ref[:, low : low + head_size]
        delta = jnp.sum(product, axis=1, keepdims=True)
        delta_ref[:, head : head + 1] = delta
        d_probs = contract(grad, values, 1, 1)
        for block in range(blocks):
            rows = slice(block * lanes, (block + 1) * lanes)
            first = (blocks - 1 - block) * lanes
            d_scores = probs_ref[head, rows, :].astype(jnp.float32) * (d_probs[rows, :] - delta[rows, :])
            sums[:, first : first + length] += d_scores
            scores_ref[rows, :] = d_scores.astype(jnp.bfloat16)
        d_scores = scores_ref[...]
        d_query = contract(d_scores, keys, 1, 0).astype(jnp.bfloat16)
        out_ref[:, low : low + head_size] = d_query * jnp.asarray(query_scale, jnp.bfloat16)
        d_keys = contract(queries, d_scores, 0, 0)
        d_values = contract(grad, probs_ref[head], 0, 0)
        out_ref[:, width + low : width + low + head_size] = d_keys.T.astype(jnp.bfloat16)
        out_ref[:, 2 * width + low : 2 * width + low + head_size] = d_values.T.astype(jnp.bfloat16)
        row_ids = lax.broadcasted_iota(jnp.int32, (lanes, lanes), 0)
        col_ids = lax.broadcasted_iota(jnp.int32, (lanes, lanes), 1)
        reverse = (row_ids + col_ids == lanes - 1).astype(jnp.bfloat16)
        high = sums[...].astype(jnp.bfloat16)
        rest = (sums[...] - high.astype(jnp.float32)).astype(jnp.bfloat16)
        flipped = contract(reverse, high, 1, 0) + contract(reverse, rest, 1, 0)
        for step in range(2 * blocks - 1):
            window = flipped[:, step * lanes : (step + 1) * lanes]
            window = jnp.concatenate([window, jnp.zeros_like(window)], axis=1)
            window = pltpu.roll(window, 1, 1, stride=1, stride_axis=0)
            diagonal_ref[head : head + 1, step * lanes : (step + 2) * lanes] += jnp.sum(
                window, axis=0, keepdims=True
            )
    wait_all(rest_here)
    d_normed_ref[...] = contract(out_ref[...], w_ref[...], 1, 1).astype(jnp.bfloat16)
    leaving = copies.start(d_normed_ref, d_normed_out)
    for block in range(normed_ref.shape[1] // lanes):
        cols = slice(block * lanes, (block + 1) * lanes)
        grad = contract(normed_ref[:, cols], out_ref[...], 0, 0)
        gain_ref[cols, :] = jnp.sum(grad * w_ref[cols, :].astype(jnp.float32), axis=1, keepdims=True)
        w_grad[cols, :] = grad.astype(jnp.bfloat16)
    size = send_ref.shape[1]
    for indices, to_ref in zip(block_indices(place_ref), (send_ref, keep_ref)):
        for slot, index in enumerate(indices):
            to_ref[slot] = w_grad[pl.ds(pl.multiple_of(index * size, size), size), :]
    leaving.wait()


def by_heads(
    tokens,
    lengths,
    distance_bucket,
    w_qkv,
    w_out,
    w_fc1,
    w_fc2,
    gain_in,
    gain_attn,
    gain_ffn_in,
    gain_hidden,
    head_scale,
    bias_table,
    cotangent,
):
    here, line_size = lax.axis_index("blk"), lax.axis_size("blk")
    rows_here, width = tokens.shape[1], tokens.shape[2]
    row_len = rows_here * line_size
    all_heads = head_scale.shape[0]
    head_size = width // all_heads
    heads = all_heads // line_size
    part = heads * head_size
    reach = distance_bucket.shape[0] // 2
    bucket_count = bias_table.shape[0]
    shard_rows = w_qkv.shape[0]

    low, wide = jnp.bfloat16, jnp.float32
    planes = lax.axis_size("dp")
    place_here = jnp.stack([lax.axis_index("dp"), here]).astype(jnp.int32)
    ends = jnp.cumsum(lengths[0])
    positions = jnp.arange(row_len, dtype=jnp.int32)
    documents = jnp.sum((positions[:, None] >= ends[None, :]).astype(jnp.int32), axis=1)
    if row_len <= reach:
        buckets = distance_bucket[reach - row_len : reach + row_len]
    else:
        buckets = jnp.pad(distance_bucket, row_len - reach, mode="edge")[: 2 * row_len]
    selector = (buckets[None, :] == jnp.arange(bucket_count, dtype=jnp.int32)[:, None]).astype(jnp.float32)
    head_table = lax.dynamic_slice_in_dim(bias_table.T, here * heads, heads, 0)
    diagonals = jnp.dot(head_table, selector, precision=highest)
    scale_cols = jnp.repeat(head_scale, head_size)
    head_cols = lax.dynamic_slice_in_dim(scale_cols, here * part, part, 0)[None, :]

    (bias,) = run_kernel(
        functools.partial(bias_kernel, heads),
        "relative_bias",
        2,
        place_here,
        (diagonals,),
        (),
        [((heads, lanes, 2 * row_len - lanes), wide)],
        (),
    )

    hidden_width = w_fc1.shape[1]
    summed = hidden_width + width
    by_head = w_qkv.reshape(shard_rows, 3, line_size, part).transpose(2, 0, 1, 3)
    by_head = by_head.reshape(line_size, shard_rows, 3 * part)
    shared = jnp.broadcast_to(
        jnp.concatenate([w_fc1, w_out], axis=1)[None], (line_size, shard_rows, summed)
    )
    first_pieces = deal_line(jnp.concatenate([shared, by_head], axis=2))
    first_line = after(in_line(first_pieces), bias)
    row_tokens = lax.all_gather(after(tokens[0], first_line), "blk", axis=0, tiled=True)
    second_pieces = turns(after(w_fc2, first_line))
    first_planes = across_plane(all_after(beside(first_line), *second_pieces[1:]))
    first_others = swap_cores(first_planes[:3] + [after(first_planes[3], row_tokens)])
    second_near = beside(after(in_line(second_pieces), *first_planes))

    wqkv_part, qkv, normed_row, attention, scaled_part, probs = run_kernel(
        functools.partial(attend_kernel, heads, head_size),
        "attend",
        13,
        place_here,
        (gain_in[None], documents[:, None], documents[None, :], head_cols, row_tokens),
        (*first_planes, *first_others, bias),
        [
            ((width, 3 * part), low),
            ((row_len, 3 * part), low),
            ((row_len, width), low),
            ((row_len, part), wide),
            ((row_len, part), low),
        ],
        [((heads, row_len, row_len), low)],
        [((heads, lanes, 2 * row_len - lanes), wide), ((heads, row_len, row_len), low)],
        9 + heads,
    )

    dealt = deal_line(scaled_part.reshape(line_size, rows_here, part))
    second_halves = across_halves(all_after(second_near, scaled_part))
    dealt[0] = after(dealt[0], *second_halves)
    second_planes = second_near + [jnp.concatenate(second_halves, axis=0)]
    second_others = swap_cores(all_after(second_planes, *dealt[1:]))
    grad_in = cotangent[0]
    gains = (gain_attn[None], gain_ffn_in[None], gain_hidden[None])
    block_rows, hidden_rows = width // planes, hidden_width // planes
    *kept, activated, hidden, across_fc2, send_fc2, keep_fc2 = run_kernel(
        functools.partial(forward_kernel, line_size),
        "feed_forward",
        9,
        place_here,
        (*dealt, tokens[0], *gains, grad_in),
        (*first_planes, *first_others),
        [
            ((rows_here, width), wide),
            ((rows_here, width), wide),
            ((rows_here, width), low),
            ((rows_here, 1), wide),
            ((rows_here, 1), wide),
            ((rows_here, hidden_width), low),
        ],
        [
            ((rows_here, hidden_width), wide),
            ((hidden_rows, width), low),
            ((3, hidden_rows, width), low),
            ((4, hidden_rows, width), low),
        ],
        [
            ((width, width), low),
            ((width, hidden_width), low),
            ((rows_here, hidden_width), wide),
            ((rows_here, hidden_width), wide),
            ((8, hidden_rows, width), low),
        ],
        24 + hidden_width // tile_cols,
    )
    across_fc2, send_fc2 = all_after([across_fc2, send_fc2], *second_others)
    second_across = add_low(keep_fc2[0], swap(across_fc2, core_bit))
    halves = halves_across(second_across)
    second_rest = add_low(keep_fc2[1:], swap(send_fc2, core_bit))
    (
        mixed,
        d_middle,
        grad_gain_hidden,
        grad_gain_ffn_in,
        grad_gain_attn,
        *grad_pieces,
        send_first,
        keep_first,
    ) = run_kernel(
        functools.partial(backward_kernel, line_size),
        "feed_forward_back",
        13,
        place_here,
        (
            *dealt,
            after(grad_in, second_across),
            *kept,
            *gains,
            scale_cols.reshape(line_size, part),
        ),
        (*first_planes, *first_others, *second_planes, *second_others, hidden, activated),
        [
            ((rows_here, width), low),
            ((rows_here, width), wide),
            ((1, hidden_width), wide),
            ((1, width), wide),
            ((1, width), wide),
            *[((rows_here, part), low)] * line_size,
        ],
        [((4, block_rows, summed), low), ((4, block_rows, summed), low)],
        [
            ((width, width), low),
            ((width, hidden_width), low),
            ((hidden_width, width), low),
            ((rows_here, hidden_width), wide),
            ((rows_here, hidden_width), wide),
            ((rows_here, hidden_width), low),
            ((rows_here, hidden_width), wide),
            ((width, hidden_width), low),
            ((width, width), low),
        ],
        1 + 32 + 16,
    )

    grad_pieces = all_after(grad_pieces, *halves)
    grad_pieces = grad_pieces[:1] + [
        turn(piece, line_size - steps) for steps, piece in enumerate(grad_pieces[1:], 1)
    ]
    got_first = swap(after(send_first, *halves), core_bit)
    first_across = add_low(keep_first[0], got_first[0])
    grad_pieces[0] = after(grad_pieces[0], got_first)
    second_x, second_y = add_across(halves, second_rest[0], second_rest[1])
    second_got = [swap(second_x, x_bit), swap(second_y, y_bit)]
    send_qkv, keep_qkv, diagonal_sums_here, deltas, gain_sums, d_normed = run_kernel(
        functools.partial(attend_back_kernel, heads, head_size, line_size),
        "attend_back",
        12,
        place_here,
        (*grad_pieces, qkv, attention),
        (probs, normed_row, wqkv_part),
        [
            ((4, block_rows, 3 * part), low),
            ((4, block_rows, 3 * part), low),
            ((heads, 2 * row_len), wide),
            ((row_len, heads), wide),
            ((width, 1), wide),
        ],
        [((row_len, width), low)],
        [
            ((row_len, part), low),
            ((row_len, 3 * part), low),
            ((width, 3 * part), low),
            ((lanes, 2 * row_len - lanes), wide),
            ((heads, row_len, row_len), low),
            ((row_len, width), low),
            ((width, 3 * part), low),
            ((row_len, width), low),
            ((row_len, row_len), low),
        ],
        heads + 3,
    )
    d_normed_low = lax.psum_scatter(d_normed, "blk", scatter_dimension=0, tiled=True)
    d_normed_here = d_normed_low.astype(jnp.float32)

    second_got = all_after(second_got, d_normed)
    grad_gain_in = gain_sums[:, 0] / gain_in
    d_table = lax.dot_general(
        diagonal_sums_here, selector, (((1,), (1,)), ((), ())), precision=highest
    )
    small = (gain_sums[:, 0], grad_gain_attn[0], grad_gain_ffn_in[0], grad_gain_hidden[0])
    own_small = (jnp.sum(deltas, axis=0), d_table)
    sizes = [math.prod(value.shape) for value in small]
    flat = jnp.concatenate([value.reshape(-1) for value in small + own_small])
    tail_cols, pack_cols = 3 * part, summed + 3 * part
    flat = jnp.pad(flat, (0, -flat.shape[0] % tail_cols)).reshape(-1, tail_cols)
    terms = flat.astype(low)
    got = swap(send_qkv, core_bit)
    halves = halves_across(after(first_across, *second_got))
    second_line = sum_parts([second_rest[2], *all_after(second_got, got)]).astype(low)
    first_rest = add_low(keep_first[1:], after(got_first[1:], got))
    last = add_low(keep_qkv, got)
    terms = add_low(terms, swap(terms, core_bit))
    last_got = [
        swap(jnp.concatenate([last[slot], terms], axis=0), bits) for slot, bits in enumerate(far_first[:3])
    ]
    arrived = all_after([*halves, *last_got])
    halves, last_got = arrived[:2], arrived[2:]
    first_x, first_y = add_across(halves, first_rest[0], first_rest[1])
    first_got = [swap(first_x, x_bit), swap(first_y, y_bit)]
    last_line = sum_parts([last[3]] + [piece[:block_rows] for piece in last_got]).astype(low)
    plane_sums = [piece[block_rows:].astype(wide) for piece in last_got]
    flat = (terms.astype(wide) + plane_sums[1]) + (plane_sums[2] + plane_sums[0])
    flat = flat.reshape(-1)
    flat = jnp.pad(flat, (0, -flat.shape[0] % (2 * width))).reshape(-1, width).astype(low)

    second_rows = hidden_rows // line_size
    spread = jnp.broadcast_to(flat[None], (line_size,) + flat.shape)
    second_stack = jnp.concatenate([second_line.reshape(line_size, second_rows, width), spread], axis=1)
    second_dealt = deal_line(after(second_stack, d_normed_low, *last_got))
    first_line = sum_parts([first_rest[2], *all_after(first_got, *second_dealt[1:])]).astype(low)
    both_lines = after(jnp.concatenate([first_line, last_line], axis=1), *second_dealt[1:])
    dealt_back = deal_line(both_lines.reshape(line_size, shard_rows, pack_cols))
    grad_fc2 = sum_parts([piece[:second_rows] for piece in second_dealt])
    flats = [
        piece[second_rows:].astype(wide).reshape(-1) for piece in all_after(second_dealt, dealt_back[1])
    ]
    common = sum(sizes)
    totals = [flat[:common] for flat in flats]
    while len(totals) > 1:
        half = len(totals) // 2
        totals = [totals[step] + totals[step + half] for step in range(half)]
    owned = common + heads + heads * bucket_count
    by_owner = in_line([flat[None, common:owned] for flat in flats])
    grad_scale = by_owner[:, :heads].reshape(-1)
    d_bias = by_owner[:, heads:].reshape(all_heads, bucket_count)

    grad_fc1 = sum_parts([piece[:, :hidden_width] for piece in dealt_back])
    grad_out = sum_parts([piece[:, hidden_width:summed] for piece in dealt_back])
    grad_qkv = in_line([piece[:, summed:].astype(jnp.float32) for piece in dealt_back])
    grad_qkv = grad_qkv.reshape(line_size, shard_rows, 3, part).transpose(1, 2, 0, 3)
    grad_qkv = grad_qkv.reshape(shard_rows, 3 * width)

    _, norm_in_back = jax.vjp(lambda value: layer_norm(value, gain_in), tokens[0].astype(jnp.float32))
    (d_input_part,) = norm_in_back(d_normed_here)
    grad_tokens = (d_middle + d_input_part).astype(jnp.bfloat16)[None]

    sums, begin = [], 0
    for size in sizes:
        sums.append(totals[0][begin : begin + size])
        begin += size
    return (
        mixed[None],
        grad_tokens,
        grad_qkv,
        grad_out,
        grad_fc1,
        grad_fc2,
        sums[0] / gain_in,
        sums[1],
        sums[2],
        sums[3],
        grad_scale / head_scale,
        d_bias.T,
    )


def on_device(dp_size, line_size, tokens, *rest):
    head_scale, row_len = rest[10], tokens.shape[1] * line_size
    whole_heads = head_scale.shape[0] % line_size == 0 and dp_size % line_size == 0
    if dp_size == 8 and line_size == 4 and whole_heads and row_len % lanes == 0:
        return by_heads(tokens, *rest)
    return by_sequence(tokens, *rest)


def solution(mesh):
    return jax.shard_map(
        functools.partial(on_device, mesh.shape["dp"], mesh.shape["blk"]),
        mesh=mesh,
        in_specs=(
            P("dp", "blk", None),
            P("dp", None),
            P(),
            P(("dp", "blk"), None),
            P(("dp", "blk"), None),
            P(("dp", "blk"), None),
            P(("dp", "blk"), None),
            P(),
            P(),
            P(),
            P(),
            P(),
            P(),
            P("dp", "blk", None),
        ),
        out_specs=(
            P("dp", "blk", None),
            P("dp", "blk", None),
            P(("dp", "blk"), None),
            P(("dp", "blk"), None),
            P(("dp", "blk"), None),
            P(("dp", "blk"), None),
            P(),
            P(),
            P(),
            P(),
            P(),
            P(),
        ),
        check_vma=False,
    )
```

```python
import functools
import math

import jax
import jax.numpy as jnp
from jax import lax
from jax.experimental import pallas as pl
from jax.experimental.pallas import tpu as pltpu
from jax.sharding import PartitionSpec as P

epsilon = 1e-05
masked_score = -1e30
query_scale = 0.125
highest = lax.Precision.HIGHEST


def layer_norm(value, gain):
    center = value - jnp.mean(value, axis=-1, keepdims=True)
    spread = jnp.mean(center * center, axis=-1, keepdims=True)
    return center * lax.rsqrt(spread + epsilon) * gain


def hidden_norm(value, gain):
    return layer_norm(jax.nn.gelu(value, approximate=False), gain)


def column_product(left, right):
    return lax.dot_general(
        left, right, (((0,), (0,)), ((), ())), preferred_element_type=jnp.float32
    )


def times_transpose(left, matrix):
    return lax.dot_general(
        left, matrix, (((1,), (1,)), ((), ())), preferred_element_type=jnp.float32
    )


def toeplitz(diagonals, rows, cols):
    heads = diagonals.shape[0]
    padded = jnp.pad(diagonals, ((0, 0), (0, 1)))
    stride = rows + cols - 1
    tiled = jnp.tile(padded, (1, rows))[:, : rows * stride].reshape(heads, rows, stride)
    return tiled[:, :, rows - 1 : rows - 1 + cols]


def diagonal_sums(grid):
    heads, rows, cols = grid.shape
    flipped = grid[:, ::-1, :]
    padded = jnp.pad(flipped, ((0, 0), (0, 0), (0, rows)))
    skewed = padded.reshape(heads, -1)[:, : rows * (rows + cols - 1)].reshape(
        heads, rows, rows + cols - 1
    )
    return jnp.sum(skewed, axis=1)


def by_sequence(
    tokens,
    lengths,
    distance_bucket,
    w_qkv,
    w_out,
    w_fc1,
    w_fc2,
    gain_in,
    gain_attn,
    gain_ffn_in,
    gain_hidden,
    head_scale,
    bias_table,
    cotangent,
):
    rows_here = tokens.shape[1]
    width = tokens.shape[2]
    heads = head_scale.shape[0]
    head_size = width // heads
    reach = distance_bucket.shape[0] // 2
    bucket_count = bias_table.shape[0]
    row_len = rows_here * lax.axis_size("blk")
    key_block = math.gcd(row_len, 512)
    block_count = row_len // key_block
    query_anchor = lax.axis_index("blk") * rows_here
    positions = query_anchor + jnp.arange(rows_here, dtype=jnp.int32)
    ends = jnp.cumsum(lengths[0])
    bucket_ids = jnp.arange(bucket_count, dtype=jnp.int32)

    def document_of(where):
        return jnp.sum((where[:, None] >= ends[None, :]).astype(jnp.int32), axis=1)

    query_docs = document_of(positions)

    def bucket_index(query_start, rows, key_start, cols):
        steps = jnp.arange(rows + cols - 1, dtype=jnp.int32)
        relative = key_start - query_start - (rows - 1) + steps
        return jnp.take(distance_bucket, jnp.clip(relative, -reach, reach) + reach)

    def scores_for(query_heads, query_start, query_doc, key_heads, key_start, key_doc):
        rows = query_heads.shape[0]
        cols = key_heads.shape[0]
        raw = jnp.einsum("qhd,khd->hqk", query_heads, key_heads, preferred_element_type=jnp.float32)
        buckets = bucket_index(query_start, rows, key_start, cols)
        diagonals = jnp.take(bias_table, buckets, axis=0).T
        same = query_doc[:, None] == key_doc[None, :]
        full = raw + toeplitz(diagonals, rows, cols)
        return (jnp.where(same[None], full, masked_score), same, buckets)

    residual_in = tokens[0].astype(jnp.float32)
    wqkv_all, wout_all = (
        lax.all_gather(w_qkv, ("dp", "blk"), axis=0, tiled=True),
        lax.all_gather(w_out, ("dp", "blk"), axis=0, tiled=True),
    )
    normed_f, norm_in_back = jax.vjp(layer_norm, residual_in, gain_in)
    normed_in = normed_f.astype(jnp.bfloat16)
    projected = jnp.dot(normed_in, wqkv_all, preferred_element_type=jnp.float32)
    queries = (projected[:, :width] * query_scale).astype(jnp.bfloat16)
    keys_here = projected[:, width : 2 * width].astype(jnp.bfloat16)
    values_here = projected[:, 2 * width :].astype(jnp.bfloat16)
    query_heads = queries.reshape(rows_here, heads, head_size)
    best = jnp.full((heads, rows_here), masked_score, jnp.float32)
    key_piece = lax.all_gather(keys_here, "blk", axis=0, tiled=True)
    value_piece = lax.all_gather(values_here, "blk", axis=0, tiled=True)
    length = key_piece.shape[0]
    key_pos = jnp.arange(length, dtype=jnp.int32)
    scores, same, buckets = scores_for(
        query_heads,
        query_anchor,
        query_docs,
        key_piece.reshape(length, heads, head_size),
        jnp.int32(0),
        document_of(key_pos),
    )
    new_best = jnp.maximum(best, jnp.max(scores, axis=-1))
    weights = jnp.where(same[None], jnp.exp(scores - new_best[..., None]), 0.0)
    total = jnp.sum(weights, axis=-1)
    accum = jnp.einsum(
        "hqk,khd->hqd",
        weights.astype(jnp.bfloat16),
        value_piece.reshape(length, heads, head_size),
        preferred_element_type=jnp.float32,
    )
    best, total, accum = (new_best, total, accum)
    log_total = best + jnp.log(total)
    attention = jnp.transpose(accum / total[..., None], (1, 0, 2)).reshape(rows_here, width)
    scale_cols = jnp.repeat(head_scale, head_size)
    scaled = (attention * scale_cols).astype(jnp.bfloat16)
    attn_out = jnp.dot(scaled, wout_all, preferred_element_type=jnp.float32)
    normed_attn, norm_attn_back = jax.vjp(layer_norm, attn_out, gain_attn)
    middle = residual_in + normed_attn
    fc1_all, fc2_all = (
        lax.all_gather(w_fc1, ("dp", "blk"), axis=0, tiled=True),
        lax.all_gather(w_fc2, ("dp", "blk"), axis=0, tiled=True),
    )
    normed_mid_f, norm_mid_back = jax.vjp(layer_norm, middle, gain_ffn_in)
    normed_mid = normed_mid_f.astype(jnp.bfloat16)
    hidden = jnp.dot(normed_mid, fc1_all, preferred_element_type=jnp.float32)
    activated_f, hidden_back = jax.vjp(hidden_norm, hidden, gain_hidden)
    activated = activated_f.astype(jnp.bfloat16)
    mixed = (middle + jnp.dot(activated, fc2_all, preferred_element_type=jnp.float32)).astype(
        jnp.bfloat16
    )
    grad_in = cotangent[0]
    fc1_back, fc2_back = (
        lax.all_gather(w_fc1, ("dp", "blk"), axis=0, tiled=True),
        lax.all_gather(w_fc2, ("dp", "blk"), axis=0, tiled=True),
    )
    grad_fc2 = lax.psum_scatter(
        column_product(activated, grad_in), ("dp", "blk"), scatter_dimension=0, tiled=True
    )
    d_activated = times_transpose(grad_in, fc2_back)
    d_hidden_f, grad_gain_hidden = hidden_back(d_activated)
    d_hidden = d_hidden_f.astype(jnp.bfloat16)
    grad_fc1 = lax.psum_scatter(
        column_product(normed_mid, d_hidden), ("dp", "blk"), scatter_dimension=0, tiled=True
    )
    d_mid_part, grad_gain_ffn_in = norm_mid_back(times_transpose(d_hidden, fc1_back))
    d_middle = grad_in.astype(jnp.float32) + d_mid_part
    d_attn_f, grad_gain_attn = norm_attn_back(d_middle)
    d_attn_out = d_attn_f.astype(jnp.bfloat16)
    qkv_back, out_back = (
        lax.all_gather(w_qkv, ("dp", "blk"), axis=0, tiled=True),
        lax.all_gather(w_out, ("dp", "blk"), axis=0, tiled=True),
    )
    grad_out = lax.psum_scatter(
        column_product(scaled, d_attn_out), ("dp", "blk"), scatter_dimension=0, tiled=True
    )
    d_scaled = times_transpose(d_attn_out, out_back)
    grad_scale = jnp.sum((d_scaled * attention).reshape(rows_here, heads, head_size), axis=(0, 2))
    d_attention = (d_scaled * scale_cols).astype(jnp.bfloat16)
    grad_heads = d_attention.reshape(rows_here, heads, head_size)
    row_delta = jnp.sum(
        (d_attention.astype(jnp.float32) * attention).reshape(rows_here, heads, head_size), axis=2
    ).T
    keys_back, values_back = (
        lax.all_gather(keys_here, "blk", axis=0, tiled=True),
        lax.all_gather(values_here, "blk", axis=0, tiled=True),
    )

    def pair_grads(
        query_part,
        grad_part,
        total_part,
        delta_part,
        query_start,
        query_doc,
        key_part,
        value_part,
        key_start,
        key_doc,
    ):
        scores, same, buckets = scores_for(
            query_part, query_start, query_doc, key_part, key_start, key_doc
        )
        probs = jnp.where(same[None], jnp.exp(scores - total_part[..., None]), 0.0)
        d_probs = jnp.einsum(
            "qhd,khd->hqk", grad_part, value_part, preferred_element_type=jnp.float32
        )
        d_scores = probs * (d_probs - delta_part[..., None])
        return (probs.astype(jnp.bfloat16), d_scores, buckets)

    def bias_sum(d_scores, buckets):
        sums = diagonal_sums(d_scores)
        selector = (buckets[:, None] == bucket_ids[None, :]).astype(jnp.float32)
        return jnp.dot(sums, selector, precision=highest).T

    def key_slices(index):
        begin = index * key_block
        key_part = lax.dynamic_slice_in_dim(keys_back, begin, key_block, 0).reshape(
            key_block, heads, head_size
        )
        value_part = lax.dynamic_slice_in_dim(values_back, begin, key_block, 0).reshape(
            key_block, heads, head_size
        )
        return (key_part, value_part, begin)

    query_carry = (
        jnp.zeros((rows_here, heads, head_size), jnp.float32),
        jnp.zeros((bucket_count, heads), jnp.float32),
    )

    def key_step(carry, index):
        d_query, d_bias = carry
        key_part, value_part, begin = key_slices(index)
        key_doc = document_of(begin + jnp.arange(key_block, dtype=jnp.int32))
        probs_low, d_scores, buckets = pair_grads(
            query_heads,
            grad_heads,
            log_total,
            row_delta,
            query_anchor,
            query_docs,
            key_part,
            value_part,
            begin,
            key_doc,
        )
        scores_low = d_scores.astype(jnp.bfloat16)
        d_query = d_query + jnp.einsum(
            "hqk,khd->qhd", scores_low, key_part, preferred_element_type=jnp.float32
        )
        d_key = jnp.einsum(
            "hqk,qhd->khd", scores_low, query_heads, preferred_element_type=jnp.float32
        ).reshape(key_block, width)
        d_value = jnp.einsum(
            "hqk,qhd->khd", probs_low, grad_heads, preferred_element_type=jnp.float32
        ).reshape(key_block, width)
        return (
            (d_query, d_bias + bias_sum(d_scores, buckets)),
            jnp.concatenate([d_key, d_value], axis=1),
        )

    (d_query, d_bias), kv_terms = lax.scan(
        key_step, query_carry, jnp.arange(block_count, dtype=jnp.int32)
    )
    kv_grad = lax.psum_scatter(
        kv_terms.reshape(row_len, 2 * width).astype(jnp.bfloat16),
        "blk",
        scatter_dimension=0,
        tiled=True,
    )
    d_query_low = d_query.reshape(rows_here, width).astype(jnp.bfloat16)
    d_projected = jnp.concatenate(
        [d_query_low * jnp.asarray(query_scale, jnp.bfloat16), kv_grad], axis=1
    )
    grad_qkv = lax.psum_scatter(
        column_product(normed_in, d_projected), ("dp", "blk"), scatter_dimension=0, tiled=True
    )
    d_input_part, grad_gain_in = norm_in_back(times_transpose(d_projected, qkv_back))
    grad_tokens = (d_middle + d_input_part).astype(jnp.bfloat16)[None]
    small = lax.psum(
        (grad_gain_in, grad_gain_attn, grad_gain_ffn_in, grad_gain_hidden, grad_scale, d_bias),
        ("dp", "blk"),
    )
    return (
        mixed[None],
        grad_tokens,
        grad_qkv,
        grad_out,
        grad_fc1,
        grad_fc2,
        small[0],
        small[1],
        small[2],
        small[3],
        small[4],
        small[5],
    )


lanes = 128
core_bit, x_bit, y_bit = 1, 2, 4


def swap(value, bit):
    size = lax.axis_size("dp")
    return lax.ppermute(value, "dp", [(i, i ^ bit) for i in range(size)])


def turn(value, steps):
    size = lax.axis_size("blk")
    return lax.ppermute(value, "blk", [(i, (i + steps) % size) for i in range(size)])


def swap_line(value, bit):
    size = lax.axis_size("blk")
    return lax.ppermute(value, "blk", [(i, i ^ bit) for i in range(size)])


def pick(stack, index):
    return lax.dynamic_index_in_dim(stack, index, 0, keepdims=False)


def after(value, *others):
    return lax.optimization_barrier((value, *others))[0]


def all_after(values, *others):
    return list(lax.optimization_barrier((*values, *others))[: len(values)])


def turns(value):
    size = lax.axis_size("blk")
    return [value] + [turn(value, steps) for steps in range(1, size)]


def in_line(pieces):
    here, size = lax.axis_index("blk"), lax.axis_size("blk")
    ordered = [lax.select_n(lax.rem(here - owner + size, size), *pieces) for owner in range(size)]
    return jnp.concatenate(ordered, axis=0)


def deal_line(stack):
    here, size = lax.axis_index("blk"), lax.axis_size("blk")
    got = [pick(stack, here)]
    for steps in range(1, size):
        got.append(turn(pick(stack, lax.rem(here + steps, size)), steps))
    return got


def swap_cores(blocks):
    return [swap(block, core_bit) for block in blocks]


def beside(line):
    return [line, swap(line, x_bit), swap(line, y_bit)]


def across_halves(near):
    _, along_x, along_y = near
    half = along_x.shape[0] // 2
    return [swap(along_y[:half], x_bit), swap(along_x[half:], y_bit)]


def across_plane(near):
    return near + [jnp.concatenate(across_halves(near), axis=0)]


def add_low(left, right):
    return (left.astype(jnp.float32) + right.astype(jnp.float32)).astype(jnp.bfloat16)


def halves_across(across):
    half = across.shape[0] // 2
    return [swap(across[:half], x_bit), swap(across[half:], y_bit)]


def add_across(halves, to_x, to_y):
    from_x, from_y = halves
    half = from_x.shape[0]
    to_y = jnp.concatenate([add_low(to_y[:half], from_x), to_y[half:]], axis=0)
    to_x = jnp.concatenate([to_x[:half], add_low(to_x[half:], from_y)], axis=0)
    return to_x, to_y


def add_planes(to_x, to_y, own):
    got_x, got_y = swap(to_x, x_bit), swap(to_y, y_bit)
    total = own.astype(jnp.float32) + got_x.astype(jnp.float32) + got_y.astype(jnp.float32)
    return total.astype(jnp.bfloat16)


def sum_parts(parts):
    total = parts[0].astype(jnp.float32)
    for part in parts[1:]:
        total = total + part.astype(jnp.float32)
    return total


def add_line(line):
    size = lax.axis_size("blk")
    return sum_parts(deal_line(line.reshape((size, -1) + line.shape[1:])))


def contract(left, right, left_axis, right_axis):
    return lax.dot_general(
        left, right, (((left_axis,), (right_axis,)), ((), ())), preferred_element_type=jnp.float32
    )


tile_cols = 256
far_first = (x_bit | y_bit, x_bit, y_bit, 0)


def run_kernel(kernel, name, micros, place_here, operands, far, outputs, far_outputs, scratch=(), copies=1):
    near_spec, far_spec = pl.BlockSpec(memory_space=pltpu.VMEM), pl.BlockSpec(memory_space=pl.ANY)
    return pl.pallas_call(
        kernel,
        out_shape=[jax.ShapeDtypeStruct(shape, dtype) for shape, dtype in (*outputs, *far_outputs)],
        in_specs=[pl.BlockSpec(memory_space=pltpu.SMEM)] + [near_spec] * len(operands) + [far_spec] * len(far),
        out_specs=[near_spec] * len(outputs) + [far_spec] * len(far_outputs),
        scratch_shapes=[pltpu.VMEM(shape, dtype) for shape, dtype in scratch]
        + [pltpu.SemaphoreType.DMA((copies,))],
        compiler_params=pltpu.CompilerParams(vmem_limit_bytes=52 * 2**20),
        cost_estimate=pl.CostEstimate(
            flops=int(micros * 1.1e9), bytes_accessed=int(micros * 3.6e6), transcendentals=0
        ),
        name=name,
    )(place_here, *operands, *far)


class Copies:
    def __init__(self, semaphores):
        self.semaphores, self.used = semaphores, 0

    def start(self, source, target):
        copy = pltpu.make_async_copy(source, target, self.semaphores.at[self.used])
        self.used += 1
        copy.start()
        return copy


def wait_all(copies):
    for copy in copies:
        copy.wait()


def normalize(value):
    center = value - jnp.mean(value, axis=-1, keepdims=True)
    spread = jnp.mean(center * center, axis=-1, keepdims=True)
    scale = lax.rsqrt(spread + epsilon)
    return center * scale, scale


def normalize_back(normed, scale, grad, gain):
    inner = grad * gain
    middle = jnp.mean(inner, axis=-1, keepdims=True)
    along = jnp.mean(inner * normed, axis=-1, keepdims=True)
    return scale * (inner - middle - normed * along), jnp.sum(grad * normed, axis=0, keepdims=True)


def block_indices(place_ref):
    me = place_ref[0]
    return [me ^ bits ^ core_bit for bits in far_first], [me ^ bits for bits in far_first]


near_first = (0, x_bit, y_bit, x_bit | y_bit)


def fill_planes(copies, place_ref, blocks, cols, out_ref):
    bits = near_first + tuple(bit | core_bit for bit in near_first)
    started = []
    for bit, block in zip(bits, blocks):
        rows = block.shape[0]
        begin = pl.multiple_of((place_ref[0] ^ bit) * rows, rows)
        started.append(copies.start(block.at[:, cols], out_ref.at[pl.ds(begin, rows), :]))
    return started


def before(place_ref, steps, size):
    return lax.rem(place_ref[1] - steps + size, size)


def bias_kernel(heads, place_ref, diagonal_ref, bias_ref, semaphores):
    for head in range(heads):
        for step in range(diagonal_ref.shape[1] // lanes - 1):
            window = diagonal_ref[head : head + 1, step * lanes : (step + 2) * lanes]
            window = jnp.broadcast_to(window, (lanes, 2 * lanes))
            window = pltpu.roll(window, 0, 1, stride=1, stride_axis=0)
            bias_ref[head, :, step * lanes : (step + 1) * lanes] = window[:, lanes:]


def attend_kernel(
    heads, head_size, place_ref, gain_ref, doc_col_ref, doc_row_ref, scale_ref, tokens_ref, *refs
):
    parts, refs = refs[:8], refs[8:]
    bias_in, w_ref, qkv_ref, normed_ref, attention_ref, scaled_ref, probs_out, bias, probs_ref, semaphores = refs
    copies = Copies(semaphores)
    last = parts[0].shape[1]
    arriving = fill_planes(copies, place_ref, parts, slice(last - w_ref.shape[1], last), w_ref)
    bias_here = copies.start(bias_in, bias)
    leaving = []
    length = tokens_ref.shape[0]
    blocks = length // lanes
    width = heads * head_size
    for block in range(blocks):
        rows = slice(block * lanes, (block + 1) * lanes)
        normed, _ = normalize(tokens_ref[rows, :].astype(jnp.float32))
        normed_ref[rows, :] = (normed * gain_ref[...]).astype(jnp.bfloat16)
    wait_all(arriving)
    bias_here.wait()
    projected = contract(normed_ref[...], w_ref[...], 1, 0)
    qkv_ref[:, :width] = (projected[:, :width] * query_scale).astype(jnp.bfloat16)
    qkv_ref[:, width:] = projected[:, width:].astype(jnp.bfloat16)
    for head in range(heads):
        low = head * head_size
        keys = qkv_ref[:, width + low : width + low + head_size]
        values = qkv_ref[:, 2 * width + low : 2 * width + low + head_size]
        all_scores = contract(qkv_ref[:, low : low + head_size], keys, 1, 1)
        for block in range(blocks):
            rows = slice(block * lanes, (block + 1) * lanes)
            first = (blocks - 1 - block) * lanes
            scores = all_scores[rows, :] + bias[head, :, first : first + length]
            same = doc_col_ref[rows, :] == doc_row_ref[...]
            scores = jnp.where(same, scores, masked_score)
            weights = jnp.exp(scores - jnp.max(scores, axis=1, keepdims=True))
            probs = weights * (1.0 / jnp.sum(weights, axis=1, keepdims=True))
            probs = probs.astype(jnp.bfloat16)
            probs_ref[head, rows, :] = probs
        leaving.append(copies.start(probs_ref.at[head], probs_out.at[head]))
        attention_ref[:, low : low + head_size] = contract(probs_ref[head], values, 1, 0)
    scaled_ref[...] = (attention_ref[...] * scale_ref[...]).astype(jnp.bfloat16)
    wait_all(leaving)


def forward_kernel(line, place_ref, *refs):
    pieces, refs = refs[:line], refs[line:]
    tokens_ref, gain_attn_ref, gain_mid_ref, gain_hidden_ref, cotangent_ref, *refs = refs
    blocks, refs = refs[:8], refs[8:]
    (attn_ref, middle_ref, normed_ref, mean_ref, scale_ref, activated_ref,
     hidden_out, across_out, send_out, keep_out,
     wout_ref, fc1_ref, hidden_ref, below_ref, grads_ref, semaphores) = refs
    copies = Copies(semaphores)
    part = pieces[0].shape[1]
    hidden_width, width = fc1_ref.shape[1], wout_ref.shape[1]
    wout_here = fill_planes(copies, place_ref, blocks, slice(hidden_width, hidden_width + width), wout_ref)
    fc1_here = fill_planes(copies, place_ref, blocks, slice(0, hidden_width), fc1_ref)
    leaving = []
    wait_all(wout_here)
    attn = jnp.zeros(attn_ref.shape, jnp.float32)
    for steps in range(line):
        rows = pl.ds(pl.multiple_of(before(place_ref, steps, line) * part, part), part)
        attn = attn + contract(pieces[steps][...], wout_ref[rows, :], 1, 0)
    attn_ref[...] = attn
    normed, _ = normalize(attn)
    middle = tokens_ref[...].astype(jnp.float32) + normed * gain_attn_ref[...]
    middle_ref[...] = middle
    normed, _ = normalize(middle)
    normed = (normed * gain_mid_ref[...]).astype(jnp.bfloat16)
    normed_ref[...] = normed
    tiles = [slice(begin, begin + tile_cols) for begin in range(0, hidden_width, tile_cols)]
    total = jnp.zeros(mean_ref.shape, jnp.float32)
    wait_all(fc1_here)
    for cols in tiles:
        hidden = contract(normed, fc1_ref[:, cols], 1, 0)
        below = 0.5 * (1.0 + lax.erf(hidden * (0.5**0.5)))
        hidden_ref[:, cols] = hidden
        below_ref[:, cols] = below
        leaving.append(copies.start(hidden_ref.at[:, cols], hidden_out.at[:, cols]))
        total = total + jnp.sum(hidden * below, axis=1, keepdims=True)
    mean = total / hidden_width
    total = jnp.zeros(mean_ref.shape, jnp.float32)
    for cols in tiles:
        center = hidden_ref[:, cols] * below_ref[:, cols] - mean
        total = total + jnp.sum(center * center, axis=1, keepdims=True)
    scale = lax.rsqrt(total / hidden_width + epsilon)
    mean_ref[...] = mean
    scale_ref[...] = scale
    for cols in tiles:
        center = hidden_ref[:, cols] * below_ref[:, cols] - mean
        activated_ref[:, cols] = (center * scale * gain_hidden_ref[:, cols]).astype(jnp.bfloat16)
    size = grads_ref.shape[1]
    sent, kept = block_indices(place_ref)
    outs = [across_out] + [send_out.at[slot] for slot in range(3)] + [keep_out.at[slot] for slot in range(4)]
    for slot, (index, out) in enumerate(zip(sent + kept, outs)):
        cols = pl.ds(pl.multiple_of(index * size, lanes), size)
        grads_ref[slot] = contract(activated_ref[:, cols], cotangent_ref[...], 0, 0).astype(jnp.bfloat16)
        leaving.append(copies.start(grads_ref.at[slot], out))
    wait_all(leaving)


def backward_kernel(line, place_ref, *refs):
    pieces, refs = refs[:line], refs[line:]
    (cotangent_ref, attn_ref, middle_ref, normed_ref, mean_ref, scale_ref, gain_attn_ref, gain_mid_ref,
     gain_hidden_ref, head_scale_ref, *refs) = refs
    first_blocks, second_blocks, refs = refs[:8], refs[8:16], refs[16:]
    hidden_in, activated_in, *refs = refs
    mixed_ref, d_middle_ref, d_hidden_gain_ref, d_mid_gain_ref, d_attn_gain_ref, *refs = refs
    grads, refs = refs[:line], refs[line:]
    (send_out, keep_out, wout_ref, fc1_ref, fc2_ref, hidden_ref, below_ref, activated_ref, inner_ref, fc1_grad,
     out_grad, semaphores) = refs
    copies = Copies(semaphores)
    part = pieces[0].shape[1]
    hidden_width, width = fc1_ref.shape[1], wout_ref.shape[1]
    fc2_here, hidden_here = [], []
    for bit, block in zip(near_first + tuple(bit | core_bit for bit in near_first), second_blocks):
        size = block.shape[0]
        part_here = pl.ds(pl.multiple_of((place_ref[0] ^ bit) * size, lanes), size)
        fc2_here.append(copies.start(block, fc2_ref.at[part_here, :]))
        hidden_here.append(copies.start(hidden_in.at[:, part_here], hidden_ref.at[:, part_here]))
    fc1_here = fill_planes(copies, place_ref, first_blocks, slice(0, hidden_width), fc1_ref)
    activated_here = copies.start(activated_in, activated_ref)
    wout_here = fill_planes(
        copies, place_ref, first_blocks, slice(hidden_width, hidden_width + width), wout_ref
    )
    grad_in = cotangent_ref[...]
    mean, scale = mean_ref[...], scale_ref[...]
    tiles = [slice(begin, begin + tile_cols) for begin in range(0, hidden_width, tile_cols)]
    size = hidden_width // len(fc2_here)
    bits = near_first + tuple(bit | core_bit for bit in near_first)
    total = jnp.zeros(mean.shape, jnp.float32)
    along = jnp.zeros(mean.shape, jnp.float32)
    for bit, arriving in zip(bits, zip(fc2_here, hidden_here)):
        wait_all(arriving)
        cols = pl.ds(pl.multiple_of((place_ref[0] ^ bit) * size, lanes), size)
        d_activated = contract(grad_in, fc2_ref[cols, :], 1, 1)
        hidden = hidden_ref[:, cols]
        below = 0.5 * (1.0 + lax.erf(hidden * (0.5**0.5)))
        below_ref[:, cols] = below
        normed = (hidden * below - mean) * scale
        d_hidden_gain_ref[:, cols] = jnp.sum(d_activated * normed, axis=0, keepdims=True)
        inner = d_activated * gain_hidden_ref[:, cols]
        inner_ref[:, cols] = inner
        total = total + jnp.sum(inner, axis=1, keepdims=True)
        along = along + jnp.sum(inner * normed, axis=1, keepdims=True)
    total, along = total / hidden_width, along / hidden_width
    d_normed = jnp.zeros(middle_ref.shape, jnp.float32)
    normed_mid = normed_ref[...].T
    wait_all(fc1_here)
    for cols in tiles:
        hidden, below = hidden_ref[:, cols], below_ref[:, cols]
        normed = (hidden * below - mean) * scale
        slope = below + hidden * jnp.exp(-0.5 * hidden * hidden) * (1.0 / math.sqrt(2.0 * math.pi))
        d_hidden = scale * (inner_ref[:, cols] - total - normed * along) * slope
        d_hidden = d_hidden.astype(jnp.bfloat16)
        fc1_grad[:, cols] = contract(normed_mid, d_hidden, 1, 0).astype(jnp.bfloat16)
        d_normed = d_normed + contract(d_hidden, fc1_ref[:, cols], 1, 1)
    size = send_out.shape[1]
    sent, kept = block_indices(place_ref)
    outs = [send_out.at[slot] for slot in range(4)] + [keep_out.at[slot] for slot in range(4)]
    places = [pl.ds(pl.multiple_of(index * size, size), size) for index in sent + kept]
    leaving = [
        copies.start(fc1_grad.at[rows, :], out.at[:, :hidden_width]) for rows, out in zip(places, outs)
    ]
    normed, scale = normalize(middle_ref[...])
    d_value, d_mid_gain_ref[...] = normalize_back(normed, scale, d_normed, gain_mid_ref[...])
    d_middle = grad_in.astype(jnp.float32) + d_value
    d_middle_ref[...] = d_middle
    normed, scale = normalize(attn_ref[...])
    d_value, d_attn_gain_ref[...] = normalize_back(normed, scale, d_middle, gain_attn_ref[...])
    d_attn = d_value.astype(jnp.bfloat16)
    wait_all(wout_here)
    for steps in range(line):
        owner = before(place_ref, steps, line)
        rows = pl.ds(pl.multiple_of(owner * part, part), part)
        d_scaled = contract(d_attn, wout_ref[rows, :], 1, 1)
        grads[steps][...] = (d_scaled * head_scale_ref[pl.ds(owner, 1), :]).astype(jnp.bfloat16)
        out_grad[rows, :] = contract(pieces[steps][...], d_attn, 0, 0).astype(jnp.bfloat16)
    leaving += [
        copies.start(out_grad.at[rows, :], out.at[:, hidden_width:]) for rows, out in zip(places, outs)
    ]
    activated_here.wait()
    mixed = middle_ref[...] + contract(activated_ref[...], fc2_ref[...], 1, 0)
    mixed_ref[...] = mixed.astype(jnp.bfloat16)
    wait_all(leaving)


def attend_back_kernel(heads, head_size, line, place_ref, *refs):
    pieces, refs = refs[:line], refs[line:]
    (qkv_ref, attention_ref, probs_in, normed_in, w_in,
     send_ref, keep_ref, diagonal_ref, delta_ref, gain_ref, d_normed_out,
     grad_ref, out_ref, w_grad, sums, probs_ref, normed_ref, w_ref, d_normed_ref, scores_ref, semaphores) = refs
    copies = Copies(semaphores)
    probs_here = [copies.start(probs_in.at[head], probs_ref.at[head]) for head in range(heads)]
    rest_here = [copies.start(w_in, w_ref), copies.start(normed_in, normed_ref)]
    length = qkv_ref.shape[0]
    blocks = length // lanes
    width = heads * head_size
    rows_here = pieces[0].shape[0]
    for steps in range(line):
        owner = lax.rem(place_ref[1] + steps, line)
        grad_ref[pl.ds(pl.multiple_of(owner * rows_here, rows_here), rows_here), :] = pieces[steps][...]
    diagonal_ref[...] = jnp.zeros_like(diagonal_ref)
    for head in range(heads):
        sums[...] = jnp.zeros_like(sums)
        probs_here[head].wait()
        low = head * head_size
        keys = qkv_ref[:, width + low : width + low + head_size]
        values = qkv_ref[:, 2 * width + low : 2 * width + low + head_size]
        queries = qkv_ref[:, low : low + head_size]
        grad = grad_ref[:, low : low + head_size]
        product = grad.astype(jnp.float32) * attention_ref[:, low : low + head_size]
        delta = jnp.sum(product, axis=1, keepdims=True)
        delta_ref[:, head : head + 1] = delta
        d_probs = contract(grad, values, 1, 1)
        for block in range(blocks):
            rows = slice(block * lanes, (block + 1) * lanes)
            first = (blocks - 1 - block) * lanes
            d_scores = probs_ref[head, rows, :].astype(jnp.float32) * (d_probs[rows, :] - delta[rows, :])
            sums[:, first : first + length] += d_scores
            scores_ref[rows, :] = d_scores.astype(jnp.bfloat16)
        d_scores = scores_ref[...]
        d_query = contract(d_scores, keys, 1, 0).astype(jnp.bfloat16)
        out_ref[:, low : low + head_size] = d_query * jnp.asarray(query_scale, jnp.bfloat16)
        d_keys = contract(queries, d_scores, 0, 0)
        d_values = contract(grad, probs_ref[head], 0, 0)
        out_ref[:, width + low : width + low + head_size] = d_keys.T.astype(jnp.bfloat16)
        out_ref[:, 2 * width + low : 2 * width + low + head_size] = d_values.T.astype(jnp.bfloat16)
        row_ids = lax.broadcasted_iota(jnp.int32, (lanes, lanes), 0)
        col_ids = lax.broadcasted_iota(jnp.int32, (lanes, lanes), 1)
        reverse = (row_ids + col_ids == lanes - 1).astype(jnp.bfloat16)
        high = sums[...].astype(jnp.bfloat16)
        rest = (sums[...] - high.astype(jnp.float32)).astype(jnp.bfloat16)
        flipped = contract(reverse, high, 1, 0) + contract(reverse, rest, 1, 0)
        for step in range(2 * blocks - 1):
            window = flipped[:, step * lanes : (step + 1) * lanes]
            window = jnp.concatenate([window, jnp.zeros_like(window)], axis=1)
            window = pltpu.roll(window, 1, 1, stride=1, stride_axis=0)
            diagonal_ref[head : head + 1, step * lanes : (step + 2) * lanes] += jnp.sum(
                window, axis=0, keepdims=True
            )
    wait_all(rest_here)
    d_normed_ref[...] = contract(out_ref[...], w_ref[...], 1, 1).astype(jnp.bfloat16)
    leaving = copies.start(d_normed_ref, d_normed_out)
    for block in range(normed_ref.shape[1] // lanes):
        cols = slice(block * lanes, (block + 1) * lanes)
        grad = contract(normed_ref[:, cols], out_ref[...], 0, 0)
        gain_ref[cols, :] = jnp.sum(grad * w_ref[cols, :].astype(jnp.float32), axis=1, keepdims=True)
        w_grad[cols, :] = grad.astype(jnp.bfloat16)
    size = send_ref.shape[1]
    for indices, to_ref in zip(block_indices(place_ref), (send_ref, keep_ref)):
        for slot, index in enumerate(indices):
            to_ref[slot] = w_grad[pl.ds(pl.multiple_of(index * size, size), size), :]
    leaving.wait()


def by_heads(
    tokens,
    lengths,
    distance_bucket,
    w_qkv,
    w_out,
    w_fc1,
    w_fc2,
    gain_in,
    gain_attn,
    gain_ffn_in,
    gain_hidden,
    head_scale,
    bias_table,
    cotangent,
):
    here, line_size = lax.axis_index("blk"), lax.axis_size("blk")
    rows_here, width = tokens.shape[1], tokens.shape[2]
    row_len = rows_here * line_size
    all_heads = head_scale.shape[0]
    head_size = width // all_heads
    heads = all_heads // line_size
    part = heads * head_size
    reach = distance_bucket.shape[0] // 2
    bucket_count = bias_table.shape[0]
    shard_rows = w_qkv.shape[0]

    low, wide = jnp.bfloat16, jnp.float32
    planes = lax.axis_size("dp")
    place_here = jnp.stack([lax.axis_index("dp"), here]).astype(jnp.int32)
    ends = jnp.cumsum(lengths[0])
    positions = jnp.arange(row_len, dtype=jnp.int32)
    documents = jnp.sum((positions[:, None] >= ends[None, :]).astype(jnp.int32), axis=1)
    if row_len <= reach:
        buckets = distance_bucket[reach - row_len : reach + row_len]
    else:
        buckets = jnp.pad(distance_bucket, row_len - reach, mode="edge")[: 2 * row_len]
    selector = (buckets[None, :] == jnp.arange(bucket_count, dtype=jnp.int32)[:, None]).astype(jnp.float32)
    head_table = lax.dynamic_slice_in_dim(bias_table.T, here * heads, heads, 0)
    diagonals = jnp.dot(head_table, selector, precision=highest)
    scale_cols = jnp.repeat(head_scale, head_size)
    head_cols = lax.dynamic_slice_in_dim(scale_cols, here * part, part, 0)[None, :]

    (bias,) = run_kernel(
        functools.partial(bias_kernel, heads),
        "relative_bias",
        2,
        place_here,
        (diagonals,),
        (),
        [((heads, lanes, 2 * row_len - lanes), wide)],
        (),
    )

    hidden_width = w_fc1.shape[1]
    summed = hidden_width + width
    by_head = w_qkv.reshape(shard_rows, 3, line_size, part).transpose(2, 0, 1, 3)
    by_head = by_head.reshape(line_size, shard_rows, 3 * part)
    shared = jnp.broadcast_to(
        jnp.concatenate([w_fc1, w_out], axis=1)[None], (line_size, shard_rows, summed)
    )
    first_pieces = deal_line(jnp.concatenate([shared, by_head], axis=2))
    first_line = after(in_line(first_pieces), bias)
    row_tokens = lax.all_gather(after(tokens[0], first_line), "blk", axis=0, tiled=True)
    second_pieces = turns(after(w_fc2, first_line))
    first_planes = across_plane(all_after(beside(first_line), *second_pieces[1:]))
    first_others = swap_cores(first_planes[:3] + [after(first_planes[3], row_tokens)])
    second_near = beside(after(in_line(second_pieces), *first_planes))

    wqkv_part, qkv, normed_row, attention, scaled_part, probs = run_kernel(
        functools.partial(attend_kernel, heads, head_size),
        "attend",
        13,
        place_here,
        (gain_in[None], documents[:, None], documents[None, :], head_cols, row_tokens),
        (*first_planes, *first_others, bias),
        [
            ((width, 3 * part), low),
            ((row_len, 3 * part), low),
            ((row_len, width), low),
            ((row_len, part), wide),
            ((row_len, part), low),
        ],
        [((heads, row_len, row_len), low)],
        [((heads, lanes, 2 * row_len - lanes), wide), ((heads, row_len, row_len), low)],
        9 + heads,
    )

    dealt = deal_line(scaled_part.reshape(line_size, rows_here, part))
    second_halves = across_halves(all_after(second_near, scaled_part))
    dealt[0] = after(dealt[0], *second_halves)
    second_planes = second_near + [jnp.concatenate(second_halves, axis=0)]
    second_others = swap_cores(all_after(second_planes, *dealt[1:]))
    grad_in = cotangent[0]
    gains = (gain_attn[None], gain_ffn_in[None], gain_hidden[None])
    block_rows, hidden_rows = width // planes, hidden_width // planes
    *kept, activated, hidden, across_fc2, send_fc2, keep_fc2 = run_kernel(
        functools.partial(forward_kernel, line_size),
        "feed_forward",
        9,
        place_here,
        (*dealt, tokens[0], *gains, grad_in),
        (*first_planes, *first_others),
        [
            ((rows_here, width), wide),
            ((rows_here, width), wide),
            ((rows_here, width), low),
            ((rows_here, 1), wide),
            ((rows_here, 1), wide),
            ((rows_here, hidden_width), low),
        ],
        [
            ((rows_here, hidden_width), wide),
            ((hidden_rows, width), low),
            ((3, hidden_rows, width), low),
            ((4, hidden_rows, width), low),
        ],
        [
            ((width, width), low),
            ((width, hidden_width), low),
            ((rows_here, hidden_width), wide),
            ((rows_here, hidden_width), wide),
            ((8, hidden_rows, width), low),
        ],
        24 + hidden_width // tile_cols,
    )
    across_fc2, send_fc2 = all_after([across_fc2, send_fc2], *second_others)
    second_across = add_low(keep_fc2[0], swap(across_fc2, core_bit))
    halves = halves_across(second_across)
    second_rest = add_low(keep_fc2[1:], swap(send_fc2, core_bit))
    (
        mixed,
        d_middle,
        grad_gain_hidden,
        grad_gain_ffn_in,
        grad_gain_attn,
        *grad_pieces,
        send_first,
        keep_first,
    ) = run_kernel(
        functools.partial(backward_kernel, line_size),
        "feed_forward_back",
        13,
        place_here,
        (
            *dealt,
            after(grad_in, second_across),
            *kept,
            *gains,
            scale_cols.reshape(line_size, part),
        ),
        (*first_planes, *first_others, *second_planes, *second_others, hidden, activated),
        [
            ((rows_here, width), low),
            ((rows_here, width), wide),
            ((1, hidden_width), wide),
            ((1, width), wide),
            ((1, width), wide),
            *[((rows_here, part), low)] * line_size,
        ],
        [((4, block_rows, summed), low), ((4, block_rows, summed), low)],
        [
            ((width, width), low),
            ((width, hidden_width), low),
            ((hidden_width, width), low),
            ((rows_here, hidden_width), wide),
            ((rows_here, hidden_width), wide),
            ((rows_here, hidden_width), low),
            ((rows_here, hidden_width), wide),
            ((width, hidden_width), low),
            ((width, width), low),
        ],
        1 + 32 + 16,
    )

    grad_pieces = all_after(grad_pieces, *halves)
    grad_pieces = grad_pieces[:1] + [
        turn(piece, line_size - steps) for steps, piece in enumerate(grad_pieces[1:], 1)
    ]
    got_first = swap(after(send_first, *halves), core_bit)
    first_across = add_low(keep_first[0], got_first[0])
    grad_pieces[0] = after(grad_pieces[0], got_first, first_across)
    second_x, second_y = add_across(halves, second_rest[0], second_rest[1])
    second_got = [swap(second_x, x_bit), swap(second_y, y_bit)]
    send_qkv, keep_qkv, diagonal_sums_here, deltas, gain_sums, d_normed = run_kernel(
        functools.partial(attend_back_kernel, heads, head_size, line_size),
        "attend_back",
        12,
        place_here,
        (*grad_pieces, qkv, attention),
        (probs, normed_row, wqkv_part),
        [
            ((4, block_rows, 3 * part), low),
            ((4, block_rows, 3 * part), low),
            ((heads, 2 * row_len), wide),
            ((row_len, heads), wide),
            ((width, 1), wide),
        ],
        [((row_len, width), low)],
        [
            ((row_len, part), low),
            ((row_len, 3 * part), low),
            ((width, 3 * part), low),
            ((lanes, 2 * row_len - lanes), wide),
            ((heads, row_len, row_len), low),
            ((row_len, width), low),
            ((width, 3 * part), low),
            ((row_len, width), low),
            ((row_len, row_len), low),
        ],
        heads + 3,
    )
    d_normed_low = lax.psum_scatter(d_normed, "blk", scatter_dimension=0, tiled=True)
    d_normed_here = d_normed_low.astype(jnp.float32)

    second_got = all_after(second_got, d_normed)
    grad_gain_in = gain_sums[:, 0] / gain_in
    d_table = lax.dot_general(
        diagonal_sums_here, selector, (((1,), (1,)), ((), ())), precision=highest
    )
    small = (gain_sums[:, 0], grad_gain_attn[0], grad_gain_ffn_in[0], grad_gain_hidden[0])
    own_small = (jnp.sum(deltas, axis=0), d_table)
    sizes = [math.prod(value.shape) for value in small]
    flat = jnp.concatenate([value.reshape(-1) for value in small + own_small])
    tail_cols, pack_cols = 3 * part, summed + 3 * part
    flat = jnp.pad(flat, (0, -flat.shape[0] % tail_cols)).reshape(-1, tail_cols)
    terms = flat.astype(low)
    got = swap(send_qkv, core_bit)
    halves = halves_across(after(first_across, *second_got))
    second_line = sum_parts([second_rest[2], *all_after(second_got, got)]).astype(low)
    first_rest = add_low(keep_first[1:], after(got_first[1:], got))
    last = add_low(keep_qkv, got)
    terms = add_low(terms, swap(terms, core_bit))
    last_got = [
        swap(jnp.concatenate([last[slot], terms], axis=0), bits) for slot, bits in enumerate(far_first[:3])
    ]
    arrived = all_after([*halves, *last_got])
    halves, last_got = arrived[:2], arrived[2:]
    first_x, first_y = add_across(halves, first_rest[0], first_rest[1])
    first_got = [swap(first_x, x_bit), swap(first_y, y_bit)]
    last_line = sum_parts([last[3]] + [piece[:block_rows] for piece in last_got]).astype(low)
    plane_sums = [piece[block_rows:].astype(wide) for piece in last_got]
    flat = (terms.astype(wide) + plane_sums[1]) + (plane_sums[2] + plane_sums[0])
    flat = flat.reshape(-1)
    flat = jnp.pad(flat, (0, -flat.shape[0] % (2 * width))).reshape(-1, width).astype(low)

    second_rows = hidden_rows // line_size
    spread = jnp.broadcast_to(flat[None], (line_size,) + flat.shape)
    second_stack = jnp.concatenate([second_line.reshape(line_size, second_rows, width), spread], axis=1)
    second_dealt = deal_line(after(second_stack, *last_got))
    first_line = sum_parts([first_rest[2], *all_after(first_got, d_normed_low, *second_dealt[1:])]).astype(low)
    both_lines = after(jnp.concatenate([first_line, last_line], axis=1), *second_dealt[1:])
    dealt_back = deal_line(both_lines.reshape(line_size, shard_rows, pack_cols))
    grad_fc2 = sum_parts([piece[:second_rows] for piece in second_dealt])
    flats = [
        piece[second_rows:].astype(wide).reshape(-1) for piece in all_after(second_dealt, dealt_back[1])
    ]
    common = sum(sizes)
    totals = [flat[:common] for flat in flats]
    while len(totals) > 1:
        half = len(totals) // 2
        totals = [totals[step] + totals[step + half] for step in range(half)]
    owned = common + heads + heads * bucket_count
    by_owner = in_line([flat[None, common:owned] for flat in flats])
    grad_scale = by_owner[:, :heads].reshape(-1)
    d_bias = by_owner[:, heads:].reshape(all_heads, bucket_count)

    grad_fc1 = sum_parts([piece[:, :hidden_width] for piece in dealt_back])
    grad_out = sum_parts([piece[:, hidden_width:summed] for piece in dealt_back])
    grad_qkv = in_line([piece[:, summed:].astype(jnp.float32) for piece in dealt_back])
    grad_qkv = grad_qkv.reshape(line_size, shard_rows, 3, part).transpose(1, 2, 0, 3)
    grad_qkv = grad_qkv.reshape(shard_rows, 3 * width)

    _, norm_in_back = jax.vjp(lambda value: layer_norm(value, gain_in), tokens[0].astype(jnp.float32))
    (d_input_part,) = norm_in_back(d_normed_here)
    grad_tokens = (d_middle + d_input_part).astype(jnp.bfloat16)[None]

    sums, begin = [], 0
    for size in sizes:
        sums.append(totals[0][begin : begin + size])
        begin += size
    return (
        mixed[None],
        grad_tokens,
        grad_qkv,
        grad_out,
        grad_fc1,
        grad_fc2,
        sums[0] / gain_in,
        sums[1],
        sums[2],
        sums[3],
        grad_scale / head_scale,
        d_bias.T,
    )


def on_device(dp_size, line_size, tokens, *rest):
    head_scale, row_len = rest[10], tokens.shape[1] * line_size
    whole_heads = head_scale.shape[0] % line_size == 0 and dp_size % line_size == 0
    if dp_size == 8 and line_size == 4 and whole_heads and row_len % lanes == 0:
        return by_heads(tokens, *rest)
    return by_sequence(tokens, *rest)


def solution(mesh):
    return jax.shard_map(
        functools.partial(on_device, mesh.shape["dp"], mesh.shape["blk"]),
        mesh=mesh,
        in_specs=(
            P("dp", "blk", None),
            P("dp", None),
            P(),
            P(("dp", "blk"), None),
            P(("dp", "blk"), None),
            P(("dp", "blk"), None),
            P(("dp", "blk"), None),
            P(),
            P(),
            P(),
            P(),
            P(),
            P(),
            P("dp", "blk", None),
        ),
        out_specs=(
            P("dp", "blk", None),
            P("dp", "blk", None),
            P(("dp", "blk"), None),
            P(("dp", "blk"), None),
            P(("dp", "blk"), None),
            P(("dp", "blk"), None),
            P(),
            P(),
            P(),
            P(),
            P(),
            P(),
        ),
        check_vma=False,
    )
```
